32 devices in a mesh: groups: 2 (over x), ctx: 16 (over z, y, core).
Axes of the slice: x: 2, y: 2, z: 4, core: 2. Of those that a mesh axis runs over, the one named last changes fastest.
Arguments:
- queries: bfloat16 [4096, 4096], P(('groups', 'ctx')), parts along dimension 0, may hold values from -400 to 400
- span_keys: bfloat16 [4096, 512], P(('groups', 'ctx')), parts along dimension 0, may hold values from -25 to 25
- span_values: bfloat16 [4096, 512], P(('groups', 'ctx')), parts along dimension 0, may hold values from -96 to 96
- cache_keys: bfloat16 [65536, 512], P(('groups', 'ctx')), parts along dimension 0, may hold values from -24 to 24
- cache_values: bfloat16 [65536, 512], P(('groups', 'ctx')), parts along dimension 0, may hold values from -96 to 96
- vertical_blocks: int32 [8, 16], P('groups'), parts along dimension 0, may hold values from 0 to 511, as said below
- slash_offsets: int32 [8, 64], P('groups'), parts along dimension 0, may hold values from 0 to 127, as said below
Outputs:
- attended: bfloat16 [4096, 4096], P(('groups', 'ctx')), parts along dimension 0
The draws below stay inside these ranges and needn't reach their ends.
There are 2 independent parts, one for each index of `groups`. The reference program is written for one: setup_inputs(seed, part) draws one part's arguments, and reference() takes and returns one part's arrays. A program takes and returns all parts, laid end to end along the dimension named above; each array names one. Nothing has to cross between parts.
Inputs may be any that keep to these rules, and one draw needn't show every extreme that they name: `vertical_blocks`: each row holds 16 different block numbers of the cache; the first key-value head always reads the cache's last block. `slash_offsets`: each row holds 64 different offsets, always among them 0, 1 and 127.
All inputs are finite; a program needn't handle non-finite values.
Results may differ from the reference program's by a relative error of at most 0.005.
Values may be sent and summed in bfloat16 or wider, within the bound.
No kernel may reach another device: no remote copies, remote signals or barrier semaphores. Data moves between devices by JAX's collectives and lax.ppermute only.
A program may use at most 64 MiB of HBM per device.

```python
import math
import jax
import jax.numpy as jnp
from jax import lax

KVH = 4
GROUP = 8
HD = 128
QH = 32
QDEV = 128
VBLOCK = 64
NV = 16
NS = 64
SMAX = 128
NQ = 2048
NCTX = 32768


def paired_keys(key):
    raw = jnp.clip(jax.random.normal(jax.random.fold_in(key, 101), (NQ, KVH * HD), jnp.float32), -6.0, 6.0)
    made = raw
    return made


def draw_span_keys(key, part):
    made = paired_keys(key)
    return made.astype(jnp.bfloat16)


def draw_queries(key, part):
    own = jax.random.fold_in(key, 5)
    raw = jnp.clip(jax.random.normal(own, (NQ, QH * HD), jnp.float32), -6.0, 6.0)
    return raw.astype(jnp.bfloat16)


def draw_cache_keys(key, part):
    own = jax.random.fold_in(key, 7)
    raw = jnp.clip(jax.random.normal(own, (NCTX, KVH * HD), jnp.float32), -6.0, 6.0)
    return raw.astype(jnp.bfloat16)


def draw_vertical_blocks(key, part):
    own = jax.random.fold_in(key, 9)
    blocks_all = NCTX // VBLOCK
    first_rest = jax.random.permutation(jax.random.fold_in(own, 99), blocks_all - 1)[:NV - 1]
    first_row = jnp.concatenate([jnp.full((1,), blocks_all - 1, jnp.int32), first_rest.astype(jnp.int32)])
    first_row = first_row[jax.random.permutation(jax.random.fold_in(own, 98), NV)]
    rows_list = [first_row]
    for kv_head in range(1, KVH):
        rows_list.append(jax.random.permutation(jax.random.fold_in(own, kv_head), blocks_all)[:NV].astype(jnp.int32))
    return jnp.stack(rows_list).astype(jnp.int32)


def draw_slash_offsets(key, part):
    own = jax.random.fold_in(key, 11)
    fixed_part = jnp.array([0, 1, SMAX - 1], jnp.int32)
    rows_list = []
    for kv_head in range(KVH):
        picks = jax.random.permutation(jax.random.fold_in(own, kv_head), SMAX - 3)[:NS - 3].astype(jnp.int32) + 2
        rows_list.append(jnp.concatenate([fixed_part, picks]))
    return jnp.stack(rows_list).astype(jnp.int32)


def levels(own_key, dims, split, smallest, high):
    gain, own = 1.0, jax.random.fold_in(own_key, 6)
    for axis_at, parts in split:
        draws = jnp.exp(jax.random.uniform(jax.random.fold_in(own, axis_at), (parts,), jnp.float32, smallest / len(split), high / len(split)))
        gain = gain * jnp.repeat(draws, dims[axis_at] // parts).reshape([-1 if axis == axis_at else 1 for axis in range(len(dims))])
    return gain


def scatter_about(key, dims, deviation, reach, pieces=(), kind=jnp.bfloat16):
    values = jax.random.normal(key, dims, jnp.float32) * deviation
    if len(pieces) > 0:
        values = levels(key, dims, pieces, -0.22, 0.18) * values
    return jnp.clip(values, min=-reach, max=reach).astype(kind)


def setup_inputs(seed: int = 0, part: int = 0) -> dict:
    key_of = jax.random.split(jax.random.key(seed), 8)
    own_keys = jax.random.split(jax.random.fold_in(key_of[7], part), 8)
    return {
        "queries": draw_queries(jax.random.fold_in(jax.random.fold_in(key_of[7], part), 71), part),
        "span_keys": draw_span_keys(jax.random.fold_in(jax.random.fold_in(key_of[7], part), 71), part),
        "span_values": scatter_about(own_keys[2], (NQ, KVH * HD), 16.0, 96.0, ((0, 16),)),
        "cache_keys": draw_cache_keys(jax.random.fold_in(jax.random.fold_in(key_of[7], part), 71), part),
        "cache_values": scatter_about(own_keys[4], (NCTX, KVH * HD), 16.0, 96.0, ((0, 16),)),
        "vertical_blocks": draw_vertical_blocks(jax.random.fold_in(jax.random.fold_in(key_of[7], part), 71), part),
        "slash_offsets": draw_slash_offsets(jax.random.fold_in(jax.random.fold_in(key_of[7], part), 71), part),
    }


def band_mask(offset_row, tile_first):
    query_ids = jnp.arange(QDEV, dtype=jnp.int32)[:, None]
    key_ids = jnp.arange(SMAX + QDEV, dtype=jnp.int32)[None, :]
    distance = query_ids + SMAX - key_ids
    table = jnp.zeros((SMAX,), jnp.bool_).at[offset_row].set(True)
    inside = (distance >= 0) & (distance < SMAX)
    chosen = inside & table[jnp.clip(distance, 0, SMAX - 1)]
    return chosen & (key_ids >= SMAX * tile_first)

def attend_tile(query_tile, key_sets, value_sets, offsets, tile_first):
    factor = 1.0 / math.sqrt(HD)
    grouped = query_tile.reshape(QDEV, KVH, GROUP, HD)
    results = []
    for kv_head in range(KVH):
        query_rows = grouped[:, kv_head].transpose(1, 0, 2).reshape(GROUP * QDEV, HD)
        scores = jnp.dot(query_rows, key_sets[kv_head].T, preferred_element_type=jnp.float32) * factor
        scores = scores.reshape(GROUP, QDEV, -1)
        allowed = jnp.concatenate([jnp.ones((QDEV, NV * VBLOCK), jnp.bool_), band_mask(offsets[kv_head], tile_first)], axis=1)
        scores = jnp.where(allowed[None], scores, -jnp.inf)
        largest = lax.optimization_barrier(jnp.max(scores, axis=-1, keepdims=True))
        expos = jnp.exp(scores - largest)
        weights = (expos / lax.optimization_barrier(jnp.sum(expos, axis=-1, keepdims=True))).astype(jnp.bfloat16)
        mixed = jnp.dot(weights.reshape(GROUP * QDEV, -1), value_sets[kv_head], preferred_element_type=jnp.float32)
        results.append(mixed.reshape(GROUP, QDEV, HD).transpose(1, 0, 2))
    return jnp.stack(results, axis=1).reshape(QDEV, KVH * GROUP * HD).astype(jnp.bfloat16)

def reference(queries, span_keys, span_values, cache_keys, cache_values, vertical_blocks, slash_offsets):
    cache_k = cache_keys.reshape(NCTX // VBLOCK, VBLOCK, KVH, HD)
    cache_v = cache_values.reshape(NCTX // VBLOCK, VBLOCK, KVH, HD)
    vert_k = [cache_k[vertical_blocks[kv_head], :, kv_head, :].reshape(NV * VBLOCK, HD) for kv_head in range(KVH)]
    vert_v = [cache_v[vertical_blocks[kv_head], :, kv_head, :].reshape(NV * VBLOCK, HD) for kv_head in range(KVH)]
    padding = jnp.zeros((SMAX, KVH * HD), jnp.bfloat16)
    padded_k = jnp.concatenate([padding, span_keys], axis=0)
    padded_v = jnp.concatenate([padding, span_values], axis=0)

    def one_tile(tile):
        start = (tile * QDEV).astype(jnp.int32)
        query_tile = lax.dynamic_slice_in_dim(queries, start, QDEV, 0)
        band_k = lax.dynamic_slice_in_dim(padded_k, start, SMAX + QDEV, 0).reshape(SMAX + QDEV, KVH, HD)
        band_v = lax.dynamic_slice_in_dim(padded_v, start, SMAX + QDEV, 0).reshape(SMAX + QDEV, KVH, HD)
        key_sets = [jnp.concatenate([vert_k[kv_head], band_k[:, kv_head, :]], axis=0) for kv_head in range(KVH)]
        value_sets = [jnp.concatenate([vert_v[kv_head], band_v[:, kv_head, :]], axis=0) for kv_head in range(KVH)]
        tile_first = (tile == 0).astype(jnp.int32)
        return attend_tile(query_tile, key_sets, value_sets, slash_offsets, tile_first)
    tiles = lax.map(one_tile, jnp.arange(NQ // QDEV, dtype=jnp.int32))
    return tiles.reshape(NQ, QH * HD)
```

```python
import functools
import math

import jax
import jax.numpy as jnp
from jax import lax
from jax.experimental import pallas as pl
from jax.experimental.pallas import tpu as pltpu
from jax.sharding import PartitionSpec as P

KVH = 4
GROUP = 8
HD = 128
QDEV = 128
VBLOCK = 64
NV = 16
NS = 64
SMAX = 128
ENTRIES = KVH * NV
FACTOR = math.log2(math.e) / math.sqrt(HD)
LOW = -1e38

ANY = pl.BlockSpec(memory_space=pl.ANY)
SMEM = pl.BlockSpec(memory_space=pltpu.SMEM)


def band_mask(offsets_ref, head, first):
    columns = lax.broadcasted_iota(jnp.int32, (8, SMAX + QDEV), 1)
    distance = SMAX - columns
    row = jnp.zeros((8, SMAX + QDEV), jnp.int32)
    for at in range(NS):
        row = jnp.where(distance == offsets_ref[head, at], 1, row)
    rows = jnp.concatenate([row] * (QDEV // 8), axis=0)
    rolled = pltpu.roll(rows, 0, 1, stride=1, stride_axis=0)
    keys = lax.broadcasted_iota(jnp.int32, (QDEV, SMAX + QDEV), 1)
    return (rolled > 0) & (keys >= jnp.where(first, SMAX, 0))


def attend_rows(rows, keys, values_ones, mask):
    scores = lax.dot_general(
        rows, keys, (((1,), (1,)), ((), ())), preferred_element_type=jnp.float32
    )
    if mask is not None:
        wide = scores.shape[1] - mask.shape[1]
        reps = rows.shape[0] // QDEV
        tiled = jnp.concatenate([mask] * reps, axis=0)
        band = jnp.where(tiled, scores[:, wide:], LOW)
        scores = jnp.concatenate([scores[:, :wide], band], axis=1)
    largest = jnp.max(scores, axis=1, keepdims=True) * FACTOR
    weights = jnp.exp2(scores * FACTOR - largest).astype(jnp.bfloat16)
    mixed = jnp.dot(weights, values_ones, preferred_element_type=jnp.float32)
    return largest, mixed


def dense_kernel(
    offsets, queries, keys, values, before_k, own_k, before_v, own_v, out, kbuf, vbuf
):
    head = pl.program_id(0)
    first = lax.axis_index("ctx") == 0
    wide = NV * VBLOCK
    kbuf[:wide] = keys[0]
    kbuf[wide : wide + SMAX] = before_k[...]
    kbuf[wide + SMAX :] = own_k[...]
    vbuf[:wide, :HD] = values[0]
    vbuf[wide : wide + SMAX, :HD] = before_v[...]
    vbuf[wide + SMAX :, :HD] = own_v[...]
    vbuf[:, HD:] = jnp.ones((wide + SMAX + QDEV, HD), jnp.bfloat16)
    mask = band_mask(offsets, head, first)
    for at in range(0, GROUP, 2):
        rows = jnp.concatenate(
            [queries[:, (at + i) * HD : (at + i + 1) * HD] for i in range(2)], axis=0
        )
        _, mixed = attend_rows(rows, kbuf[...], vbuf[...], mask)
        result = (mixed[:, :HD] / mixed[:, HD:]).astype(jnp.bfloat16)
        for i in range(2):
            out[:, (at + i) * HD : (at + i + 1) * HD] = result[i * QDEV : (i + 1) * QDEV]


def head_block(rows):
    return pl.BlockSpec((rows, HD), lambda head: (0, head))


def attend_dense(offsets, queries, keys, values, bands):
    wide = NV * VBLOCK
    return pl.pallas_call(
        dense_kernel,
        grid=(KVH,),
        out_shape=jax.ShapeDtypeStruct(queries.shape, jnp.bfloat16),
        in_specs=[
            SMEM,
            pl.BlockSpec((QDEV, GROUP * HD), lambda head: (0, head)),
            pl.BlockSpec((1, wide, HD), lambda head: (head, 0, 0)),
            pl.BlockSpec((1, wide, HD), lambda head: (head, 0, 0)),
        ]
        + [head_block(QDEV)] * 4,
        out_specs=pl.BlockSpec((QDEV, GROUP * HD), lambda head: (0, head)),
        scratch_shapes=[
            pltpu.VMEM((wide + SMAX + QDEV, HD), jnp.bfloat16),
            pltpu.VMEM((wide + SMAX + QDEV, 2 * HD), jnp.bfloat16),
        ],
        compiler_params=pltpu.CompilerParams(vmem_limit_bytes=48 * 2**20),
        name="attend_dense",
    )(offsets, queries, keys, values, *bands)


def owned_kernel(per_device, blocks, cache_k, cache_v, out_k, out_v, sems):
    me = lax.axis_index("ctx")
    out_k[...] = jnp.zeros_like(out_k)
    out_v[...] = jnp.zeros_like(out_v)

    def copies(entry):
        head, at = entry // NV, entry % NV
        block = blocks[head, at]
        local = block % per_device
        rows = pl.ds(pl.multiple_of(local * VBLOCK, VBLOCK), VBLOCK)
        columns = pl.ds(pl.multiple_of(head * HD, HD), HD)
        pairs = ((cache_k, out_k, 0), (cache_v, out_v, 1))
        return block // per_device == me, [
            pltpu.make_async_copy(source.at[rows, columns], target.at[entry], sems.at[entry, i])
            for source, target, i in pairs
        ]

    def start(entry, carry):
        mine, both = copies(entry)

        @pl.when(mine)
        def _():
            for copy in both:
                copy.start()

        return carry

    def wait(entry, carry):
        mine, both = copies(entry)

        @pl.when(mine)
        def _():
            for copy in both:
                copy.wait()

        return carry

    lax.fori_loop(0, ENTRIES, start, 0)
    lax.fori_loop(0, ENTRIES, wait, 0)


def owned_blocks(blocks, cache_k, cache_v):
    shape = jax.ShapeDtypeStruct((ENTRIES, VBLOCK, HD), jnp.bfloat16)
    whole = pl.BlockSpec(memory_space=pltpu.VMEM)
    return pl.pallas_call(
        functools.partial(owned_kernel, cache_k.shape[0] // VBLOCK),
        out_shape=(shape, shape),
        in_specs=[SMEM, ANY, ANY],
        out_specs=(whole, whole),
        scratch_shapes=[pltpu.SemaphoreType.DMA((ENTRIES, 2))],
        compiler_params=pltpu.CompilerParams(vmem_limit_bytes=16 * 2**20),
        name="owned_blocks",
    )(blocks, cache_k, cache_v)


def permuted(array, pairs):
    return lax.ppermute(array, "ctx", pairs)


def general(queries, bands, cache_k, cache_v, blocks, offsets):
    mine = owned_blocks(blocks, cache_k, cache_v)
    keys, values = lax.psum(mine, "ctx")
    keys = keys.reshape(KVH, NV * VBLOCK, HD)
    values = values.reshape(KVH, NV * VBLOCK, HD)
    return attend_dense(offsets, queries, keys, values, bands)


def shards(queries, span_k, span_v, cache_k, cache_v, blocks, offsets):
    peers = lax.axis_size("ctx")
    ahead = [(i, i + 1) for i in range(peers - 1)]
    bands = (permuted(span_k, ahead), span_k, permuted(span_v, ahead), span_v)
    return general(queries, bands, cache_k, cache_v, blocks, offsets)


def solution(mesh):
    rows = P(("groups", "ctx"), None)
    heads = P("groups", None)
    return jax.shard_map(
        shards,
        mesh=mesh,
        in_specs=(rows, rows, rows, rows, rows, heads, heads),
        out_specs=rows,
        check_vma=False,
    )
```

```python
import functools
import math

import jax
import jax.numpy as jnp
from jax import lax
from jax.experimental import pallas as pl
from jax.experimental.pallas import tpu as pltpu
from jax.sharding import PartitionSpec as P

KVH = 4
GROUP = 8
HD = 128
QDEV = 128
VBLOCK = 64
NV = 16
NS = 64
SMAX = 128
ENTRIES = KVH * NV
FACTOR = math.log2(math.e) / math.sqrt(HD)
LOW = -1e38

ANY = pl.BlockSpec(memory_space=pl.ANY)
SMEM = pl.BlockSpec(memory_space=pltpu.SMEM)


def band_mask(offsets_ref, head, first):
    columns = lax.broadcasted_iota(jnp.int32, (8, SMAX + QDEV), 1)
    distance = SMAX - columns
    row = jnp.zeros((8, SMAX + QDEV), jnp.int32)
    for at in range(NS):
        row = jnp.where(distance == offsets_ref[head, at], 1, row)
    rows = jnp.concatenate([row] * (QDEV // 8), axis=0)
    rolled = pltpu.roll(rows, 0, 1, stride=1, stride_axis=0)
    keys = lax.broadcasted_iota(jnp.int32, (QDEV, SMAX + QDEV), 1)
    return (rolled > 0) & (keys >= jnp.where(first, SMAX, 0))


def attend_rows(rows, keys, values_ones, mask):
    scores = lax.dot_general(
        rows, keys, (((1,), (1,)), ((), ())), preferred_element_type=jnp.float32
    )
    if mask is not None:
        wide = scores.shape[1] - mask.shape[1]
        reps = rows.shape[0] // QDEV
        tiled = jnp.concatenate([mask] * reps, axis=0)
        band = jnp.where(tiled, scores[:, wide:], LOW)
        scores = jnp.concatenate([scores[:, :wide], band], axis=1)
    largest = jnp.max(scores, axis=1, keepdims=True) * FACTOR
    weights = jnp.exp2(scores * FACTOR - largest).astype(jnp.bfloat16)
    mixed = jnp.dot(weights, values_ones, preferred_element_type=jnp.float32)
    return largest, mixed


def dense_kernel(
    offsets, queries, keys, values, before_k, own_k, before_v, own_v, out, kbuf, vbuf
):
    head = pl.program_id(0)
    first = lax.axis_index("ctx") == 0
    wide = NV * VBLOCK
    kbuf[:wide] = keys[0]
    kbuf[wide : wide + SMAX] = before_k[...]
    kbuf[wide + SMAX :] = own_k[...]
    vbuf[:wide, :HD] = values[0]
    vbuf[wide : wide + SMAX, :HD] = before_v[...]
    vbuf[wide + SMAX :, :HD] = own_v[...]
    vbuf[:, HD:] = jnp.ones((wide + SMAX + QDEV, HD), jnp.bfloat16)
    mask = band_mask(offsets, head, first)
    for at in range(0, GROUP, 2):
        rows = jnp.concatenate(
            [queries[:, (at + i) * HD : (at + i + 1) * HD] for i in range(2)], axis=0
        )
        _, mixed = attend_rows(rows, kbuf[...], vbuf[...], mask)
        result = (mixed[:, :HD] / mixed[:, HD:]).astype(jnp.bfloat16)
        for i in range(2):
            out[:, (at + i) * HD : (at + i + 1) * HD] = result[i * QDEV : (i + 1) * QDEV]


def head_block(rows):
    return pl.BlockSpec((rows, HD), lambda head: (0, head))


def attend_dense(offsets, queries, keys, values, bands):
    wide = NV * VBLOCK
    return pl.pallas_call(
        dense_kernel,
        grid=(KVH,),
        out_shape=jax.ShapeDtypeStruct(queries.shape, jnp.bfloat16),
        in_specs=[
            SMEM,
            pl.BlockSpec((QDEV, GROUP * HD), lambda head: (0, head)),
            pl.BlockSpec((1, wide, HD), lambda head: (head, 0, 0)),
            pl.BlockSpec((1, wide, HD), lambda head: (head, 0, 0)),
        ]
        + [head_block(QDEV)] * 4,
        out_specs=pl.BlockSpec((QDEV, GROUP * HD), lambda head: (0, head)),
        scratch_shapes=[
            pltpu.VMEM((wide + SMAX + QDEV, HD), jnp.bfloat16),
            pltpu.VMEM((wide + SMAX + QDEV, 2 * HD), jnp.bfloat16),
        ],
        compiler_params=pltpu.CompilerParams(vmem_limit_bytes=48 * 2**20),
        name="attend_dense",
    )(offsets, queries, keys, values, *bands)


def owned_kernel(per_device, blocks, cache_k, cache_v, out_k, out_v, sems):
    me = lax.axis_index("ctx")
    out_k[...] = jnp.zeros_like(out_k)
    out_v[...] = jnp.zeros_like(out_v)

    def copies(entry):
        head, at = entry // NV, entry % NV
        block = blocks[head, at]
        local = block % per_device
        rows = pl.ds(pl.multiple_of(local * VBLOCK, VBLOCK), VBLOCK)
        columns = pl.ds(pl.multiple_of(head * HD, HD), HD)
        pairs = ((cache_k, out_k, 0), (cache_v, out_v, 1))
        return block // per_device == me, [
            pltpu.make_async_copy(source.at[rows, columns], target.at[entry], sems.at[entry, i])
            for source, target, i in pairs
        ]

    def start(entry, carry):
        mine, both = copies(entry)

        @pl.when(mine)
        def _():
            for copy in both:
                copy.start()

        return carry

    def wait(entry, carry):
        mine, both = copies(entry)

        @pl.when(mine)
        def _():
            for copy in both:
                copy.wait()

        return carry

    lax.fori_loop(0, ENTRIES, start, 0)
    lax.fori_loop(0, ENTRIES, wait, 0)


def owned_blocks(blocks, cache_k, cache_v):
    shape = jax.ShapeDtypeStruct((ENTRIES, VBLOCK, HD), jnp.bfloat16)
    whole = pl.BlockSpec(memory_space=pltpu.VMEM)
    return pl.pallas_call(
        functools.partial(owned_kernel, cache_k.shape[0] // VBLOCK),
        out_shape=(shape, shape),
        in_specs=[SMEM, ANY, ANY],
        out_specs=(whole, whole),
        scratch_shapes=[pltpu.SemaphoreType.DMA((ENTRIES, 2))],
        compiler_params=pltpu.CompilerParams(vmem_limit_bytes=16 * 2**20),
        name="owned_blocks",
    )(blocks, cache_k, cache_v)


STAGES = 2
ROWS = VBLOCK // STAGES
WHOLE = pl.BlockSpec(memory_space=pltpu.VMEM)


def room(share):
    mean = ENTRIES * share
    wide = mean + 3.0 * math.sqrt(mean * (1.0 - share)) + 1.5
    return min(ENTRIES, math.ceil(wide))


def owner_of(blocks, entry, per_device):
    return lax.div(blocks[entry // NV, entry % NV], per_device)


def pack_kernel(per_device, limit, blocks, cache_k, cache_v, kept, sent, sems):
    me = lax.axis_index("ctx")
    odd = lax.rem(me, 2)

    def each(act):
        def step(entry, count):
            head = entry // NV
            block = blocks[head, entry % NV]
            owner = lax.div(block, per_device)
            mine = owner == me
            local = block - owner * per_device
            columns = pl.ds(pl.multiple_of(head * HD, HD), HD)

            @pl.when(mine & (count < limit))
            def _():
                for parity, pair in enumerate(((cache_k, cache_v), (cache_v, cache_k))):

                    @pl.when(odd == parity)
                    def _(pair=pair):
                        for stage in range(STAGES):
                            rows = pl.ds(pl.multiple_of(local * VBLOCK + stage * ROWS, ROWS), ROWS)
                            for i, target in enumerate((kept, sent)):
                                act(
                                    pltpu.make_async_copy(
                                        pair[i].at[rows, columns],
                                        target.at[stage, count],
                                        sems.at[count, stage, i],
                                    )
                                )

            return count + mine.astype(jnp.int32)

        lax.fori_loop(0, ENTRIES, step, 0)

    each(lambda copy: copy.start())
    each(lambda copy: copy.wait())


def pack(blocks, cache_k, cache_v, limit):
    shape = jax.ShapeDtypeStruct((STAGES, limit, ROWS, HD), jnp.bfloat16)
    return pl.pallas_call(
        functools.partial(pack_kernel, cache_k.shape[0] // VBLOCK, limit),
        out_shape=(shape, shape),
        in_specs=[SMEM, ANY, ANY],
        out_specs=(WHOLE, WHOLE),
        scratch_shapes=[pltpu.SemaphoreType.DMA((limit, STAGES, 2))],
        compiler_params=pltpu.CompilerParams(vmem_limit_bytes=16 * 2**20),
        name="pack",
    )(blocks, cache_k, cache_v)


def merge_loop(blocks, per_device, known, bit, limit, copy_mine, copy_other):
    me = lax.axis_index("ctx")

    def step(entry, carry):
        at_mine, at_other = carry
        away = (owner_of(blocks, entry, per_device) ^ me) & ~known
        mine, other = away == 0, away == bit
        place = at_mine + at_other

        @pl.when(mine & (at_mine < limit))
        def _():
            copy_mine(entry, at_mine, place)

        @pl.when(other & (at_other < limit))
        def _():
            copy_other(entry, at_other, place)

        return at_mine + mine.astype(jnp.int32), at_other + other.astype(jnp.int32)

    lax.fori_loop(0, ENTRIES, step, (0, 0))


def merge_kernel(per_device, known, bit, limit, blocks, mine, other, *outs):
    def copied(source):
        def copy(entry, at, place):
            @pl.when(place < outs[0].shape[0])
            def _():
                if len(outs) == 1:
                    outs[0][place] = source[at]
                else:
                    for stage, out in enumerate(outs):
                        out[place] = source[stage, at]

        return copy

    merge_loop(blocks, per_device, known, bit, limit, copied(mine), copied(other))


def merged(blocks, per_device, known, bit, mine, other, size):
    count = STAGES if mine.ndim == 4 else 1
    shape = jax.ShapeDtypeStruct((size, ROWS, HD), jnp.bfloat16)
    return pl.pallas_call(
        functools.partial(merge_kernel, per_device, known, bit, mine.shape[-3]),
        out_shape=(shape,) * count,
        in_specs=[SMEM, WHOLE, WHOLE],
        out_specs=(WHOLE,) * count,
        compiler_params=pltpu.CompilerParams(vmem_limit_bytes=16 * 2**20),
        name="merge",
    )(blocks, mine, other)


def stage_kernel(per_device, known, bit, banded, last, *refs):
    refs = list(refs)
    blocks = refs.pop(0)
    offsets = refs.pop(0) if banded else None
    queries, mine, other, mine_twin, other_twin = refs[:5]
    refs = refs[5:]
    if banded:
        before_k, before_v, own_k, own_v = refs[:4]
        refs = refs[4:]
    else:
        largest_in, mixed_in = refs[:2]
        refs = refs[2:]
    outs, (kbuf, vbuf) = refs[:-2], refs[-2:]
    head = pl.program_id(0)
    me = lax.axis_index("ctx")
    wide = NV * ROWS

    @pl.when(head == 0)
    def _():
        def assemble(first, second):
            def copied(pair):
                def copy(entry, at, place):
                    rows = pl.ds(pl.multiple_of(lax.rem(entry, NV) * ROWS, ROWS), ROWS)
                    first[entry // NV, rows, :HD] = pair[0][at]
                    second[entry // NV, rows, :HD] = pair[1][at]

                return copy

            merge_loop(
                blocks,
                per_device,
                known,
                bit,
                mine.shape[0],
                copied((mine, mine_twin)),
                copied((other, other_twin)),
            )

        @pl.when(lax.rem(me, 2) == 0)
        def _():
            assemble(kbuf, vbuf)

        @pl.when(lax.rem(me, 2) == 1)
        def _():
            assemble(vbuf, kbuf)

        for at in range(KVH):
            vbuf[at, :, HD:] = jnp.ones((vbuf.shape[1], HD), jnp.bfloat16)

    mask = None
    if banded:
        kbuf[head, wide : wide + SMAX] = before_k[...]
        kbuf[head, wide + SMAX :] = own_k[...]
        vbuf[head, wide : wide + SMAX, :HD] = before_v[...]
        vbuf[head, wide + SMAX :, :HD] = own_v[...]
        mask = band_mask(offsets, head, me == 0)
    for at in range(0, GROUP, 2):
        rows = jnp.concatenate(
            [queries[:, (at + i) * HD : (at + i + 1) * HD] for i in range(2)], axis=0
        )
        tile = slice(at * QDEV, (at + 2) * QDEV)
        largest, mixed = attend_rows(rows, kbuf[head], vbuf[head], mask)
        if not banded:
            before = largest_in[tile, :1]
            above = jnp.maximum(before, largest)
            mixed = mixed * jnp.exp2(largest - above) + mixed_in[tile] * jnp.exp2(before - above)
            largest = above
        if last:
            result = (mixed[:, :HD] / mixed[:, HD:]).astype(jnp.bfloat16)
            for i in range(2):
                outs[0][:, (at + i) * HD : (at + i + 1) * HD] = result[i * QDEV : (i + 1) * QDEV]
        else:
            outs[0][tile] = jnp.broadcast_to(largest, (2 * QDEV, HD))
            outs[1][tile] = mixed


def attend_stage(known, bit, per_device, blocks, queries, lists, offsets=None, bands=None, state=None):
    banded, last = bands is not None, state is not None
    tall = GROUP * QDEV
    head_rows = pl.BlockSpec((QDEV, GROUP * HD), lambda head: (0, head))
    specs = [SMEM] + [SMEM] * banded + [head_rows] + [WHOLE] * 4
    args = [blocks] + [offsets] * banded + [queries, *lists]
    states = [
        pl.BlockSpec((tall, HD), lambda head: (head, 0)),
        pl.BlockSpec((tall, 2 * HD), lambda head: (head, 0)),
    ]
    if banded:
        before, own_k, own_v = bands
        second = pl.BlockSpec((QDEV, HD), lambda head: (0, head + KVH))
        specs += [head_block(QDEV), second, head_block(QDEV), head_block(QDEV)]
        args += [before, before, own_k, own_v]
    else:
        specs += states
        args += state
    if last:
        out_shape = jax.ShapeDtypeStruct(queries.shape, jnp.bfloat16)
        out_specs = head_rows
    else:
        out_shape = (
            jax.ShapeDtypeStruct((KVH * tall, HD), jnp.float32),
            jax.ShapeDtypeStruct((KVH * tall, 2 * HD), jnp.float32),
        )
        out_specs = tuple(states)
    keys = NV * ROWS + (SMAX + QDEV) * banded
    return pl.pallas_call(
        functools.partial(stage_kernel, per_device, known, bit, banded, last),
        grid=(KVH,),
        out_shape=out_shape,
        in_specs=specs,
        out_specs=out_specs,
        scratch_shapes=[
            pltpu.VMEM((KVH, keys, HD), jnp.bfloat16),
            pltpu.VMEM((KVH, keys, 2 * HD), jnp.bfloat16),
        ],
        compiler_params=pltpu.CompilerParams(vmem_limit_bytes=48 * 2**20),
        cost_estimate=pl.CostEstimate(
            flops=4 * KVH * tall * keys * HD,
            bytes_accessed=8 * 2**20,
            transcendentals=KVH * tall * keys,
        ),
        name="attend_last" if last else "attend_first",
    )(*args)


def permuted(array, pairs):
    return lax.ppermute(array, "ctx", pairs)


def swapped(array, bit):
    return permuted(array, [(i, i ^ bit) for i in range(lax.axis_size("ctx"))])


def fits(blocks, per_device, peers, bits):
    owners = (blocks // per_device).reshape(1, ENTRIES)
    ids = jnp.arange(peers, dtype=jnp.int32)[:, None]
    fine = jnp.bool_(True)
    known = 0
    for bit in [0] + bits[:-1]:
        known |= bit
        counts = jnp.sum((((owners ^ ids) & ~known) == 0).astype(jnp.int32), axis=1)
        fine &= jnp.max(counts) <= room((1 << known.bit_count()) / peers)
    return fine


def general(queries, bands, cache_k, cache_v, blocks, offsets):
    mine = owned_blocks(blocks, cache_k, cache_v)
    keys, values = lax.psum(mine, "ctx")
    keys = keys.reshape(KVH, NV * VBLOCK, HD)
    values = values.reshape(KVH, NV * VBLOCK, HD)
    before, own_k, own_v = bands
    wide = KVH * HD
    bands = (before[:, :wide], own_k, before[:, wide:], own_v)
    return attend_dense(offsets, queries, keys, values, bands)


def shards(queries, span_k, span_v, cache_k, cache_v, blocks, offsets):
    peers = lax.axis_size("ctx")
    per_device = cache_k.shape[0] // VBLOCK
    ahead = [(i, i + 1) for i in range(peers - 1)]
    bits = [1] + [1 << at for at in range(peers.bit_length() - 2, 0, -1)]

    kept, sent = pack(blocks, cache_k, cache_v, room(1 / peers))
    other = swapped(sent, 1)
    lists = merged(blocks, per_device, 0, 1, kept, other, room(2 / peers))
    known = 1
    pairs = []
    for mine in lists:
        known = 1
        for bit in bits[1:]:
            other = swapped(mine, bit)
            if bit == bits[-1]:
                break
            share = (1 << (known | bit).bit_count()) / peers
            (mine,) = merged(blocks, per_device, known, bit, mine, other, room(share))
            known |= bit
        pairs.append((mine, other, swapped(mine, 1), swapped(other, 1)))

    before = permuted(jnp.concatenate([span_k, span_v], axis=1), ahead)
    bands = (before, span_k, span_v)
    shared = (known, bits[-1], per_device, blocks, queries)
    state = attend_stage(*shared, pairs[0], offsets=offsets, bands=bands)
    return lax.cond(
        fits(blocks, per_device, peers, bits),
        lambda: attend_stage(*shared, pairs[1], state=state),
        lambda: general(queries, bands, cache_k, cache_v, blocks, offsets),
    )


def solution(mesh):
    rows = P(("groups", "ctx"), None)
    heads = P("groups", None)
    return jax.shard_map(
        shards,
        mesh=mesh,
        in_specs=(rows, rows, rows, rows, rows, heads, heads),
        out_specs=rows,
        check_vma=False,
    )
```

```python
import functools
import math

import jax
import jax.numpy as jnp
from jax import lax
from jax.experimental import pallas as pl
from jax.experimental.pallas import tpu as pltpu
from jax.sharding import PartitionSpec as P

KVH = 4
GROUP = 8
HD = 128
QDEV = 128
VBLOCK = 64
NV = 16
NS = 64
SMAX = 128
ENTRIES = KVH * NV
FACTOR = math.log2(math.e) / math.sqrt(HD)
LOW = -1e38

ANY = pl.BlockSpec(memory_space=pl.ANY)
SMEM = pl.BlockSpec(memory_space=pltpu.SMEM)


def band_mask(offsets_ref, head, first):
    columns = lax.broadcasted_iota(jnp.int32, (8, SMAX + QDEV), 1)
    distance = SMAX - columns
    row = jnp.zeros((8, SMAX + QDEV), jnp.int32)
    for at in range(NS):
        row = jnp.where(distance == offsets_ref[head, at], 1, row)
    rows = jnp.concatenate([row] * (QDEV // 8), axis=0)
    rolled = pltpu.roll(rows, 0, 1, stride=1, stride_axis=0)
    keys = lax.broadcasted_iota(jnp.int32, (QDEV, SMAX + QDEV), 1)
    return (rolled > 0) & (keys >= jnp.where(first, SMAX, 0))


def attend_rows(rows, keys, values_ones, mask):
    scores = lax.dot_general(
        rows, keys, (((1,), (1,)), ((), ())), preferred_element_type=jnp.float32
    )
    if mask is not None:
        wide = scores.shape[1] - mask.shape[1]
        reps = rows.shape[0] // QDEV
        tiled = jnp.concatenate([mask] * reps, axis=0)
        band = jnp.where(tiled, scores[:, wide:], LOW)
        scores = jnp.concatenate([scores[:, :wide], band], axis=1)
    largest = jnp.max(scores, axis=1, keepdims=True) * FACTOR
    weights = jnp.exp2(scores * FACTOR - largest).astype(jnp.bfloat16)
    mixed = jnp.dot(weights, values_ones, preferred_element_type=jnp.float32)
    return largest, mixed


def dense_kernel(
    offsets, queries, keys, values, before_k, own_k, before_v, own_v, out, kbuf, vbuf
):
    head = pl.program_id(0)
    first = lax.axis_index("ctx") == 0
    wide = NV * VBLOCK
    kbuf[:wide] = keys[0]
    kbuf[wide : wide + SMAX] = before_k[...]
    kbuf[wide + SMAX :] = own_k[...]
    vbuf[:wide, :HD] = values[0]
    vbuf[wide : wide + SMAX, :HD] = before_v[...]
    vbuf[wide + SMAX :, :HD] = own_v[...]
    vbuf[:, HD:] = jnp.ones((wide + SMAX + QDEV, HD), jnp.bfloat16)
    mask = band_mask(offsets, head, first)
    for at in range(0, GROUP, 2):
        rows = jnp.concatenate(
            [queries[:, (at + i) * HD : (at + i + 1) * HD] for i in range(2)], axis=0
        )
        _, mixed = attend_rows(rows, kbuf[...], vbuf[...], mask)
        result = (mixed[:, :HD] / mixed[:, HD:]).astype(jnp.bfloat16)
        for i in range(2):
            out[:, (at + i) * HD : (at + i + 1) * HD] = result[i * QDEV : (i + 1) * QDEV]


def head_block(rows):
    return pl.BlockSpec((rows, HD), lambda head: (0, head))


def attend_dense(offsets, queries, keys, values, bands):
    wide = NV * VBLOCK
    return pl.pallas_call(
        dense_kernel,
        grid=(KVH,),
        out_shape=jax.ShapeDtypeStruct(queries.shape, jnp.bfloat16),
        in_specs=[
            SMEM,
            pl.BlockSpec((QDEV, GROUP * HD), lambda head: (0, head)),
            pl.BlockSpec((1, wide, HD), lambda head: (head, 0, 0)),
            pl.BlockSpec((1, wide, HD), lambda head: (head, 0, 0)),
        ]
        + [head_block(QDEV)] * 4,
        out_specs=pl.BlockSpec((QDEV, GROUP * HD), lambda head: (0, head)),
        scratch_shapes=[
            pltpu.VMEM((wide + SMAX + QDEV, HD), jnp.bfloat16),
            pltpu.VMEM((wide + SMAX + QDEV, 2 * HD), jnp.bfloat16),
        ],
        compiler_params=pltpu.CompilerParams(vmem_limit_bytes=48 * 2**20),
        name="attend_dense",
    )(offsets, queries, keys, values, *bands)


def owned_kernel(per_device, blocks, cache_k, cache_v, out_k, out_v, sems):
    me = lax.axis_index("ctx")
    out_k[...] = jnp.zeros_like(out_k)
    out_v[...] = jnp.zeros_like(out_v)

    def copies(entry):
        head, at = entry // NV, entry % NV
        block = blocks[head, at]
        local = block % per_device
        rows = pl.ds(pl.multiple_of(local * VBLOCK, VBLOCK), VBLOCK)
        columns = pl.ds(pl.multiple_of(head * HD, HD), HD)
        pairs = ((cache_k, out_k, 0), (cache_v, out_v, 1))
        return block // per_device == me, [
            pltpu.make_async_copy(source.at[rows, columns], target.at[entry], sems.at[entry, i])
            for source, target, i in pairs
        ]

    def start(entry, carry):
        mine, both = copies(entry)

        @pl.when(mine)
        def _():
            for copy in both:
                copy.start()

        return carry

    def wait(entry, carry):
        mine, both = copies(entry)

        @pl.when(mine)
        def _():
            for copy in both:
                copy.wait()

        return carry

    lax.fori_loop(0, ENTRIES, start, 0)
    lax.fori_loop(0, ENTRIES, wait, 0)


def owned_blocks(blocks, cache_k, cache_v):
    shape = jax.ShapeDtypeStruct((ENTRIES, VBLOCK, HD), jnp.bfloat16)
    whole = pl.BlockSpec(memory_space=pltpu.VMEM)
    return pl.pallas_call(
        functools.partial(owned_kernel, cache_k.shape[0] // VBLOCK),
        out_shape=(shape, shape),
        in_specs=[SMEM, ANY, ANY],
        out_specs=(whole, whole),
        scratch_shapes=[pltpu.SemaphoreType.DMA((ENTRIES, 2))],
        compiler_params=pltpu.CompilerParams(vmem_limit_bytes=16 * 2**20),
        name="owned_blocks",
    )(blocks, cache_k, cache_v)


STAGES = 2
ROWS = VBLOCK // STAGES
WHOLE = pl.BlockSpec(memory_space=pltpu.VMEM)


def room(share):
    mean = ENTRIES * share
    wide = mean + 3.0 * math.sqrt(mean * (1.0 - share)) + 1.5
    return min(ENTRIES + 1, math.ceil(wide))


def owner_of(block, per_device):
    if per_device & (per_device - 1) == 0:
        return lax.shift_right_logical(block, per_device.bit_length() - 1)
    return lax.div(block, per_device)


def pack_kernel(per_device, limit, blocks, cache_k, cache_v, kept, sent, sems):
    me = lax.axis_index("ctx")
    even = lax.rem(me, 2) == 0
    count = jnp.int32(0)
    for entry in range(ENTRIES):
        head = entry // NV
        block = blocks[head, entry % NV]
        owner = owner_of(block, per_device)
        mine = owner == me
        local = block - owner * per_device

        def start(pair, head=head, local=local, count=count):
            rows = pl.ds(pl.multiple_of(local * VBLOCK, VBLOCK), VBLOCK)
            for i, target in enumerate((kept, sent)):
                source = pair[i].at[rows, pl.ds(head * HD, HD)]
                pltpu.make_async_copy(source, target.at[count], sems.at[count, i]).start()

        @pl.when(mine & (count < limit))
        def _(start=start):
            @pl.when(even)
            def _():
                start((cache_k, cache_v))

            @pl.when(jnp.logical_not(even))
            def _():
                start((cache_v, cache_k))

        count += mine.astype(jnp.int32)

    for at in range(limit):

        @pl.when(at < count)
        def _(at=at):
            for i, target in enumerate((kept, sent)):
                source = cache_k.at[pl.ds(0, VBLOCK), pl.ds(0, HD)]
                pltpu.make_async_copy(source, target.at[at], sems.at[at, i]).wait()


def pack(blocks, cache_k, cache_v, limit):
    shape = jax.ShapeDtypeStruct((limit, VBLOCK, HD), jnp.bfloat16)
    return pl.pallas_call(
        functools.partial(pack_kernel, cache_k.shape[0] // VBLOCK, limit),
        out_shape=(shape, shape),
        in_specs=[SMEM, ANY, ANY],
        out_specs=(WHOLE, WHOLE),
        scratch_shapes=[pltpu.SemaphoreType.DMA((limit, 2))],
        compiler_params=pltpu.CompilerParams(vmem_limit_bytes=16 * 2**20),
        name="pack",
    )(blocks, cache_k, cache_v)


def walk(blocks, per_device, known, bit, limits, act):
    me = lax.axis_index("ctx")
    at_mine = at_other = jnp.int32(0)
    for entry in range(ENTRIES):
        away = (owner_of(blocks[entry // NV, entry % NV], per_device) ^ me) & ~known
        mine, other = away == 0, away == bit
        tops = jnp.minimum(at_mine, limits[0] - 1), jnp.minimum(at_other, limits[1] - 1)
        act(entry, *tops, at_mine + at_other, other)
        at_mine += mine.astype(jnp.int32)
        at_other += other.astype(jnp.int32)


def merge_kernel(per_device, known, bit, blocks, mine, other, *outs):
    size = outs[0].shape[0]

    def act(entry, at_mine, at_other, place, theirs):
        tile = jnp.where(theirs, other[at_other], mine[at_mine])
        place = jnp.minimum(place, size - 1)
        for stage, out in enumerate(outs):
            out[place] = tile[stage * ROWS : (stage + 1) * ROWS]

    walk(blocks, per_device, known, bit, (mine.shape[0], other.shape[0]), act)


def merged(blocks, per_device, known, bit, mine, other, size):
    count = mine.shape[1] // ROWS
    shape = jax.ShapeDtypeStruct((size, ROWS, HD), jnp.bfloat16)
    return pl.pallas_call(
        functools.partial(merge_kernel, per_device, known, bit),
        out_shape=(shape,) * count,
        in_specs=[SMEM, WHOLE, WHOLE],
        out_specs=(WHOLE,) * count,
        compiler_params=pltpu.CompilerParams(vmem_limit_bytes=16 * 2**20),
        name="merge",
    )(blocks, mine, other)


def stage_kernel(per_device, known, bit, banded, last, *refs):
    refs = list(refs)
    blocks = refs.pop(0)
    offsets = refs.pop(0) if banded else None
    queries, mine, other, mine_twin, other_twin = refs[:5]
    refs = refs[5:]
    if banded:
        before_k, before_v, own_k, own_v = refs[:4]
        refs = refs[4:]
    else:
        largest_in, mixed_in = refs[:2]
        refs = refs[2:]
    outs, (kbuf, vbuf) = refs[:-2], refs[-2:]
    head = pl.program_id(0)
    me = lax.axis_index("ctx")
    wide = NV * ROWS

    @pl.when(head == 0)
    def _():
        even = lax.rem(me, 2) == 0

        def act(entry, at_mine, at_other, place, theirs):
            tile = jnp.where(theirs, other[at_other], mine[at_mine])
            twin = jnp.where(theirs, other_twin[at_other], mine_twin[at_mine])
            rows = pl.ds(entry % NV * ROWS, ROWS)
            kbuf[entry // NV, rows] = jnp.where(even, tile, twin)
            vbuf[entry // NV, rows, :HD] = jnp.where(even, twin, tile)

        walk(blocks, per_device, known, bit, (mine.shape[0], other.shape[0]), act)
        for at in range(KVH):
            vbuf[at, :, HD:] = jnp.ones((vbuf.shape[1], HD), jnp.bfloat16)

    mask = None
    if banded:
        kbuf[head, wide : wide + SMAX] = before_k[...]
        kbuf[head, wide + SMAX :] = own_k[...]
        vbuf[head, wide : wide + SMAX, :HD] = before_v[...]
        vbuf[head, wide + SMAX :, :HD] = own_v[...]
        mask = band_mask(offsets, head, me == 0)
    for at in range(0, GROUP, 2):
        rows = jnp.concatenate(
            [queries[:, (at + i) * HD : (at + i + 1) * HD] for i in range(2)], axis=0
        )
        tile = slice(at * QDEV, (at + 2) * QDEV)
        largest, mixed = attend_rows(rows, kbuf[head], vbuf[head], mask)
        if not banded:
            before = largest_in[tile, :1]
            above = jnp.maximum(before, largest)
            mixed = mixed * jnp.exp2(largest - above) + mixed_in[tile] * jnp.exp2(before - above)
            largest = above
        if last:
            result = (mixed[:, :HD] / mixed[:, HD:]).astype(jnp.bfloat16)
            for i in range(2):
                outs[0][:, (at + i) * HD : (at + i + 1) * HD] = result[i * QDEV : (i + 1) * QDEV]
        else:
            outs[0][tile] = jnp.broadcast_to(largest, (2 * QDEV, HD))
            outs[1][tile] = mixed


def attend_stage(known, bit, per_device, blocks, queries, lists, offsets=None, bands=None, state=None):
    banded, last = bands is not None, state is not None
    tall = GROUP * QDEV
    head_rows = pl.BlockSpec((QDEV, GROUP * HD), lambda head: (0, head))
    specs = [SMEM] + [SMEM] * banded + [head_rows] + [WHOLE] * 4
    args = [blocks] + [offsets] * banded + [queries, *lists]
    states = [
        pl.BlockSpec((tall, HD), lambda head: (head, 0)),
        pl.BlockSpec((tall, 2 * HD), lambda head: (head, 0)),
    ]
    if banded:
        before, own_k, own_v = bands
        second = pl.BlockSpec((QDEV, HD), lambda head: (0, head + KVH))
        specs += [head_block(QDEV), second, head_block(QDEV), head_block(QDEV)]
        args += [before, before, own_k, own_v]
    else:
        specs += states
        args += state
    if last:
        out_shape = jax.ShapeDtypeStruct(queries.shape, jnp.bfloat16)
        out_specs = head_rows
    else:
        out_shape = (
            jax.ShapeDtypeStruct((KVH * tall, HD), jnp.float32),
            jax.ShapeDtypeStruct((KVH * tall, 2 * HD), jnp.float32),
        )
        out_specs = tuple(states)
    keys = NV * ROWS + (SMAX + QDEV) * banded
    return pl.pallas_call(
        functools.partial(stage_kernel, per_device, known, bit, banded, last),
        grid=(KVH,),
        out_shape=out_shape,
        in_specs=specs,
        out_specs=out_specs,
        scratch_shapes=[
            pltpu.VMEM((KVH, keys, HD), jnp.bfloat16),
            pltpu.VMEM((KVH, keys, 2 * HD), jnp.bfloat16),
        ],
        compiler_params=pltpu.CompilerParams(vmem_limit_bytes=48 * 2**20),
        cost_estimate=pl.CostEstimate(
            flops=4 * KVH * tall * keys * HD,
            bytes_accessed=8 * 2**20,
            transcendentals=KVH * tall * keys,
        ),
        name="attend_last" if last else "attend_first",
    )(*args)


def permuted(array, pairs):
    return lax.ppermute(array, "ctx", pairs)


def swapped(array, bit):
    return permuted(array, [(i, i ^ bit) for i in range(lax.axis_size("ctx"))])


def fits(blocks, per_device, peers, bits):
    masks = [sum(bits[:at]) for at in range(len(bits))]
    most = [room((1 << at) / peers) - (at > 0) for at in range(len(bits))]
    owners = (blocks // per_device).reshape(1, 1, ENTRIES)
    ids = jnp.arange(peers, dtype=jnp.int32)[None, :, None]
    away = (owners ^ ids) & ~jnp.array(masks, jnp.int32)[:, None, None]
    counts = jnp.sum((away == 0).astype(jnp.int32), axis=2)
    return jnp.all(counts <= jnp.array(most, jnp.int32)[:, None])


def general(queries, bands, cache_k, cache_v, blocks, offsets, bits):
    keys, values = owned_blocks(blocks, cache_k, cache_v)
    for bit in bits:
        keys, values = keys + swapped(keys, bit), values + swapped(values, bit)
    keys = keys.reshape(KVH, NV * VBLOCK, HD)
    values = values.reshape(KVH, NV * VBLOCK, HD)
    before, own_k, own_v = bands
    wide = KVH * HD
    bands = (before[:, :wide], own_k, before[:, wide:], own_v)
    return attend_dense(offsets, queries, keys, values, bands)


def shards(queries, span_k, span_v, cache_k, cache_v, blocks, offsets):
    peers = lax.axis_size("ctx")
    per_device = cache_k.shape[0] // VBLOCK
    ahead = [(i, i + 1) for i in range(peers - 1)]
    bits = [1] + [1 << at for at in range(peers.bit_length() - 2, 0, -1)]

    kept, sent = pack(blocks, cache_k, cache_v, room(1 / peers))
    mine = list(merged(blocks, per_device, 0, 1, kept, swapped(sent, 1), room(2 / peers)))
    before = permuted(jnp.concatenate([span_k, span_v], axis=1), ahead)
    other = [None] * STAGES
    known = 1
    for bit in bits[1:]:
        other[0] = swapped(mine[0], bit)
        if bit == bits[1]:
            other[0], before = lax.optimization_barrier((other[0], before))
            other[0], mine[1] = lax.optimization_barrier((other[0], mine[1]))
        other[1] = swapped(mine[1], bit)
        if bit == bits[-1]:
            break
        size = room((1 << (known | bit).bit_count()) / peers)
        for stage in range(STAGES):
            (mine[stage],) = merged(blocks, per_device, known, bit, mine[stage], other[stage], size)
        known |= bit
    lists = [(m, o, swapped(m, 1), swapped(o, 1)) for m, o in zip(mine, other)]

    bands = (before, span_k, span_v)
    shared = (known, bits[-1], per_device, blocks, queries)
    state = attend_stage(*shared, lists[0], offsets=offsets, bands=bands)
    return lax.cond(
        fits(blocks, per_device, peers, bits),
        lambda: attend_stage(*shared, lists[1], state=state),
        lambda: general(queries, bands, cache_k, cache_v, blocks, offsets, bits),
    )


def solution(mesh):
    rows = P(("groups", "ctx"), None)
    heads = P("groups", None)
    return jax.shard_map(
        shards,
        mesh=mesh,
        in_specs=(rows, rows, rows, rows, rows, heads, heads),
        out_specs=rows,
        check_vma=False,
    )
```

```python
import functools
import math

import jax
import jax.numpy as jnp
from jax import lax
from jax.experimental import pallas as pl
from jax.experimental.pallas import tpu as pltpu
from jax.sharding import PartitionSpec as P

KVH = 4
GROUP = 8
HD = 128
QDEV = 128
VBLOCK = 64
NV = 16
NS = 64
SMAX = 128
ENTRIES = KVH * NV
FACTOR = math.log2(math.e) / math.sqrt(HD)
LOW = -1e38

ANY = pl.BlockSpec(memory_space=pl.ANY)
SMEM = pl.BlockSpec(memory_space=pltpu.SMEM)


def band_mask(offsets_ref, head, first):
    columns = lax.broadcasted_iota(jnp.int32, (8, SMAX + QDEV), 1)
    distance = SMAX - columns
    row = jnp.zeros((8, SMAX + QDEV), jnp.int32)
    for at in range(NS):
        row = jnp.where(distance == offsets_ref[head, at], 1, row)
    rows = jnp.concatenate([row] * (QDEV // 8), axis=0)
    rolled = pltpu.roll(rows, 0, 1, stride=1, stride_axis=0)
    keys = lax.broadcasted_iota(jnp.int32, (QDEV, SMAX + QDEV), 1)
    return (rolled > 0) & (keys >= jnp.where(first, SMAX, 0))


def attend_rows(rows, keys, values_ones, mask):
    scores = lax.dot_general(
        rows, keys, (((1,), (1,)), ((), ())), preferred_element_type=jnp.float32
    )
    if mask is not None:
        wide = scores.shape[1] - mask.shape[1]
        reps = rows.shape[0] // QDEV
        tiled = jnp.concatenate([mask] * reps, axis=0)
        band = jnp.where(tiled, scores[:, wide:], LOW)
        scores = jnp.concatenate([scores[:, :wide], band], axis=1)
    largest = jnp.max(scores, axis=1, keepdims=True) * FACTOR
    weights = jnp.exp2(scores * FACTOR - largest).astype(jnp.bfloat16)
    mixed = jnp.dot(weights, values_ones, preferred_element_type=jnp.float32)
    return largest, mixed


def dense_kernel(
    offsets, queries, keys, values, before_k, own_k, before_v, own_v, out, kbuf, vbuf
):
    head = pl.program_id(0)
    first = lax.axis_index("ctx") == 0
    wide = NV * VBLOCK
    kbuf[:wide] = keys[0]
    kbuf[wide : wide + SMAX] = before_k[...]
    kbuf[wide + SMAX :] = own_k[...]
    vbuf[:wide, :HD] = values[0]
    vbuf[wide : wide + SMAX, :HD] = before_v[...]
    vbuf[wide + SMAX :, :HD] = own_v[...]
    vbuf[:, HD:] = jnp.ones((wide + SMAX + QDEV, HD), jnp.bfloat16)
    mask = band_mask(offsets, head, first)
    for at in range(0, GROUP, 2):
        rows = jnp.concatenate(
            [queries[:, (at + i) * HD : (at + i + 1) * HD] for i in range(2)], axis=0
        )
        _, mixed = attend_rows(rows, kbuf[...], vbuf[...], mask)
        result = (mixed[:, :HD] / mixed[:, HD:]).astype(jnp.bfloat16)
        for i in range(2):
            out[:, (at + i) * HD : (at + i + 1) * HD] = result[i * QDEV : (i + 1) * QDEV]


def head_block(rows):
    return pl.BlockSpec((rows, HD), lambda head: (0, head))


def attend_dense(offsets, queries, keys, values, bands):
    wide = NV * VBLOCK
    return pl.pallas_call(
        dense_kernel,
        grid=(KVH,),
        out_shape=jax.ShapeDtypeStruct(queries.shape, jnp.bfloat16),
        in_specs=[
            SMEM,
            pl.BlockSpec((QDEV, GROUP * HD), lambda head: (0, head)),
            pl.BlockSpec((1, wide, HD), lambda head: (head, 0, 0)),
            pl.BlockSpec((1, wide, HD), lambda head: (head, 0, 0)),
        ]
        + [head_block(QDEV)] * 4,
        out_specs=pl.BlockSpec((QDEV, GROUP * HD), lambda head: (0, head)),
        scratch_shapes=[
            pltpu.VMEM((wide + SMAX + QDEV, HD), jnp.bfloat16),
            pltpu.VMEM((wide + SMAX + QDEV, 2 * HD), jnp.bfloat16),
        ],
        compiler_params=pltpu.CompilerParams(vmem_limit_bytes=48 * 2**20),
        name="attend_dense",
    )(offsets, queries, keys, values, *bands)


def owned_kernel(per_device, blocks, cache_k, cache_v, out_k, out_v, sems):
    me = lax.axis_index("ctx")
    out_k[...] = jnp.zeros_like(out_k)
    out_v[...] = jnp.zeros_like(out_v)

    def copies(entry):
        head, at = entry // NV, entry % NV
        block = blocks[head, at]
        local = block % per_device
        rows = pl.ds(pl.multiple_of(local * VBLOCK, VBLOCK), VBLOCK)
        columns = pl.ds(pl.multiple_of(head * HD, HD), HD)
        pairs = ((cache_k, out_k, 0), (cache_v, out_v, 1))
        return block // per_device == me, [
            pltpu.make_async_copy(source.at[rows, columns], target.at[entry], sems.at[entry, i])
            for source, target, i in pairs
        ]

    def start(entry, carry):
        mine, both = copies(entry)

        @pl.when(mine)
        def _():
            for copy in both:
                copy.start()

        return carry

    def wait(entry, carry):
        mine, both = copies(entry)

        @pl.when(mine)
        def _():
            for copy in both:
                copy.wait()

        return carry

    lax.fori_loop(0, ENTRIES, start, 0)
    lax.fori_loop(0, ENTRIES, wait, 0)


def owned_blocks(blocks, cache_k, cache_v):
    shape = jax.ShapeDtypeStruct((ENTRIES, VBLOCK, HD), jnp.bfloat16)
    whole = pl.BlockSpec(memory_space=pltpu.VMEM)
    return pl.pallas_call(
        functools.partial(owned_kernel, cache_k.shape[0] // VBLOCK),
        out_shape=(shape, shape),
        in_specs=[SMEM, ANY, ANY],
        out_specs=(whole, whole),
        scratch_shapes=[pltpu.SemaphoreType.DMA((ENTRIES, 2))],
        compiler_params=pltpu.CompilerParams(vmem_limit_bytes=16 * 2**20),
        name="owned_blocks",
    )(blocks, cache_k, cache_v)


STAGES = 2
TILE = 2
OUT_SPACE = pltpu.HBM
ROWS = VBLOCK // STAGES
WHOLE = pl.BlockSpec(memory_space=pltpu.VMEM)


def room(share):
    mean = ENTRIES * share
    wide = mean + 3.0 * math.sqrt(mean * (1.0 - share)) + 1.5
    return min(ENTRIES + 1, math.ceil(wide))


def owner_of(block, per_device):
    if per_device & (per_device - 1) == 0:
        return lax.shift_right_logical(block, per_device.bit_length() - 1)
    return lax.div(block, per_device)


def pack_kernel(per_device, limit, blocks, cache_k, cache_v, kept, sent, sems):
    me = lax.axis_index("ctx")
    even = lax.rem(me, 2) == 0
    count = jnp.int32(0)
    for entry in range(ENTRIES):
        head = entry // NV
        block = blocks[head, entry % NV]
        owner = owner_of(block, per_device)
        mine = owner == me
        local = block - owner * per_device

        def start(pair, head=head, local=local, count=count):
            rows = pl.ds(pl.multiple_of(local * VBLOCK, VBLOCK), VBLOCK)
            for i, target in enumerate((kept, sent)):
                source = pair[i].at[rows, pl.ds(head * HD, HD)]
                pltpu.make_async_copy(source, target.at[count], sems.at[count, i]).start()

        @pl.when(mine & (count < limit))
        def _(start=start):
            @pl.when(even)
            def _():
                start((cache_k, cache_v))

            @pl.when(jnp.logical_not(even))
            def _():
                start((cache_v, cache_k))

        count += mine.astype(jnp.int32)

    for at in range(limit):

        @pl.when(at < count)
        def _(at=at):
            for i, target in enumerate((kept, sent)):
                source = cache_k.at[pl.ds(0, VBLOCK), pl.ds(0, HD)]
                pltpu.make_async_copy(source, target.at[at], sems.at[at, i]).wait()


def pack(blocks, cache_k, cache_v, limit):
    shape = jax.ShapeDtypeStruct((limit, VBLOCK, HD), jnp.bfloat16)
    return pl.pallas_call(
        functools.partial(pack_kernel, cache_k.shape[0] // VBLOCK, limit),
        out_shape=(shape, shape),
        in_specs=[SMEM, ANY, ANY],
        out_specs=(WHOLE, WHOLE),
        scratch_shapes=[pltpu.SemaphoreType.DMA((limit, 2))],
        compiler_params=pltpu.CompilerParams(vmem_limit_bytes=16 * 2**20),
        name="pack",
    )(blocks, cache_k, cache_v)


def walk(blocks, per_device, known, bit, limits, act):
    me = lax.axis_index("ctx")
    at_mine = at_other = jnp.int32(0)
    for entry in range(ENTRIES):
        away = (owner_of(blocks[entry // NV, entry % NV], per_device) ^ me) & ~known
        mine, other = away == 0, away == bit
        tops = jnp.minimum(at_mine, limits[0] - 1), jnp.minimum(at_other, limits[1] - 1)
        act(entry, *tops, at_mine + at_other, other)
        at_mine += mine.astype(jnp.int32)
        at_other += other.astype(jnp.int32)


def merge_kernel(per_device, known, bit, blocks, mine, other, *outs):
    size = outs[0].shape[0]

    def act(entry, at_mine, at_other, place, theirs):
        tile = jnp.where(theirs, other[at_other], mine[at_mine])
        place = jnp.minimum(place, size - 1)
        for stage, out in enumerate(outs):
            out[place] = tile[stage * ROWS : (stage + 1) * ROWS]

    walk(blocks, per_device, known, bit, (mine.shape[0], other.shape[0]), act)


def merged(blocks, per_device, known, bit, mine, other, size):
    count = mine.shape[1] // ROWS
    shape = jax.ShapeDtypeStruct((size, ROWS, HD), jnp.bfloat16)
    return pl.pallas_call(
        functools.partial(merge_kernel, per_device, known, bit),
        out_shape=(shape,) * count,
        in_specs=[SMEM, WHOLE, WHOLE],
        out_specs=(WHOLE,) * count,
        compiler_params=pltpu.CompilerParams(vmem_limit_bytes=16 * 2**20),
        name="merge",
    )(blocks, mine, other)


def stage_kernel(per_device, known, bit, banded, last, *refs):
    refs = list(refs)
    blocks = refs.pop(0)
    offsets = refs.pop(0) if banded else None
    queries, mine, other, mine_twin, other_twin = refs[:5]
    refs = refs[5:]
    if banded:
        before, own_k, own_v = refs[:3]
        refs = refs[3:]
    else:
        largest_in, total_in, mixed_in = refs[:3]
        refs = refs[3:]
    if last:
        out, kbuf, vbuf, held, sems = refs
    else:
        largest_out, total_out, mixed_out, kbuf, vbuf = refs
    me = lax.axis_index("ctx")
    even = lax.rem(me, 2) == 0
    wide = NV * ROWS

    def act(entry, at_mine, at_other, place, theirs):
        tile = jnp.where(theirs, other[at_other], mine[at_mine])
        twin = jnp.where(theirs, other_twin[at_other], mine_twin[at_mine])
        rows = pl.ds(entry % NV * ROWS, ROWS)
        kbuf[entry // NV, rows] = jnp.where(even, tile, twin)
        vbuf[entry // NV, rows, :HD] = jnp.where(even, twin, tile)

    walk(blocks, per_device, known, bit, (mine.shape[0], other.shape[0]), act)
    copies = []
    for head in range(KVH):
        columns = slice(head * HD, (head + 1) * HD)
        vbuf[head, :, HD:] = jnp.ones((vbuf.shape[1], HD), jnp.bfloat16)
        mask = None
        if banded:
            values = slice((KVH + head) * HD, (KVH + head + 1) * HD)
            kbuf[head, wide : wide + SMAX] = before[:, columns]
            kbuf[head, wide + SMAX :] = own_k[:, columns]
            vbuf[head, wide : wide + SMAX, :HD] = before[:, values]
            vbuf[head, wide + SMAX :, :HD] = own_v[:, columns]
            mask = band_mask(offsets, head, me == 0)
        for at in range(0, GROUP, TILE):
            rows = jnp.concatenate(
                [
                    queries[:, (head * GROUP + at + i) * HD : (head * GROUP + at + i + 1) * HD]
                    for i in range(TILE)
                ],
                axis=0,
            )
            start = (head * GROUP + at) * QDEV
            tile = slice(start, start + TILE * QDEV)
            largest, mixed = attend_rows(rows, kbuf[head], vbuf[head], mask)
            mixed, total = mixed[:, :HD], mixed[:, HD:]
            largest = jnp.broadcast_to(largest, mixed.shape)
            if not banded:
                above = jnp.maximum(largest_in[tile], largest)
                now, then = jnp.exp2(largest - above), jnp.exp2(largest_in[tile] - above)
                mixed = mixed * now + mixed_in[tile] * then
                total = total * now + total_in[tile] * then
                largest = above
            if last:
                result = (mixed / total).astype(jnp.bfloat16)
                for i in range(TILE):
                    held[head, :, (at + i) * HD : (at + i + 1) * HD] = result[
                        i * QDEV : (i + 1) * QDEV
                    ]
            else:
                largest_out[tile], total_out[tile], mixed_out[tile] = largest, total, mixed
        if last:
            span = pl.ds(head * GROUP * HD, GROUP * HD)
            copies.append(pltpu.make_async_copy(held.at[head], out.at[:, span], sems.at[head]))
            copies[-1].start()
    for copy in copies:
        copy.wait()


def attend_stage(known, bit, per_device, blocks, queries, lists, offsets=None, bands=None, state=None):
    banded, last = bands is not None, state is not None
    tall = KVH * GROUP * QDEV
    args = [blocks] + [offsets] * banded + [queries, *lists]
    args += list(bands if banded else state)
    specs = [SMEM] * (1 + banded) + [WHOLE] * (len(args) - 1 - banded)
    keys = NV * ROWS + (SMAX + QDEV) * banded
    scratch = [
        pltpu.VMEM((KVH, keys, HD), jnp.bfloat16),
        pltpu.VMEM((KVH, keys, 2 * HD), jnp.bfloat16),
    ]
    if last:
        out_shape = jax.ShapeDtypeStruct(queries.shape, jnp.bfloat16)
        out_specs = pl.BlockSpec(memory_space=OUT_SPACE)
        scratch += [
            pltpu.VMEM((KVH, QDEV, GROUP * HD), jnp.bfloat16),
            pltpu.SemaphoreType.DMA((KVH,)),
        ]
    else:
        out_shape = (jax.ShapeDtypeStruct((tall, HD), jnp.float32),) * 3
        out_specs = (WHOLE,) * 3
    return pl.pallas_call(
        functools.partial(stage_kernel, per_device, known, bit, banded, last),
        out_shape=out_shape,
        in_specs=specs,
        out_specs=out_specs,
        scratch_shapes=scratch,
        compiler_params=pltpu.CompilerParams(vmem_limit_bytes=48 * 2**20),
        cost_estimate=pl.CostEstimate(
            flops=4 * tall * keys * HD,
            bytes_accessed=8 * 2**20,
            transcendentals=tall * keys,
        ),
        name="attend_last" if last else "attend_first",
    )(*args)


def permuted(array, pairs):
    return lax.ppermute(array, "ctx", pairs)


def swapped(array, bit):
    return permuted(array, [(i, i ^ bit) for i in range(lax.axis_size("ctx"))])


def fits(blocks, per_device, peers, bits):
    masks = [sum(bits[:at]) for at in range(len(bits))]
    most = [room((1 << at) / peers) - (at > 0) for at in range(len(bits))]
    owners = (blocks // per_device).reshape(1, 1, ENTRIES)
    ids = jnp.arange(peers, dtype=jnp.int32)[None, :, None]
    away = (owners ^ ids) & ~jnp.array(masks, jnp.int32)[:, None, None]
    counts = jnp.sum((away == 0).astype(jnp.int32), axis=2)
    return jnp.all(counts <= jnp.array(most, jnp.int32)[:, None])


def general(queries, bands, cache_k, cache_v, blocks, offsets, bits):
    keys, values = owned_blocks(blocks, cache_k, cache_v)
    for bit in bits:
        keys, values = keys + swapped(keys, bit), values + swapped(values, bit)
    keys = keys.reshape(KVH, NV * VBLOCK, HD)
    values = values.reshape(KVH, NV * VBLOCK, HD)
    before, own_k, own_v = bands
    wide = KVH * HD
    bands = (before[:, :wide], own_k, before[:, wide:], own_v)
    return attend_dense(offsets, queries, keys, values, bands)


def shards(queries, span_k, span_v, cache_k, cache_v, blocks, offsets):
    peers = lax.axis_size("ctx")
    per_device = cache_k.shape[0] // VBLOCK
    ahead = [(i, i + 1) for i in range(peers - 1)]
    bits = [1] + [1 << at for at in range(peers.bit_length() - 2, 0, -1)]

    kept, sent = pack(blocks, cache_k, cache_v, room(1 / peers))
    mine = list(merged(blocks, per_device, 0, 1, kept, swapped(sent, 1), room(2 / peers)))
    before = permuted(jnp.concatenate([span_k, span_v], axis=1), ahead)
    other = [None] * STAGES
    known = 1
    for bit in bits[1:]:
        other[0] = swapped(mine[0], bit)
        if bit == bits[1]:
            other[0], before = lax.optimization_barrier((other[0], before))
        other[1] = swapped(mine[1], bit)
        if bit == bits[-1]:
            break
        size = room((1 << (known | bit).bit_count()) / peers)
        for stage in range(STAGES):
            (mine[stage],) = merged(blocks, per_device, known, bit, mine[stage], other[stage], size)
        known |= bit
    twins = [swapped(m, 1) for m in mine]

    bands = (before, span_k, span_v)
    shared = (known, bits[-1], per_device, blocks, queries)
    lists = (mine[0], other[0], twins[0], swapped(other[0], 1))
    state = attend_stage(*shared, lists, offsets=offsets, bands=bands)
    state, late = lax.optimization_barrier((state, other[1]))
    lists = (mine[1], late, twins[1], swapped(late, 1))
    return lax.cond(
        fits(blocks, per_device, peers, bits),
        lambda: attend_stage(*shared, lists, state=state),
        lambda: general(queries, bands, cache_k, cache_v, blocks, offsets, bits),
    )


def solution(mesh):
    rows = P(("groups", "ctx"), None)
    heads = P("groups", None)
    return jax.shard_map(
        shards,
        mesh=mesh,
        in_specs=(rows, rows, rows, rows, rows, heads, heads),
        out_specs=rows,
        check_vma=False,
    )
```

```python
import functools
import math

import jax
import jax.numpy as jnp
from jax import lax
from jax.experimental import pallas as pl
from jax.experimental.pallas import tpu as pltpu
from jax.sharding import PartitionSpec as P

KVH = 4
GROUP = 8
HD = 128
QDEV = 128
VBLOCK = 64
NV = 16
NS = 64
SMAX = 128
ENTRIES = KVH * NV
FACTOR = math.log2(math.e) / math.sqrt(HD)
LOW = -1e38

ANY = pl.BlockSpec(memory_space=pl.ANY)
SMEM = pl.BlockSpec(memory_space=pltpu.SMEM)


def band_mask(offsets_ref, head, first):
    columns = lax.broadcasted_iota(jnp.int32, (8, SMAX + QDEV), 1)
    distance = SMAX - columns
    row = jnp.zeros((8, SMAX + QDEV), jnp.int32)
    for at in range(NS):
        row = jnp.where(distance == offsets_ref[head, at], 1, row)
    rows = jnp.concatenate([row] * (QDEV // 8), axis=0)
    rolled = pltpu.roll(rows, 0, 1, stride=1, stride_axis=0)
    keys = lax.broadcasted_iota(jnp.int32, (QDEV, SMAX + QDEV), 1)
    return (rolled > 0) & (keys >= jnp.where(first, SMAX, 0))


def attend_rows(rows, keys, values_ones, mask):
    scores = lax.dot_general(
        rows, keys, (((1,), (1,)), ((), ())), preferred_element_type=jnp.float32
    )
    if mask is not None:
        wide = scores.shape[1] - mask.shape[1]
        reps = rows.shape[0] // QDEV
        tiled = jnp.concatenate([mask] * reps, axis=0)
        band = jnp.where(tiled, scores[:, wide:], LOW)
        scores = jnp.concatenate([scores[:, :wide], band], axis=1)
    largest = jnp.max(scores, axis=1, keepdims=True) * FACTOR
    weights = jnp.exp2(scores * FACTOR - largest).astype(jnp.bfloat16)
    mixed = jnp.dot(weights, values_ones, preferred_element_type=jnp.float32)
    return largest, mixed


def dense_kernel(
    offsets, queries, keys, values, before_k, own_k, before_v, own_v, out, kbuf, vbuf
):
    head = pl.program_id(0)
    first = lax.axis_index("ctx") == 0
    wide = NV * VBLOCK
    kbuf[:wide] = keys[0]
    kbuf[wide : wide + SMAX] = before_k[...]
    kbuf[wide + SMAX :] = own_k[...]
    vbuf[:wide, :HD] = values[0]
    vbuf[wide : wide + SMAX, :HD] = before_v[...]
    vbuf[wide + SMAX :, :HD] = own_v[...]
    vbuf[:, HD:] = jnp.ones((wide + SMAX + QDEV, HD), jnp.bfloat16)
    mask = band_mask(offsets, head, first)
    for at in range(0, GROUP, 2):
        rows = jnp.concatenate(
            [queries[:, (at + i) * HD : (at + i + 1) * HD] for i in range(2)], axis=0
        )
        _, mixed = attend_rows(rows, kbuf[...], vbuf[...], mask)
        result = (mixed[:, :HD] / mixed[:, HD:]).astype(jnp.bfloat16)
        for i in range(2):
            out[:, (at + i) * HD : (at + i + 1) * HD] = result[i * QDEV : (i + 1) * QDEV]


def head_block(rows):
    return pl.BlockSpec((rows, HD), lambda head: (0, head))


def attend_dense(offsets, queries, keys, values, bands):
    wide = NV * VBLOCK
    return pl.pallas_call(
        dense_kernel,
        grid=(KVH,),
        out_shape=jax.ShapeDtypeStruct(queries.shape, jnp.bfloat16),
        in_specs=[
            SMEM,
            pl.BlockSpec((QDEV, GROUP * HD), lambda head: (0, head)),
            pl.BlockSpec((1, wide, HD), lambda head: (head, 0, 0)),
            pl.BlockSpec((1, wide, HD), lambda head: (head, 0, 0)),
        ]
        + [head_block(QDEV)] * 4,
        out_specs=pl.BlockSpec((QDEV, GROUP * HD), lambda head: (0, head)),
        scratch_shapes=[
            pltpu.VMEM((wide + SMAX + QDEV, HD), jnp.bfloat16),
            pltpu.VMEM((wide + SMAX + QDEV, 2 * HD), jnp.bfloat16),
        ],
        compiler_params=pltpu.CompilerParams(vmem_limit_bytes=48 * 2**20),
        name="attend_dense",
    )(offsets, queries, keys, values, *bands)


def owned_kernel(per_device, blocks, cache_k, cache_v, out_k, out_v, sems):
    me = lax.axis_index("ctx")
    out_k[...] = jnp.zeros_like(out_k)
    out_v[...] = jnp.zeros_like(out_v)

    def copies(entry):
        head, at = entry // NV, entry % NV
        block = blocks[head, at]
        local = block % per_device
        rows = pl.ds(pl.multiple_of(local * VBLOCK, VBLOCK), VBLOCK)
        columns = pl.ds(pl.multiple_of(head * HD, HD), HD)
        pairs = ((cache_k, out_k, 0), (cache_v, out_v, 1))
        return block // per_device == me, [
            pltpu.make_async_copy(source.at[rows, columns], target.at[entry], sems.at[entry, i])
            for source, target, i in pairs
        ]

    def start(entry, carry):
        mine, both = copies(entry)

        @pl.when(mine)
        def _():
            for copy in both:
                copy.start()

        return carry

    def wait(entry, carry):
        mine, both = copies(entry)

        @pl.when(mine)
        def _():
            for copy in both:
                copy.wait()

        return carry

    lax.fori_loop(0, ENTRIES, start, 0)
    lax.fori_loop(0, ENTRIES, wait, 0)


def owned_blocks(blocks, cache_k, cache_v):
    shape = jax.ShapeDtypeStruct((ENTRIES, VBLOCK, HD), jnp.bfloat16)
    whole = pl.BlockSpec(memory_space=pltpu.VMEM)
    return pl.pallas_call(
        functools.partial(owned_kernel, cache_k.shape[0] // VBLOCK),
        out_shape=(shape, shape),
        in_specs=[SMEM, ANY, ANY],
        out_specs=(whole, whole),
        scratch_shapes=[pltpu.SemaphoreType.DMA((ENTRIES, 2))],
        compiler_params=pltpu.CompilerParams(vmem_limit_bytes=16 * 2**20),
        name="owned_blocks",
    )(blocks, cache_k, cache_v)


STAGES = 2
TILE = 2
OUT_SPACE = pltpu.HBM
VMEM = 24
COST = 2**20
ROWS = VBLOCK // STAGES
WHOLE = pl.BlockSpec(memory_space=pltpu.VMEM)


def room(share):
    mean = ENTRIES * share
    wide = mean + 3.0 * math.sqrt(mean * (1.0 - share)) + 1.5
    return min(ENTRIES + 1, math.ceil(wide))


def owner_of(block, per_device):
    if per_device & (per_device - 1) == 0:
        return lax.shift_right_logical(block, per_device.bit_length() - 1)
    return lax.div(block, per_device)


def pack_kernel(per_device, limit, blocks, cache_k, cache_v, kept, sent, sems):
    me = lax.axis_index("ctx")
    even = lax.rem(me, 2) == 0
    count = jnp.int32(0)
    for entry in range(ENTRIES):
        head = entry // NV
        block = blocks[head, entry % NV]
        owner = owner_of(block, per_device)
        mine = owner == me
        local = block - owner * per_device

        def start(pair, head=head, local=local, count=count):
            rows = pl.ds(pl.multiple_of(local * VBLOCK, VBLOCK), VBLOCK)
            for i, target in enumerate((kept, sent)):
                source = pair[i].at[rows, pl.ds(head * HD, HD)]
                pltpu.make_async_copy(source, target.at[count], sems.at[count, i]).start()

        @pl.when(mine & (count < limit))
        def _(start=start):
            @pl.when(even)
            def _():
                start((cache_k, cache_v))

            @pl.when(jnp.logical_not(even))
            def _():
                start((cache_v, cache_k))

        count += mine.astype(jnp.int32)

    for at in range(limit):

        @pl.when(at < count)
        def _(at=at):
            for i, target in enumerate((kept, sent)):
                source = cache_k.at[pl.ds(0, VBLOCK), pl.ds(0, HD)]
                pltpu.make_async_copy(source, target.at[at], sems.at[at, i]).wait()


def pack(blocks, cache_k, cache_v, limit):
    shape = jax.ShapeDtypeStruct((limit, VBLOCK, HD), jnp.bfloat16)
    return pl.pallas_call(
        functools.partial(pack_kernel, cache_k.shape[0] // VBLOCK, limit),
        out_shape=(shape, shape),
        in_specs=[SMEM, ANY, ANY],
        out_specs=(WHOLE, WHOLE),
        scratch_shapes=[pltpu.SemaphoreType.DMA((limit, 2))],
        compiler_params=pltpu.CompilerParams(vmem_limit_bytes=16 * 2**20),
        name="pack",
    )(blocks, cache_k, cache_v)


def walk(blocks, per_device, known, bit, limits, act):
    me = lax.axis_index("ctx")
    at_mine = at_other = jnp.int32(0)
    for entry in range(ENTRIES):
        away = (owner_of(blocks[entry // NV, entry % NV], per_device) ^ me) & ~known
        mine, other = away == 0, away == bit
        tops = jnp.minimum(at_mine, limits[0] - 1), jnp.minimum(at_other, limits[1] - 1)
        act(entry, *tops, at_mine + at_other, other)
        at_mine += mine.astype(jnp.int32)
        at_other += other.astype(jnp.int32)


def merge_kernel(per_device, known, bit, count, blocks, *refs):
    mine, other, outs = refs[:count], refs[count : 2 * count], refs[2 * count :]
    size = outs[0].shape[0]

    def act(entry, at_mine, at_other, place, theirs):
        tiles = [jnp.where(theirs, o[at_other], m[at_mine]) for m, o in zip(mine, other)]
        tile = jnp.concatenate(tiles, axis=0)
        place = jnp.minimum(place, size - 1)
        for at, out in enumerate(outs):
            rows = out.shape[1]
            out[place] = tile[at * rows : (at + 1) * rows]

    walk(blocks, per_device, known, bit, (mine[0].shape[0], other[0].shape[0]), act)


def merged(blocks, per_device, known, bit, mine, other, size):
    count = sum(m.shape[1] for m in mine) // ROWS
    shape = jax.ShapeDtypeStruct((size, ROWS, HD), jnp.bfloat16)
    return pl.pallas_call(
        functools.partial(merge_kernel, per_device, known, bit, len(mine)),
        out_shape=(shape,) * count,
        in_specs=[SMEM] + [WHOLE] * (2 * len(mine)),
        out_specs=(WHOLE,) * count,
        compiler_params=pltpu.CompilerParams(vmem_limit_bytes=16 * 2**20),
        name="merge",
    )(blocks, *mine, *other)


def stage_kernel(per_device, known, bit, banded, last, *refs):
    refs = list(refs)
    blocks = refs.pop(0)
    offsets = refs.pop(0) if banded else None
    queries, mine, other, mine_twin, other_twin = refs[:5]
    refs = refs[5:]
    if banded:
        before, own_k, own_v = refs[:3]
        refs = refs[3:]
    else:
        marks_in, mixed_in = refs[:2]
        refs = refs[2:]
    if last:
        out, kbuf, vbuf, held, sems = refs
    else:
        marks_out, mixed_out, kbuf, vbuf = refs
    me = lax.axis_index("ctx")
    even = lax.rem(me, 2) == 0
    wide = NV * ROWS

    def act(entry, at_mine, at_other, place, theirs):
        tile = jnp.where(theirs, other[at_other], mine[at_mine])
        twin = jnp.where(theirs, other_twin[at_other], mine_twin[at_mine])
        rows = pl.ds(entry % NV * ROWS, ROWS)
        kbuf[entry // NV, rows] = jnp.where(even, tile, twin)
        vbuf[entry // NV, rows, :HD] = jnp.where(even, twin, tile)

    walk(blocks, per_device, known, bit, (mine.shape[0], other.shape[0]), act)
    copies = []
    for head in range(KVH):
        columns = slice(head * HD, (head + 1) * HD)
        vbuf[head, :, HD:] = jnp.ones((vbuf.shape[1], HD), jnp.bfloat16)
        mask = None
        if banded:
            values = slice((KVH + head) * HD, (KVH + head + 1) * HD)
            kbuf[head, wide : wide + SMAX] = before[:, columns]
            kbuf[head, wide + SMAX :] = own_k[:, columns]
            vbuf[head, wide : wide + SMAX, :HD] = before[:, values]
            vbuf[head, wide + SMAX :, :HD] = own_v[:, columns]
            mask = band_mask(offsets, head, me == 0)
        for at in range(0, GROUP, TILE):
            rows = jnp.concatenate(
                [
                    queries[:, (head * GROUP + at + i) * HD : (head * GROUP + at + i + 1) * HD]
                    for i in range(TILE)
                ],
                axis=0,
            )
            start = (head * GROUP + at) * QDEV
            tile = slice(start, start + TILE * QDEV)
            largest, mixed = attend_rows(rows, kbuf[head], vbuf[head], mask)
            mixed, total = mixed[:, :HD], mixed[:, HD:]
            if not banded:
                before_largest = marks_in[tile, :1]
                above = jnp.maximum(before_largest, largest)
                now, then = jnp.exp2(largest - above), jnp.exp2(before_largest - above)
                mixed = mixed * now + mixed_in[tile] * then
                total = total * now + marks_in[tile, HD - 1 :] * then
            if last:
                result = (mixed / total).astype(jnp.bfloat16)
                for i in range(TILE):
                    held[head, :, (at + i) * HD : (at + i + 1) * HD] = result[
                        i * QDEV : (i + 1) * QDEV
                    ]
            else:
                lanes = lax.broadcasted_iota(jnp.int32, mixed.shape, 1)
                marks_out[tile] = jnp.where(lanes < HD // 2, largest, total)
                mixed_out[tile] = mixed
        if last:
            span = pl.ds(head * GROUP * HD, GROUP * HD)
            copies.append(pltpu.make_async_copy(held.at[head], out.at[:, span], sems.at[head]))
            copies[-1].start()
    for copy in copies:
        copy.wait()


def attend_stage(known, bit, per_device, blocks, queries, lists, offsets=None, bands=None, state=None):
    banded, last = bands is not None, state is not None
    tall = KVH * GROUP * QDEV
    args = [blocks] + [offsets] * banded + [queries, *lists]
    args += list(bands if banded else state)
    specs = [SMEM] * (1 + banded) + [WHOLE] * (len(args) - 1 - banded)
    keys = NV * ROWS + (SMAX + QDEV) * banded
    scratch = [
        pltpu.VMEM((KVH, keys, HD), jnp.bfloat16),
        pltpu.VMEM((KVH, keys, 2 * HD), jnp.bfloat16),
    ]
    if last:
        out_shape = jax.ShapeDtypeStruct(queries.shape, jnp.bfloat16)
        out_specs = pl.BlockSpec(memory_space=OUT_SPACE)
        scratch += [
            pltpu.VMEM((KVH, QDEV, GROUP * HD), jnp.bfloat16),
            pltpu.SemaphoreType.DMA((KVH,)),
        ]
    else:
        out_shape = (jax.ShapeDtypeStruct((tall, HD), jnp.float32),) * 2
        out_specs = (WHOLE,) * 2
    return pl.pallas_call(
        functools.partial(stage_kernel, per_device, known, bit, banded, last),
        out_shape=out_shape,
        in_specs=specs,
        out_specs=out_specs,
        scratch_shapes=scratch,
        compiler_params=pltpu.CompilerParams(vmem_limit_bytes=VMEM * 2**20),
        cost_estimate=pl.CostEstimate(flops=COST, bytes_accessed=COST, transcendentals=0),
        name="attend_last" if last else "attend_first",
    )(*args)


def permuted(array, pairs):
    return lax.ppermute(array, "ctx", pairs)


def swapped(array, bit):
    return permuted(array, [(i, i ^ bit) for i in range(lax.axis_size("ctx"))])


def fits(blocks, per_device, peers, bits):
    masks = [sum(bits[:at]) for at in range(len(bits))]
    most = [room((1 << at) / peers) - (at > 0) for at in range(len(bits))]
    owners = (blocks // per_device).reshape(1, 1, ENTRIES)
    ids = jnp.arange(peers, dtype=jnp.int32)[None, :, None]
    away = (owners ^ ids) & ~jnp.array(masks, jnp.int32)[:, None, None]
    counts = jnp.sum((away == 0).astype(jnp.int32), axis=2)
    return jnp.all(counts <= jnp.array(most, jnp.int32)[:, None])


def general(queries, bands, cache_k, cache_v, blocks, offsets, bits):
    keys, values = owned_blocks(blocks, cache_k, cache_v)
    for bit in bits:
        keys, values = keys + swapped(keys, bit), values + swapped(values, bit)
    keys = keys.reshape(KVH, NV * VBLOCK, HD)
    values = values.reshape(KVH, NV * VBLOCK, HD)
    before, own_k, own_v = bands
    wide = KVH * HD
    bands = (before[:, :wide], own_k, before[:, wide:], own_v)
    return attend_dense(offsets, queries, keys, values, bands)


def shards(queries, span_k, span_v, cache_k, cache_v, blocks, offsets):
    peers = lax.axis_size("ctx")
    per_device = cache_k.shape[0] // VBLOCK
    ahead = [(i, i + 1) for i in range(peers - 1)]
    bits = [1] + [1 << at for at in range(peers.bit_length() - 2, 0, -1)]

    kept, sent = pack(blocks, cache_k, cache_v, room(1 / peers))
    mine = merged(blocks, per_device, 0, 1, [kept], [swapped(sent, 1)], room(2 / peers))
    before = permuted(jnp.concatenate([span_k, span_v], axis=1), ahead)
    short = jnp.logical_not(fits(blocks, per_device, peers, bits)).astype(jnp.int32)
    other = [None] * STAGES
    known = 1
    for bit in bits[1:]:
        other = [swapped(m, bit) for m in mine]
        if bit == bits[1]:
            other[0], before, short = lax.optimization_barrier((other[0], before, short))
        if bit == bits[-1]:
            break
        size = room((1 << (known | bit).bit_count()) / peers)
        level = (blocks, per_device, known, bit)
        if bit == bits[1]:
            mine = merged(*level, mine, other, size)
        else:
            pairs = zip(mine, other)
            mine = [merged(*level, [m], [o], size)[0] for m, o in pairs]
        known |= bit
    twins = [swapped(m, 1) for m in mine]

    bands = (before, span_k, span_v)
    shared = (known, bits[-1], per_device, blocks, queries)
    lists = (mine[0], other[0], twins[0], swapped(other[0], 1))
    state = attend_stage(*shared, lists, offsets=offsets, bands=bands)
    state, late = lax.optimization_barrier((state, other[1]))
    lists = (mine[1], late, twins[1], swapped(late, 1))
    fast = attend_stage(*shared, lists, state=state)

    def again(carry):
        return 0, general(queries, bands, cache_k, cache_v, blocks, offsets, bits)

    return lax.while_loop(lambda carry: carry[0] > 0, again, (short, fast))[1]


def solution(mesh):
    rows = P(("groups", "ctx"), None)
    heads = P("groups", None)
    return jax.shard_map(
        shards,
        mesh=mesh,
        in_specs=(rows, rows, rows, rows, rows, heads, heads),
        out_specs=rows,
        check_vma=False,
    )
```

```python
import functools
import math

import jax
import jax.numpy as jnp
from jax import lax
from jax.experimental import pallas as pl
from jax.experimental.pallas import tpu as pltpu
from jax.sharding import PartitionSpec as P

KVH = 4
GROUP = 8
HD = 128
QDEV = 128
VBLOCK = 64
NV = 16
NS = 64
SMAX = 128
ENTRIES = KVH * NV
FACTOR = math.log2(math.e) / math.sqrt(HD)
LOW = -1e38

ANY = pl.BlockSpec(memory_space=pl.ANY)
SMEM = pl.BlockSpec(memory_space=pltpu.SMEM)


def band_mask(offsets_ref, head, first):
    columns = lax.broadcasted_iota(jnp.int32, (8, SMAX + QDEV), 1)
    distance = SMAX - columns
    row = jnp.zeros((8, SMAX + QDEV), jnp.int32)
    for at in range(NS):
        row = jnp.where(distance == offsets_ref[head, at], 1, row)
    rows = jnp.concatenate([row] * (QDEV // 8), axis=0)
    rolled = pltpu.roll(rows, 0, 1, stride=1, stride_axis=0)
    keys = lax.broadcasted_iota(jnp.int32, (QDEV, SMAX + QDEV), 1)
    return (rolled > 0) & (keys >= jnp.where(first, SMAX, 0))


def attend_rows(rows, keys, values_ones, mask, floor=None):
    scores = lax.dot_general(
        rows, keys, (((1,), (1,)), ((), ())), preferred_element_type=jnp.float32
    )
    if mask is not None:
        wide = scores.shape[1] - mask.shape[1]
        reps = rows.shape[0] // QDEV
        tiled = jnp.concatenate([mask] * reps, axis=0)
        band = jnp.where(tiled, scores[:, wide:], LOW)
        scores = jnp.concatenate([scores[:, :wide], band], axis=1)
    largest = jnp.max(scores, axis=1, keepdims=True) * FACTOR
    if floor is not None:
        largest = jnp.maximum(largest, floor)
    weights = jnp.exp2(scores * FACTOR - largest).astype(jnp.bfloat16)
    mixed = jnp.dot(weights, values_ones, preferred_element_type=jnp.float32)
    return largest, mixed


def dense_kernel(
    offsets, queries, keys, values, before_k, own_k, before_v, own_v, out, kbuf, vbuf
):
    head = pl.program_id(0)
    first = lax.axis_index("ctx") == 0
    wide = NV * VBLOCK
    kbuf[:wide] = keys[0]
    kbuf[wide : wide + SMAX] = before_k[...]
    kbuf[wide + SMAX :] = own_k[...]
    vbuf[:wide, :HD] = values[0]
    vbuf[wide : wide + SMAX, :HD] = before_v[...]
    vbuf[wide + SMAX :, :HD] = own_v[...]
    vbuf[:, HD:] = jnp.ones((wide + SMAX + QDEV, HD), jnp.bfloat16)
    mask = band_mask(offsets, head, first)
    for at in range(0, GROUP, 2):
        rows = jnp.concatenate(
            [queries[:, (at + i) * HD : (at + i + 1) * HD] for i in range(2)], axis=0
        )
        _, mixed = attend_rows(rows, kbuf[...], vbuf[...], mask)
        result = (mixed[:, :HD] / mixed[:, HD:]).astype(jnp.bfloat16)
        for i in range(2):
            out[:, (at + i) * HD : (at + i + 1) * HD] = result[i * QDEV : (i + 1) * QDEV]


def head_block(rows):
    return pl.BlockSpec((rows, HD), lambda head: (0, head))


def attend_dense(offsets, queries, keys, values, bands):
    wide = NV * VBLOCK
    return pl.pallas_call(
        dense_kernel,
        grid=(KVH,),
        out_shape=jax.ShapeDtypeStruct(queries.shape, jnp.bfloat16),
        in_specs=[
            SMEM,
            pl.BlockSpec((QDEV, GROUP * HD), lambda head: (0, head)),
            pl.BlockSpec((1, wide, HD), lambda head: (head, 0, 0)),
            pl.BlockSpec((1, wide, HD), lambda head: (head, 0, 0)),
        ]
        + [head_block(QDEV)] * 4,
        out_specs=pl.BlockSpec((QDEV, GROUP * HD), lambda head: (0, head)),
        scratch_shapes=[
            pltpu.VMEM((wide + SMAX + QDEV, HD), jnp.bfloat16),
            pltpu.VMEM((wide + SMAX + QDEV, 2 * HD), jnp.bfloat16),
        ],
        compiler_params=pltpu.CompilerParams(vmem_limit_bytes=48 * 2**20),
        name="attend_dense",
    )(offsets, queries, keys, values, *bands)


def owned_kernel(per_device, blocks, cache_k, cache_v, out_k, out_v, sems):
    me = lax.axis_index("ctx")
    out_k[...] = jnp.zeros_like(out_k)
    out_v[...] = jnp.zeros_like(out_v)

    def copies(entry):
        head, at = entry // NV, entry % NV
        block = blocks[head, at]
        local = block % per_device
        rows = pl.ds(pl.multiple_of(local * VBLOCK, VBLOCK), VBLOCK)
        columns = pl.ds(pl.multiple_of(head * HD, HD), HD)
        pairs = ((cache_k, out_k, 0), (cache_v, out_v, 1))
        return block // per_device == me, [
            pltpu.make_async_copy(source.at[rows, columns], target.at[entry], sems.at[entry, i])
            for source, target, i in pairs
        ]

    def start(entry, carry):
        mine, both = copies(entry)

        @pl.when(mine)
        def _():
            for copy in both:
                copy.start()

        return carry

    def wait(entry, carry):
        mine, both = copies(entry)

        @pl.when(mine)
        def _():
            for copy in both:
                copy.wait()

        return carry

    lax.fori_loop(0, ENTRIES, start, 0)
    lax.fori_loop(0, ENTRIES, wait, 0)


def owned_blocks(blocks, cache_k, cache_v):
    shape = jax.ShapeDtypeStruct((ENTRIES, VBLOCK, HD), jnp.bfloat16)
    whole = pl.BlockSpec(memory_space=pltpu.VMEM)
    return pl.pallas_call(
        functools.partial(owned_kernel, cache_k.shape[0] // VBLOCK),
        out_shape=(shape, shape),
        in_specs=[SMEM, ANY, ANY],
        out_specs=(whole, whole),
        scratch_shapes=[pltpu.SemaphoreType.DMA((ENTRIES, 2))],
        compiler_params=pltpu.CompilerParams(vmem_limit_bytes=16 * 2**20),
        name="owned_blocks",
    )(blocks, cache_k, cache_v)


STAGES = 2
TILE = 2
OUT_SPACE = pltpu.HBM
VMEM = 24
COST = 2**20
ROWS = VBLOCK // STAGES
WHOLE = pl.BlockSpec(memory_space=pltpu.VMEM)


def room(share):
    mean = ENTRIES * share
    wide = mean + 3.0 * math.sqrt(mean * (1.0 - share)) + 1.5
    return min(ENTRIES + 1, math.ceil(wide))


def owner_of(block, per_device):
    if per_device & (per_device - 1) == 0:
        return lax.shift_right_logical(block, per_device.bit_length() - 1)
    return lax.div(block, per_device)


def pack_kernel(per_device, limit, blocks, cache_k, cache_v, kept, sent, sems):
    me = lax.axis_index("ctx")
    even = lax.rem(me, 2) == 0
    count = jnp.int32(0)
    for entry in range(ENTRIES):
        head = entry // NV
        block = blocks[head, entry % NV]
        owner = owner_of(block, per_device)
        mine = owner == me
        local = block - owner * per_device

        def start(pair, head=head, local=local, count=count):
            rows = pl.ds(pl.multiple_of(local * VBLOCK, VBLOCK), VBLOCK)
            for i, target in enumerate((kept, sent)):
                source = pair[i].at[rows, pl.ds(head * HD, HD)]
                pltpu.make_async_copy(source, target.at[count], sems.at[count, i]).start()

        @pl.when(mine & (count < limit))
        def _(start=start):
            @pl.when(even)
            def _():
                start((cache_k, cache_v))

            @pl.when(jnp.logical_not(even))
            def _():
                start((cache_v, cache_k))

        count += mine.astype(jnp.int32)

    for at in range(limit):

        @pl.when(at < count)
        def _(at=at):
            for i, target in enumerate((kept, sent)):
                source = cache_k.at[pl.ds(0, VBLOCK), pl.ds(0, HD)]
                pltpu.make_async_copy(source, target.at[at], sems.at[at, i]).wait()


def pack(blocks, cache_k, cache_v, limit):
    shape = jax.ShapeDtypeStruct((limit, VBLOCK, HD), jnp.bfloat16)
    return pl.pallas_call(
        functools.partial(pack_kernel, cache_k.shape[0] // VBLOCK, limit),
        out_shape=(shape, shape),
        in_specs=[SMEM, ANY, ANY],
        out_specs=(WHOLE, WHOLE),
        scratch_shapes=[pltpu.SemaphoreType.DMA((limit, 2))],
        compiler_params=pltpu.CompilerParams(vmem_limit_bytes=16 * 2**20),
        name="pack",
    )(blocks, cache_k, cache_v)


def walk(blocks, per_device, known, bit, limits, act):
    me = lax.axis_index("ctx")
    at_mine = at_other = jnp.int32(0)
    for entry in range(ENTRIES):
        away = (owner_of(blocks[entry // NV, entry % NV], per_device) ^ me) & ~known
        mine, other = away == 0, away == bit
        tops = jnp.minimum(at_mine, limits[0] - 1), jnp.minimum(at_other, limits[1] - 1)
        act(entry, *tops, at_mine + at_other, other)
        at_mine += mine.astype(jnp.int32)
        at_other += other.astype(jnp.int32)


def merge_kernel(per_device, known, bit, halved, blocks, mine, other, *outs):
    size, rows = outs[0].shape[:2]
    me = lax.axis_index("ctx")
    first = pl.multiple_of(jnp.where((me & halved) == 0, 0, rows), rows) if halved else 0

    def act(entry, at_mine, at_other, place, theirs):
        place = jnp.minimum(place, size - 1)
        for at, out in enumerate(outs):
            span = pl.ds(first + at * rows, rows)
            out[place] = jnp.where(theirs, other[at_other, span], mine[at_mine, span])

    walk(blocks, per_device, known, bit, (mine.shape[0], other.shape[0]), act)


def merged(blocks, per_device, known, bit, mine, other, size, parts=1, halved=0):
    rows = mine.shape[1] // (2 if halved else parts)
    shape = jax.ShapeDtypeStruct((size, rows, HD), jnp.bfloat16)
    outs = pl.pallas_call(
        functools.partial(merge_kernel, per_device, known, bit, halved),
        out_shape=(shape,) * parts,
        in_specs=[SMEM, WHOLE, WHOLE],
        out_specs=(WHOLE,) * parts,
        compiler_params=pltpu.CompilerParams(vmem_limit_bytes=16 * 2**20),
        name="merge",
    )(blocks, mine, other)
    return outs if parts > 1 else outs[0]


def stage_kernel(per_device, known, bit, banded, last, *refs):
    refs = list(refs)
    blocks = refs.pop(0)
    offsets = refs.pop(0) if banded else None
    queries, mine, other, mine_twin, other_twin = refs[:5]
    refs = refs[5:]
    if banded:
        before, own_k, own_v = refs[:3]
        refs = refs[3:]
    else:
        marks_in, mixed_in = refs[:2]
        refs = refs[2:]
    if last:
        out, kbuf, vbuf, held, sems = refs
    else:
        marks_out, mixed_out, kbuf, vbuf = refs
    me = lax.axis_index("ctx")
    even = lax.rem(me, 2) == 0
    wide = NV * ROWS

    def act(entry, at_mine, at_other, place, theirs):
        tile = jnp.where(theirs, other[at_other], mine[at_mine])
        twin = jnp.where(theirs, other_twin[at_other], mine_twin[at_mine])
        rows = pl.ds(entry % NV * ROWS, ROWS)
        kbuf[entry // NV, rows] = jnp.where(even, tile, twin)
        vbuf[entry // NV, rows, :HD] = jnp.where(even, twin, tile)

    if not last:
        walk(blocks, per_device, known, bit, (mine.shape[0], other.shape[0]), act)
    else:
        half = wide // 2
        for head in range(KVH):
            span = slice(head * NV, (head + 1) * NV)
            for at, (own, twin) in enumerate(((mine, mine_twin), (other, other_twin))):
                tile, pair = own[span].reshape(half, HD), twin[span].reshape(half, HD)
                rows = slice(at * half, (at + 1) * half)
                kbuf[head, rows] = jnp.where(even, tile, pair)
                vbuf[head, rows, :HD] = jnp.where(even, pair, tile)
    copies = []
    for head in range(KVH):
        columns = slice(head * HD, (head + 1) * HD)
        vbuf[head, :, HD:] = jnp.ones((vbuf.shape[1], HD), jnp.bfloat16)
        mask = None
        if banded:
            values = slice((KVH + head) * HD, (KVH + head + 1) * HD)
            kbuf[head, wide : wide + SMAX] = before[:, columns]
            kbuf[head, wide + SMAX :] = own_k[:, columns]
            vbuf[head, wide : wide + SMAX, :HD] = before[:, values]
            vbuf[head, wide + SMAX :, :HD] = own_v[:, columns]
            mask = band_mask(offsets, head, me == 0)
        for at in range(0, GROUP, TILE):
            rows = jnp.concatenate(
                [
                    queries[:, (head * GROUP + at + i) * HD : (head * GROUP + at + i + 1) * HD]
                    for i in range(TILE)
                ],
                axis=0,
            )
            start = (head * GROUP + at) * QDEV
            tile = slice(start, start + TILE * QDEV)
            floor = None if banded else marks_in[tile, :1]
            largest, mixed = attend_rows(rows, kbuf[head], vbuf[head], mask, floor)
            mixed, total = mixed[:, :HD], mixed[:, HD:]
            if not banded:
                then = jnp.exp2(floor - largest)
                mixed = mixed + mixed_in[tile] * then
                total = total + marks_in[tile, HD - 1 :] * then
            if last:
                result = (mixed / total).astype(jnp.bfloat16)
                for i in range(TILE):
                    held[head, :, (at + i) * HD : (at + i + 1) * HD] = result[
                        i * QDEV : (i + 1) * QDEV
                    ]
            else:
                lanes = lax.broadcasted_iota(jnp.int32, mixed.shape, 1)
                marks_out[tile] = jnp.where(lanes < HD // 2, largest, total)
                mixed_out[tile] = mixed
        if last:
            span = pl.ds(head * GROUP * HD, GROUP * HD)
            copies.append(pltpu.make_async_copy(held.at[head], out.at[:, span], sems.at[head]))
            copies[-1].start()
    for copy in copies:
        copy.wait()


def attend_stage(known, bit, per_device, blocks, queries, lists, offsets=None, bands=None, state=None):
    banded, last = bands is not None, state is not None
    tall = KVH * GROUP * QDEV
    args = [blocks] + [offsets] * banded + [queries, *lists]
    args += list(bands if banded else state)
    specs = [SMEM] * (1 + banded) + [WHOLE] * (len(args) - 1 - banded)
    keys = NV * ROWS + (SMAX + QDEV) * banded
    scratch = [
        pltpu.VMEM((KVH, keys, HD), jnp.bfloat16),
        pltpu.VMEM((KVH, keys, 2 * HD), jnp.bfloat16),
    ]
    if last:
        out_shape = jax.ShapeDtypeStruct(queries.shape, jnp.bfloat16)
        out_specs = pl.BlockSpec(memory_space=OUT_SPACE)
        scratch += [
            pltpu.VMEM((KVH, QDEV, GROUP * HD), jnp.bfloat16),
            pltpu.SemaphoreType.DMA((KVH,)),
        ]
    else:
        out_shape = (jax.ShapeDtypeStruct((tall, HD), jnp.float32),) * 2
        out_specs = (WHOLE,) * 2
    return pl.pallas_call(
        functools.partial(stage_kernel, per_device, known, bit, banded, last),
        out_shape=out_shape,
        in_specs=specs,
        out_specs=out_specs,
        scratch_shapes=scratch,
        compiler_params=pltpu.CompilerParams(vmem_limit_bytes=VMEM * 2**20),
        cost_estimate=pl.CostEstimate(flops=COST, bytes_accessed=COST, transcendentals=0),
        name="attend_last" if last else "attend_first",
    )(*args)


def permuted(array, pairs):
    return lax.ppermute(array, "ctx", pairs)


def swapped(array, bit):
    return permuted(array, [(i, i ^ bit) for i in range(lax.axis_size("ctx"))])


def fits(blocks, per_device, peers, masks):
    most = [room((1 << mask.bit_count()) / peers) - (mask > 0) for mask in masks]
    owners = (blocks // per_device).reshape(1, 1, ENTRIES)
    ids = jnp.arange(peers, dtype=jnp.int32)[None, :, None]
    away = (owners ^ ids) & ~jnp.array(masks, jnp.int32)[:, None, None]
    counts = jnp.sum((away == 0).astype(jnp.int32), axis=2)
    return jnp.all(counts <= jnp.array(most, jnp.int32)[:, None])


def general(queries, bands, cache_k, cache_v, blocks, offsets, bits):
    keys, values = owned_blocks(blocks, cache_k, cache_v)
    for bit in bits:
        keys, values = keys + swapped(keys, bit), values + swapped(values, bit)
    keys = keys.reshape(KVH, NV * VBLOCK, HD)
    values = values.reshape(KVH, NV * VBLOCK, HD)
    before, own_k, own_v = bands
    wide = KVH * HD
    bands = (before[:, :wide], own_k, before[:, wide:], own_v)
    return attend_dense(offsets, queries, keys, values, bands)


def shards(queries, span_k, span_v, cache_k, cache_v, blocks, offsets):
    peers = lax.axis_size("ctx")
    per_device = cache_k.shape[0] // VBLOCK
    ahead = [(i, i + 1) for i in range(peers - 1)]
    near = 2
    far = [1 << at for at in range(peers.bit_length() - 2, 1, -1)]
    bits = [1] + far + [near]
    masks_a = [sum(bits[:at]) for at in range(len(bits))]
    masks_b = [1 + near + sum(far[:at]) for at in range(len(far))]

    def merge(known, bit, mine, other, **how):
        size = room((1 << (known | bit).bit_count()) / peers)
        if known + bit == peers - 1:
            size = ENTRIES
        return merged(blocks, per_device, known, bit, mine, other, size, **how)

    kept, sent = pack(blocks, cache_k, cache_v, room(1 / peers))
    mine_a, mine_b = merge(0, 1, kept, swapped(sent, 1), parts=STAGES)
    before = permuted(jnp.concatenate([span_k, span_v], axis=1), ahead)
    short = jnp.logical_not(fits(blocks, per_device, peers, masks_a + masks_b)).astype(jnp.int32)

    steps_a = list(zip(masks_a[1:], far))
    steps_b = list(zip([1] + masks_b, [near] + far))
    other_a = swapped(mine_a, far[0])
    other_b = swapped(mine_b, near)
    other_a, before, short = lax.optimization_barrier((other_a, before, short))
    for at, (known, bit) in enumerate(steps_a):
        mine_a = merge(known, bit, mine_a, other_a)
        known_b, bit_b = steps_b[at]
        mine_b = merge(known_b, bit_b, mine_b, other_b, halved=near if at == 0 else 0)
        if at < len(far) - 1:
            mine_a, mine_b = lax.optimization_barrier((mine_a, mine_b))
        other_a = swapped(mine_a, (far + [near])[at + 1])
        other_b = swapped(mine_b, far[at])
        if at < len(far) - 1:
            other_a, other_b = lax.optimization_barrier((other_a, other_b))
    mine_b = merge(*steps_b[-1], mine_b, other_b)
    other_b = swapped(mine_b, near)
    twin_a, twin_b = swapped(mine_a, 1), swapped(mine_b, 1)

    bands = (before, span_k, span_v)
    shared = (peers - 1 - near, near, per_device, blocks, queries)
    lists = (mine_a, other_a, twin_a, swapped(other_a, 1))
    state = attend_stage(*shared, lists, offsets=offsets, bands=bands)
    state, late = lax.optimization_barrier((state, other_b))
    lists = (mine_b, late, twin_b, swapped(late, 1))
    fast = attend_stage(*shared, lists, state=state)

    def again(carry):
        return 0, general(queries, bands, cache_k, cache_v, blocks, offsets, bits)

    return lax.while_loop(lambda carry: carry[0] > 0, again, (short, fast))[1]


def solution(mesh):
    rows = P(("groups", "ctx"), None)
    heads = P("groups", None)
    return jax.shard_map(
        shards,
        mesh=mesh,
        in_specs=(rows, rows, rows, rows, rows, heads, heads),
        out_specs=rows,
        check_vma=False,
    )
```

```python
import functools
import math

import jax
import jax.numpy as jnp
from jax import lax
from jax.experimental import pallas as pl
from jax.experimental.pallas import tpu as pltpu
from jax.sharding import PartitionSpec as P

KVH = 4
GROUP = 8
HD = 128
QDEV = 128
VBLOCK = 64
NV = 16
NS = 64
SMAX = 128
ENTRIES = KVH * NV
FACTOR = math.log2(math.e) / math.sqrt(HD)
LOW = -1e38

ANY = pl.BlockSpec(memory_space=pl.ANY)
SMEM = pl.BlockSpec(memory_space=pltpu.SMEM)


def band_mask(offsets_ref, head, first):
    columns = lax.broadcasted_iota(jnp.int32, (8, SMAX + QDEV), 1)
    distance = SMAX - columns
    row = jnp.zeros((8, SMAX + QDEV), jnp.int32)
    for at in range(NS):
        row = jnp.where(distance == offsets_ref[head, at], 1, row)
    rows = jnp.concatenate([row] * (QDEV // 8), axis=0)
    rolled = pltpu.roll(rows, 0, 1, stride=1, stride_axis=0)
    keys = lax.broadcasted_iota(jnp.int32, (QDEV, SMAX + QDEV), 1)
    return (rolled > 0) & (keys >= jnp.where(first, SMAX, 0))


def attend_rows(rows, keys, values_ones, mask, floor=None):
    scores = lax.dot_general(
        rows, keys, (((1,), (1,)), ((), ())), preferred_element_type=jnp.float32
    )
    if mask is not None:
        wide = scores.shape[1] - mask.shape[1]
        reps = rows.shape[0] // QDEV
        tiled = jnp.concatenate([mask] * reps, axis=0)
        band = jnp.where(tiled, scores[:, wide:], LOW)
        scores = jnp.concatenate([scores[:, :wide], band], axis=1)
    largest = jnp.max(scores, axis=1, keepdims=True) * FACTOR
    if floor is not None:
        largest = jnp.maximum(jnp.broadcast_to(largest, floor.shape), floor)
        above = jnp.concatenate([largest] * (scores.shape[1] // HD), axis=1)
    else:
        above = largest
    weights = jnp.exp2(scores * FACTOR - above).astype(jnp.bfloat16)
    mixed = jnp.dot(weights, values_ones, preferred_element_type=jnp.float32)
    return largest, mixed


def dense_kernel(
    offsets, queries, keys, values, before_k, own_k, before_v, own_v, out, kbuf, vbuf
):
    head = pl.program_id(0)
    first = lax.axis_index("ctx") == 0
    wide = NV * VBLOCK
    kbuf[:wide] = keys[0]
    kbuf[wide : wide + SMAX] = before_k[...]
    kbuf[wide + SMAX :] = own_k[...]
    vbuf[:wide, :HD] = values[0]
    vbuf[wide : wide + SMAX, :HD] = before_v[...]
    vbuf[wide + SMAX :, :HD] = own_v[...]
    vbuf[:, HD:] = jnp.ones((wide + SMAX + QDEV, HD), jnp.bfloat16)
    mask = band_mask(offsets, head, first)
    for at in range(0, GROUP, 2):
        rows = jnp.concatenate(
            [queries[:, (at + i) * HD : (at + i + 1) * HD] for i in range(2)], axis=0
        )
        _, mixed = attend_rows(rows, kbuf[...], vbuf[...], mask)
        result = (mixed[:, :HD] / mixed[:, HD:]).astype(jnp.bfloat16)
        for i in range(2):
            out[:, (at + i) * HD : (at + i + 1) * HD] = result[i * QDEV : (i + 1) * QDEV]


def head_block(rows):
    return pl.BlockSpec((rows, HD), lambda head: (0, head))


def attend_dense(offsets, queries, keys, values, bands):
    wide = NV * VBLOCK
    return pl.pallas_call(
        dense_kernel,
        grid=(KVH,),
        out_shape=jax.ShapeDtypeStruct(queries.shape, jnp.bfloat16),
        in_specs=[
            SMEM,
            pl.BlockSpec((QDEV, GROUP * HD), lambda head: (0, head)),
            pl.BlockSpec((1, wide, HD), lambda head: (head, 0, 0)),
            pl.BlockSpec((1, wide, HD), lambda head: (head, 0, 0)),
        ]
        + [head_block(QDEV)] * 4,
        out_specs=pl.BlockSpec((QDEV, GROUP * HD), lambda head: (0, head)),
        scratch_shapes=[
            pltpu.VMEM((wide + SMAX + QDEV, HD), jnp.bfloat16),
            pltpu.VMEM((wide + SMAX + QDEV, 2 * HD), jnp.bfloat16),
        ],
        compiler_params=pltpu.CompilerParams(vmem_limit_bytes=48 * 2**20),
        name="attend_dense",
    )(offsets, queries, keys, values, *bands)


def owned_kernel(per_device, blocks, cache_k, cache_v, out_k, out_v, sems):
    me = lax.axis_index("ctx")
    out_k[...] = jnp.zeros_like(out_k)
    out_v[...] = jnp.zeros_like(out_v)

    def copies(entry):
        head, at = entry // NV, entry % NV
        block = blocks[head, at]
        local = block % per_device
        rows = pl.ds(pl.multiple_of(local * VBLOCK, VBLOCK), VBLOCK)
        columns = pl.ds(pl.multiple_of(head * HD, HD), HD)
        pairs = ((cache_k, out_k, 0), (cache_v, out_v, 1))
        return block // per_device == me, [
            pltpu.make_async_copy(source.at[rows, columns], target.at[entry], sems.at[entry, i])
            for source, target, i in pairs
        ]

    def start(entry, carry):
        mine, both = copies(entry)

        @pl.when(mine)
        def _():
            for copy in both:
                copy.start()

        return carry

    def wait(entry, carry):
        mine, both = copies(entry)

        @pl.when(mine)
        def _():
            for copy in both:
                copy.wait()

        return carry

    lax.fori_loop(0, ENTRIES, start, 0)
    lax.fori_loop(0, ENTRIES, wait, 0)


def owned_blocks(blocks, cache_k, cache_v):
    shape = jax.ShapeDtypeStruct((ENTRIES, VBLOCK, HD), jnp.bfloat16)
    whole = pl.BlockSpec(memory_space=pltpu.VMEM)
    return pl.pallas_call(
        functools.partial(owned_kernel, cache_k.shape[0] // VBLOCK),
        out_shape=(shape, shape),
        in_specs=[SMEM, ANY, ANY],
        out_specs=(whole, whole),
        scratch_shapes=[pltpu.SemaphoreType.DMA((ENTRIES, 2))],
        compiler_params=pltpu.CompilerParams(vmem_limit_bytes=16 * 2**20),
        name="owned_blocks",
    )(blocks, cache_k, cache_v)


STAGES = 2
TILE = 2
OUT_SPACE = pltpu.HBM
VMEM = 24
COST = 2**20
ROWS = VBLOCK // STAGES
WHOLE = pl.BlockSpec(memory_space=pltpu.VMEM)


def room(share):
    mean = ENTRIES * share
    wide = mean + 3.0 * math.sqrt(mean * (1.0 - share)) + 1.5
    return min(ENTRIES + 1, math.ceil(wide))


def owner_of(block, per_device):
    if per_device & (per_device - 1) == 0:
        return lax.shift_right_logical(block, per_device.bit_length() - 1)
    return lax.div(block, per_device)


def pack_kernel(per_device, limit, blocks, cache_k, cache_v, kept, sent, sems):
    me = lax.axis_index("ctx")
    even = lax.rem(me, 2) == 0
    count = jnp.int32(0)
    for entry in range(ENTRIES):
        head = entry // NV
        block = blocks[head, entry % NV]
        owner = owner_of(block, per_device)
        mine = owner == me
        local = block - owner * per_device

        def start(pair, head=head, local=local, count=count):
            rows = pl.ds(pl.multiple_of(local * VBLOCK, VBLOCK), VBLOCK)
            for i, target in enumerate((kept, sent)):
                source = pair[i].at[rows, pl.ds(head * HD, HD)]
                pltpu.make_async_copy(source, target.at[count], sems.at[count, i]).start()

        @pl.when(mine & (count < limit))
        def _(start=start):
            @pl.when(even)
            def _():
                start((cache_k, cache_v))

            @pl.when(jnp.logical_not(even))
            def _():
                start((cache_v, cache_k))

        count += mine.astype(jnp.int32)

    for at in range(limit):

        @pl.when(at < count)
        def _(at=at):
            for i, target in enumerate((kept, sent)):
                source = cache_k.at[pl.ds(0, VBLOCK), pl.ds(0, HD)]
                pltpu.make_async_copy(source, target.at[at], sems.at[at, i]).wait()


def pack(blocks, cache_k, cache_v, limit):
    shape = jax.ShapeDtypeStruct((limit, VBLOCK, HD), jnp.bfloat16)
    return pl.pallas_call(
        functools.partial(pack_kernel, cache_k.shape[0] // VBLOCK, limit),
        out_shape=(shape, shape),
        in_specs=[SMEM, ANY, ANY],
        out_specs=(WHOLE, WHOLE),
        scratch_shapes=[pltpu.SemaphoreType.DMA((limit, 2))],
        compiler_params=pltpu.CompilerParams(vmem_limit_bytes=16 * 2**20),
        name="pack",
    )(blocks, cache_k, cache_v)


def walk(blocks, per_device, known, bit, limits, act):
    me = lax.axis_index("ctx")
    at_mine = at_other = jnp.int32(0)
    for entry in range(ENTRIES):
        away = (owner_of(blocks[entry // NV, entry % NV], per_device) ^ me) & ~known
        mine, other = away == 0, away == bit
        tops = jnp.minimum(at_mine, limits[0] - 1), jnp.minimum(at_other, limits[1] - 1)
        act(entry, *tops, at_mine + at_other, other)
        at_mine += mine.astype(jnp.int32)
        at_other += other.astype(jnp.int32)


def merge_kernel(per_device, known, bit, halved, blocks, mine, other, *outs):
    size, rows = outs[0].shape[:2]
    me = lax.axis_index("ctx")
    first = pl.multiple_of(jnp.where((me & halved) == 0, 0, rows), rows) if halved else 0

    def act(entry, at_mine, at_other, place, theirs):
        place = jnp.minimum(place, size - 1)
        for at, out in enumerate(outs):
            span = pl.ds(first + at * rows, rows)
            out[place] = jnp.where(theirs, other[at_other, span], mine[at_mine, span])

    walk(blocks, per_device, known, bit, (mine.shape[0], other.shape[0]), act)


def merged(blocks, per_device, known, bit, mine, other, size, parts=1, halved=0):
    rows = mine.shape[1] // (2 if halved else parts)
    shape = jax.ShapeDtypeStruct((size, rows, HD), jnp.bfloat16)
    outs = pl.pallas_call(
        functools.partial(merge_kernel, per_device, known, bit, halved),
        out_shape=(shape,) * parts,
        in_specs=[SMEM, WHOLE, WHOLE],
        out_specs=(WHOLE,) * parts,
        compiler_params=pltpu.CompilerParams(vmem_limit_bytes=16 * 2**20),
        name="merge",
    )(blocks, mine, other)
    return outs if parts > 1 else outs[0]


def stage_kernel(banded, last, *refs):
    refs = list(refs)
    offsets = refs.pop(0) if banded else None
    queries, mine, other, mine_twin, other_twin = refs[:5]
    refs = refs[5:]
    if banded:
        before, own_k, own_v = refs[:3]
        refs = refs[3:]
    else:
        largest_in, total_in, mixed_in = refs[:3]
        refs = refs[3:]
    if last:
        out, kbuf, vbuf, held, sems = refs
    else:
        largest_out, total_out, mixed_out, kbuf, vbuf = refs
    me = lax.axis_index("ctx")
    even = lax.rem(me, 2) == 0
    wide = NV * ROWS

    half = wide // 2
    for head in range(KVH):
        span = slice(head * NV, (head + 1) * NV)
        for at, (own, twin) in enumerate(((mine, mine_twin), (other, other_twin))):
            tile, pair = own[span].reshape(half, HD), twin[span].reshape(half, HD)
            rows = slice(at * half, (at + 1) * half)
            kbuf[head, rows] = jnp.where(even, tile, pair)
            vbuf[head, rows, :HD] = jnp.where(even, pair, tile)
    copies = []
    for head in range(KVH):
        columns = slice(head * HD, (head + 1) * HD)
        vbuf[head, :, HD:] = jnp.ones((vbuf.shape[1], HD), jnp.bfloat16)
        mask = None
        if banded:
            values = slice((KVH + head) * HD, (KVH + head + 1) * HD)
            kbuf[head, wide : wide + SMAX] = before[:, columns]
            kbuf[head, wide + SMAX :] = own_k[:, columns]
            vbuf[head, wide : wide + SMAX, :HD] = before[:, values]
            vbuf[head, wide + SMAX :, :HD] = own_v[:, columns]
            mask = band_mask(offsets, head, me == 0)
        for at in range(0, GROUP, TILE):
            rows = jnp.concatenate(
                [
                    queries[:, (head * GROUP + at + i) * HD : (head * GROUP + at + i + 1) * HD]
                    for i in range(TILE)
                ],
                axis=0,
            )
            start = (head * GROUP + at) * QDEV
            tile = slice(start, start + TILE * QDEV)
            floor = None if banded else largest_in[tile]
            largest, mixed = attend_rows(rows, kbuf[head], vbuf[head], mask, floor)
            mixed, total = mixed[:, :HD], mixed[:, HD:]
            if not banded:
                then = jnp.exp2(floor - largest)
                mixed = mixed + mixed_in[tile] * then
                total = total + total_in[tile] * then
            if last:
                result = (mixed / total).astype(jnp.bfloat16)
                for i in range(TILE):
                    held[head, :, (at + i) * HD : (at + i + 1) * HD] = result[
                        i * QDEV : (i + 1) * QDEV
                    ]
            else:
                largest_out[tile] = jnp.broadcast_to(largest, mixed.shape)
                total_out[tile] = total
                mixed_out[tile] = mixed
        if last:
            span = pl.ds(head * GROUP * HD, GROUP * HD)
            copies.append(pltpu.make_async_copy(held.at[head], out.at[:, span], sems.at[head]))
            copies[-1].start()
    for copy in copies:
        copy.wait()


def attend_stage(queries, lists, offsets=None, bands=None, state=None):
    banded, last = bands is not None, state is not None
    tall = KVH * GROUP * QDEV
    args = [offsets] * banded + [queries, *lists]
    args += list(bands if banded else state)
    specs = [SMEM] * banded + [WHOLE] * (len(args) - banded)
    keys = NV * ROWS + (SMAX + QDEV) * banded
    scratch = [
        pltpu.VMEM((KVH, keys, HD), jnp.bfloat16),
        pltpu.VMEM((KVH, keys, 2 * HD), jnp.bfloat16),
    ]
    if last:
        out_shape = jax.ShapeDtypeStruct(queries.shape, jnp.bfloat16)
        out_specs = pl.BlockSpec(memory_space=OUT_SPACE)
        scratch += [
            pltpu.VMEM((KVH, QDEV, GROUP * HD), jnp.bfloat16),
            pltpu.SemaphoreType.DMA((KVH,)),
        ]
    else:
        out_shape = (jax.ShapeDtypeStruct((tall, HD), jnp.float32),) * 3
        out_specs = (WHOLE,) * 3
    return pl.pallas_call(
        functools.partial(stage_kernel, banded, last),
        out_shape=out_shape,
        in_specs=specs,
        out_specs=out_specs,
        scratch_shapes=scratch,
        compiler_params=pltpu.CompilerParams(vmem_limit_bytes=VMEM * 2**20),
        cost_estimate=pl.CostEstimate(flops=COST, bytes_accessed=COST, transcendentals=0),
        name="attend_last" if last else "attend_first",
    )(*args)


def permuted(array, pairs):
    return lax.ppermute(array, "ctx", pairs)


def swapped(array, bit):
    return permuted(array, [(i, i ^ bit) for i in range(lax.axis_size("ctx"))])


def fits(blocks, per_device, peers, masks):
    most = [room((1 << mask.bit_count()) / peers) - (mask > 0) for mask in masks]
    owners = (blocks // per_device).reshape(1, 1, ENTRIES)
    ids = jnp.arange(peers, dtype=jnp.int32)[None, :, None]
    away = (owners ^ ids) & ~jnp.array(masks, jnp.int32)[:, None, None]
    counts = jnp.sum((away == 0).astype(jnp.int32), axis=2)
    return jnp.all(counts <= jnp.array(most, jnp.int32)[:, None])


def general(queries, bands, cache_k, cache_v, blocks, offsets, bits):
    keys, values = owned_blocks(blocks, cache_k, cache_v)
    for bit in bits:
        keys, values = keys + swapped(keys, bit), values + swapped(values, bit)
    keys = keys.reshape(KVH, NV * VBLOCK, HD)
    values = values.reshape(KVH, NV * VBLOCK, HD)
    before, own_k, own_v = bands
    wide = KVH * HD
    bands = (before[:, :wide], own_k, before[:, wide:], own_v)
    return attend_dense(offsets, queries, keys, values, bands)


def shards(queries, span_k, span_v, cache_k, cache_v, blocks, offsets):
    peers = lax.axis_size("ctx")
    per_device = cache_k.shape[0] // VBLOCK
    ahead = [(i, i + 1) for i in range(peers - 1)]
    near = 2
    far = [1 << at for at in range(peers.bit_length() - 2, 1, -1)]
    bits = [1, near] + far
    masks = [sum(bits[:at]) for at in range(len(bits))]

    def merge(step, mine, other, **how):
        known, bit = masks[step], bits[step]
        size = ENTRIES if step == len(bits) - 1 else room((2 << known.bit_count()) / peers)
        return merged(blocks, per_device, known, bit, mine, other, size, **how)

    kept, sent = pack(blocks, cache_k, cache_v, room(1 / peers))
    mine = list(merge(0, kept, swapped(sent, 1), parts=STAGES))
    spans, mine[1] = lax.optimization_barrier((jnp.concatenate([span_k, span_v], axis=1), mine[1]))
    before = permuted(spans, ahead)
    short = jnp.logical_not(fits(blocks, per_device, peers, masks)).astype(jnp.int32)

    other = [swapped(m, near) for m in mine]
    other[0], short = lax.optimization_barrier((other[0], short))
    for step in range(1, len(bits)):
        nearby = {"halved": near} if step == 1 else {}
        if step > 1:
            other[0], mine[1] = lax.optimization_barrier((other[0], mine[1]))
        mine[0] = merge(step, mine[0], other[0], **nearby)
        other[1], mine[0] = lax.optimization_barrier((other[1], mine[0]))
        if step == 1:
            other[1], before = lax.optimization_barrier((other[1], before))
        mine[1] = merge(step, mine[1], other[1], **nearby)
        after = (bits[2:] + [near])[step - 1]
        other = [swapped(m, after) for m in mine]
    other[0], mine[1] = lax.optimization_barrier((other[0], mine[1]))
    twins = [swapped(m, 1) for m in mine]

    bands = (before, span_k, span_v)
    lists = (mine[0], other[0], twins[0], swapped(other[0], 1))
    state = attend_stage(queries, lists, offsets=offsets, bands=bands)
    state, late = lax.optimization_barrier((state, other[1]))
    lists = (mine[1], late, twins[1], swapped(late, 1))
    fast = attend_stage(queries, lists, state=state)

    def again(carry):
        return 0, general(queries, bands, cache_k, cache_v, blocks, offsets, bits)

    return lax.while_loop(lambda carry: carry[0] > 0, again, (short, fast))[1]


def solution(mesh):
    rows = P(("groups", "ctx"), None)
    heads = P("groups", None)
    return jax.shard_map(
        shards,
        mesh=mesh,
        in_specs=(rows, rows, rows, rows, rows, heads, heads),
        out_specs=rows,
        check_vma=False,
    )
```

```python
import functools
import math

import jax
import jax.numpy as jnp
from jax import lax
from jax.experimental import pallas as pl
from jax.experimental.pallas import tpu as pltpu
from jax.sharding import PartitionSpec as P

KVH = 4
GROUP = 8
HD = 128
QDEV = 128
VBLOCK = 64
NV = 16
NS = 64
SMAX = 128
ENTRIES = KVH * NV
FACTOR = math.log2(math.e) / math.sqrt(HD)
LOW = -1e38

ANY = pl.BlockSpec(memory_space=pl.ANY)
SMEM = pl.BlockSpec(memory_space=pltpu.SMEM)


def band_mask(offsets_ref, head, first):
    columns = lax.broadcasted_iota(jnp.int32, (8, SMAX + QDEV), 1)
    distance = SMAX - columns
    row = jnp.zeros((8, SMAX + QDEV), jnp.int32)
    for at in range(NS):
        row = jnp.where(distance == offsets_ref[head, at], 1, row)
    rows = jnp.concatenate([row] * (QDEV // 8), axis=0)
    rolled = pltpu.roll(rows, 0, 1, stride=1, stride_axis=0)
    keys = lax.broadcasted_iota(jnp.int32, (QDEV, SMAX + QDEV), 1)
    return (rolled > 0) & (keys >= jnp.where(first, SMAX, 0))


def attend_rows(rows, keys, values_ones, mask, floor=None):
    scores = lax.dot_general(
        rows, keys, (((1,), (1,)), ((), ())), preferred_element_type=jnp.float32
    )
    if mask is not None:
        wide = scores.shape[1] - mask.shape[1]
        reps = rows.shape[0] // QDEV
        tiled = jnp.concatenate([mask] * reps, axis=0)
        band = jnp.where(tiled, scores[:, wide:], LOW)
        scores = jnp.concatenate([scores[:, :wide], band], axis=1)
    largest = jnp.max(scores, axis=1, keepdims=True) * FACTOR
    if floor is not None:
        largest = jnp.maximum(jnp.broadcast_to(largest, floor.shape), floor)
        above = jnp.concatenate([largest] * (scores.shape[1] // HD), axis=1)
    else:
        above = largest
    weights = jnp.exp2(scores * FACTOR - above).astype(jnp.bfloat16)
    mixed = jnp.dot(weights, values_ones, preferred_element_type=jnp.float32)
    return largest, mixed


def dense_kernel(
    offsets, queries, keys, values, before_k, own_k, before_v, own_v, out, kbuf, vbuf
):
    head = pl.program_id(0)
    first = lax.axis_index("ctx") == 0
    wide = NV * VBLOCK
    kbuf[:wide] = keys[0]
    kbuf[wide : wide + SMAX] = before_k[...]
    kbuf[wide + SMAX :] = own_k[...]
    vbuf[:wide, :HD] = values[0]
    vbuf[wide : wide + SMAX, :HD] = before_v[...]
    vbuf[wide + SMAX :, :HD] = own_v[...]
    vbuf[:, HD:] = jnp.ones((wide + SMAX + QDEV, HD), jnp.bfloat16)
    mask = band_mask(offsets, head, first)
    for at in range(0, GROUP, 2):
        rows = jnp.concatenate(
            [queries[:, (at + i) * HD : (at + i + 1) * HD] for i in range(2)], axis=0
        )
        _, mixed = attend_rows(rows, kbuf[...], vbuf[...], mask)
        result = (mixed[:, :HD] / mixed[:, HD:]).astype(jnp.bfloat16)
        for i in range(2):
            out[:, (at + i) * HD : (at + i + 1) * HD] = result[i * QDEV : (i + 1) * QDEV]


def head_block(rows):
    return pl.BlockSpec((rows, HD), lambda head: (0, head))


def attend_dense(offsets, queries, keys, values, bands):
    wide = NV * VBLOCK
    return pl.pallas_call(
        dense_kernel,
        grid=(KVH,),
        out_shape=jax.ShapeDtypeStruct(queries.shape, jnp.bfloat16),
        in_specs=[
            SMEM,
            pl.BlockSpec((QDEV, GROUP * HD), lambda head: (0, head)),
            pl.BlockSpec((1, wide, HD), lambda head: (head, 0, 0)),
            pl.BlockSpec((1, wide, HD), lambda head: (head, 0, 0)),
        ]
        + [head_block(QDEV)] * 4,
        out_specs=pl.BlockSpec((QDEV, GROUP * HD), lambda head: (0, head)),
        scratch_shapes=[
            pltpu.VMEM((wide + SMAX + QDEV, HD), jnp.bfloat16),
            pltpu.VMEM((wide + SMAX + QDEV, 2 * HD), jnp.bfloat16),
        ],
        compiler_params=pltpu.CompilerParams(vmem_limit_bytes=48 * 2**20),
        name="attend_dense",
    )(offsets, queries, keys, values, *bands)


def owned_kernel(per_device, blocks, cache_k, cache_v, out_k, out_v, sems):
    me = lax.axis_index("ctx")
    out_k[...] = jnp.zeros_like(out_k)
    out_v[...] = jnp.zeros_like(out_v)

    def copies(entry):
        head, at = entry // NV, entry % NV
        block = blocks[head, at]
        local = block % per_device
        rows = pl.ds(pl.multiple_of(local * VBLOCK, VBLOCK), VBLOCK)
        columns = pl.ds(pl.multiple_of(head * HD, HD), HD)
        pairs = ((cache_k, out_k, 0), (cache_v, out_v, 1))
        return block // per_device == me, [
            pltpu.make_async_copy(source.at[rows, columns], target.at[entry], sems.at[entry, i])
            for source, target, i in pairs
        ]

    def start(entry, carry):
        mine, both = copies(entry)

        @pl.when(mine)
        def _():
            for copy in both:
                copy.start()

        return carry

    def wait(entry, carry):
        mine, both = copies(entry)

        @pl.when(mine)
        def _():
            for copy in both:
                copy.wait()

        return carry

    lax.fori_loop(0, ENTRIES, start, 0)
    lax.fori_loop(0, ENTRIES, wait, 0)


def owned_blocks(blocks, cache_k, cache_v):
    shape = jax.ShapeDtypeStruct((ENTRIES, VBLOCK, HD), jnp.bfloat16)
    whole = pl.BlockSpec(memory_space=pltpu.VMEM)
    return pl.pallas_call(
        functools.partial(owned_kernel, cache_k.shape[0] // VBLOCK),
        out_shape=(shape, shape),
        in_specs=[SMEM, ANY, ANY],
        out_specs=(whole, whole),
        scratch_shapes=[pltpu.SemaphoreType.DMA((ENTRIES, 2))],
        compiler_params=pltpu.CompilerParams(vmem_limit_bytes=16 * 2**20),
        name="owned_blocks",
    )(blocks, cache_k, cache_v)


STAGES = 2
TILE = 2
OUT_SPACE = pltpu.HBM
VMEM = 24
COST = 2**20
ROWS = VBLOCK // STAGES
WHOLE = pl.BlockSpec(memory_space=pltpu.VMEM)


def room(share):
    mean = ENTRIES * share
    wide = mean + 3.0 * math.sqrt(mean * (1.0 - share)) + 1.5
    return min(ENTRIES + 1, math.ceil(wide))


def owner_of(block, per_device):
    if per_device & (per_device - 1) == 0:
        return lax.shift_right_logical(block, per_device.bit_length() - 1)
    return lax.div(block, per_device)


def pack_kernel(per_device, limit, blocks, cache_k, cache_v, kept, sent, sems):
    me = lax.axis_index("ctx")
    even = lax.rem(me, 2) == 0
    count = jnp.int32(0)
    for entry in range(ENTRIES):
        head = entry // NV
        block = blocks[head, entry % NV]
        owner = owner_of(block, per_device)
        mine = owner == me
        local = block - owner * per_device

        def start(pair, head=head, local=local, count=count):
            rows = pl.ds(pl.multiple_of(local * VBLOCK, VBLOCK), VBLOCK)
            for i, target in enumerate((kept, sent)):
                source = pair[i].at[rows, pl.ds(head * HD, HD)]
                pltpu.make_async_copy(source, target.at[count], sems.at[count, i]).start()

        @pl.when(mine & (count < limit))
        def _(start=start):
            @pl.when(even)
            def _():
                start((cache_k, cache_v))

            @pl.when(jnp.logical_not(even))
            def _():
                start((cache_v, cache_k))

        count += mine.astype(jnp.int32)

    for at in range(limit):

        @pl.when(at < count)
        def _(at=at):
            for i, target in enumerate((kept, sent)):
                source = cache_k.at[pl.ds(0, VBLOCK), pl.ds(0, HD)]
                pltpu.make_async_copy(source, target.at[at], sems.at[at, i]).wait()


def pack(blocks, cache_k, cache_v, limit):
    shape = jax.ShapeDtypeStruct((limit, VBLOCK, HD), jnp.bfloat16)
    return pl.pallas_call(
        functools.partial(pack_kernel, cache_k.shape[0] // VBLOCK, limit),
        out_shape=(shape, shape),
        in_specs=[SMEM, ANY, ANY],
        out_specs=(WHOLE, WHOLE),
        scratch_shapes=[pltpu.SemaphoreType.DMA((limit, 2))],
        compiler_params=pltpu.CompilerParams(vmem_limit_bytes=16 * 2**20),
        name="pack",
    )(blocks, cache_k, cache_v)


def walk(blocks, per_device, known, bit, limits, act):
    me = lax.axis_index("ctx")
    at_mine = at_other = jnp.int32(0)
    for entry in range(ENTRIES):
        away = (owner_of(blocks[entry // NV, entry % NV], per_device) ^ me) & ~known
        mine, other = away == 0, away == bit
        tops = jnp.minimum(at_mine, limits[0] - 1), jnp.minimum(at_other, limits[1] - 1)
        act(entry, *tops, at_mine + at_other, other)
        at_mine += mine.astype(jnp.int32)
        at_other += other.astype(jnp.int32)


def merge_kernel(per_device, jobs, blocks, *refs):
    refs = list(refs)
    me = lax.axis_index("ctx")
    sources = [(refs.pop(0), refs.pop(0)) for _ in jobs]
    for (known, bit, halved, parts), (mine, other) in zip(jobs, sources):
        outs = [refs.pop(0) for _ in range(parts)]
        size, rows = outs[0].shape[:2]
        first = pl.multiple_of(jnp.where((me & halved) == 0, 0, rows), rows) if halved else 0

        def act(
            entry, at_mine, at_other, place, theirs, mine=mine, other=other, outs=outs, first=first
        ):
            place = jnp.minimum(place, outs[0].shape[0] - 1)
            for at, out in enumerate(outs):
                span = pl.ds(first + at * out.shape[1], out.shape[1])
                out[place] = jnp.where(theirs, other[at_other, span], mine[at_mine, span])

        walk(blocks, per_device, known, bit, (mine.shape[0], other.shape[0]), act)


def merged(blocks, per_device, jobs):
    shapes, lists = [], []
    for _, _, halved, parts, mine, other, size in jobs:
        rows = mine.shape[1] // (2 if halved else parts)
        shapes += [jax.ShapeDtypeStruct((size, rows, HD), jnp.bfloat16)] * parts
        lists += [mine, other]
    return pl.pallas_call(
        functools.partial(merge_kernel, per_device, [job[:4] for job in jobs]),
        out_shape=tuple(shapes),
        in_specs=[SMEM] + [WHOLE] * len(lists),
        out_specs=(WHOLE,) * len(shapes),
        compiler_params=pltpu.CompilerParams(vmem_limit_bytes=16 * 2**20),
        name="merge",
    )(blocks, *lists)


def stage_kernel(per_device, known, bit, banded, last, *refs):
    refs = list(refs)
    blocks = refs.pop(0)
    offsets = refs.pop(0) if banded else None
    queries, mine, other, mine_twin, other_twin = refs[:5]
    refs = refs[5:]
    if banded:
        before, own_k, own_v = refs[:3]
        refs = refs[3:]
    else:
        largest_in, total_in, mixed_in = refs[:3]
        refs = refs[3:]
    if last:
        out, kbuf, vbuf, held, sems = refs
    else:
        largest_out, total_out, mixed_out, kbuf, vbuf = refs
    me = lax.axis_index("ctx")
    even = lax.rem(me, 2) == 0
    wide = NV * ROWS

    def act(entry, at_mine, at_other, place, theirs):
        tile = jnp.where(theirs, other[at_other], mine[at_mine])
        twin = jnp.where(theirs, other_twin[at_other], mine_twin[at_mine])
        rows = pl.ds(entry % NV * ROWS, ROWS)
        kbuf[entry // NV, rows] = jnp.where(even, tile, twin)
        vbuf[entry // NV, rows, :HD] = jnp.where(even, twin, tile)

    if not last:
        walk(blocks, per_device, known, bit, (mine.shape[0], other.shape[0]), act)
    else:
        half = wide // 2
        for head in range(KVH):
            span = slice(head * NV, (head + 1) * NV)
            for at, (own, twin) in enumerate(((mine, mine_twin), (other, other_twin))):
                tile, pair = own[span].reshape(half, HD), twin[span].reshape(half, HD)
                rows = slice(at * half, (at + 1) * half)
                kbuf[head, rows] = jnp.where(even, tile, pair)
                vbuf[head, rows, :HD] = jnp.where(even, pair, tile)
    copies = []
    for head in range(KVH):
        columns = slice(head * HD, (head + 1) * HD)
        vbuf[head, :, HD:] = jnp.ones((vbuf.shape[1], HD), jnp.bfloat16)
        mask = None
        if banded:
            values = slice((KVH + head) * HD, (KVH + head + 1) * HD)
            kbuf[head, wide : wide + SMAX] = before[:, columns]
            kbuf[head, wide + SMAX :] = own_k[:, columns]
            vbuf[head, wide : wide + SMAX, :HD] = before[:, values]
            vbuf[head, wide + SMAX :, :HD] = own_v[:, columns]
            mask = band_mask(offsets, head, me == 0)
        for at in range(0, GROUP, TILE):
            rows = jnp.concatenate(
                [
                    queries[:, (head * GROUP + at + i) * HD : (head * GROUP + at + i + 1) * HD]
                    for i in range(TILE)
                ],
                axis=0,
            )
            start = (head * GROUP + at) * QDEV
            tile = slice(start, start + TILE * QDEV)
            floor = None if banded else largest_in[tile]
            largest, mixed = attend_rows(rows, kbuf[head], vbuf[head], mask, floor)
            mixed, total = mixed[:, :HD], mixed[:, HD:]
            if not banded:
                then = jnp.exp2(floor - largest)
                mixed = mixed + mixed_in[tile] * then
                total = total + total_in[tile] * then
            if last:
                result = (mixed / total).astype(jnp.bfloat16)
                for i in range(TILE):
                    held[head, :, (at + i) * HD : (at + i + 1) * HD] = result[
                        i * QDEV : (i + 1) * QDEV
                    ]
            else:
                largest_out[tile] = jnp.broadcast_to(largest, mixed.shape)
                total_out[tile] = total
                mixed_out[tile] = mixed
        if last:
            span = pl.ds(head * GROUP * HD, GROUP * HD)
            copies.append(pltpu.make_async_copy(held.at[head], out.at[:, span], sems.at[head]))
            copies[-1].start()
    for copy in copies:
        copy.wait()


def attend_stage(known, bit, per_device, blocks, queries, lists, offsets=None, bands=None, state=None):
    banded, last = bands is not None, state is not None
    tall = KVH * GROUP * QDEV
    args = [blocks] + [offsets] * banded + [queries, *lists]
    args += list(bands if banded else state)
    specs = [SMEM] * (1 + banded) + [WHOLE] * (len(args) - 1 - banded)
    keys = NV * ROWS + (SMAX + QDEV) * banded
    scratch = [
        pltpu.VMEM((KVH, keys, HD), jnp.bfloat16),
        pltpu.VMEM((KVH, keys, 2 * HD), jnp.bfloat16),
    ]
    if last:
        out_shape = jax.ShapeDtypeStruct(queries.shape, jnp.bfloat16)
        out_specs = pl.BlockSpec(memory_space=OUT_SPACE)
        scratch += [
            pltpu.VMEM((KVH, QDEV, GROUP * HD), jnp.bfloat16),
            pltpu.SemaphoreType.DMA((KVH,)),
        ]
    else:
        out_shape = (jax.ShapeDtypeStruct((tall, HD), jnp.float32),) * 3
        out_specs = (WHOLE,) * 3
    return pl.pallas_call(
        functools.partial(stage_kernel, per_device, known, bit, banded, last),
        out_shape=out_shape,
        in_specs=specs,
        out_specs=out_specs,
        scratch_shapes=scratch,
        compiler_params=pltpu.CompilerParams(vmem_limit_bytes=VMEM * 2**20),
        cost_estimate=pl.CostEstimate(flops=COST, bytes_accessed=COST, transcendentals=0),
        name="attend_last" if last else "attend_first",
    )(*args)


def permuted(array, pairs):
    return lax.ppermute(array, "ctx", pairs)


def swapped(array, bit):
    return permuted(array, [(i, i ^ bit) for i in range(lax.axis_size("ctx"))])


def fits(blocks, per_device, peers, masks):
    most = [room((1 << mask.bit_count()) / peers) - (mask > 0) for mask in masks]
    owners = (blocks // per_device).reshape(1, 1, ENTRIES)
    ids = jnp.arange(peers, dtype=jnp.int32)[None, :, None]
    away = (owners ^ ids) & ~jnp.array(masks, jnp.int32)[:, None, None]
    counts = jnp.sum((away == 0).astype(jnp.int32), axis=2)
    return jnp.all(counts <= jnp.array(most, jnp.int32)[:, None])


def general(queries, bands, cache_k, cache_v, blocks, offsets, bits):
    keys, values = owned_blocks(blocks, cache_k, cache_v)
    for bit in bits:
        keys, values = keys + swapped(keys, bit), values + swapped(values, bit)
    keys = keys.reshape(KVH, NV * VBLOCK, HD)
    values = values.reshape(KVH, NV * VBLOCK, HD)
    before, own_k, own_v = bands
    wide = KVH * HD
    bands = (before[:, :wide], own_k, before[:, wide:], own_v)
    return attend_dense(offsets, queries, keys, values, bands)


def shards(queries, span_k, span_v, cache_k, cache_v, blocks, offsets):
    peers = lax.axis_size("ctx")
    per_device = cache_k.shape[0] // VBLOCK
    ahead = [(i, i + 1) for i in range(peers - 1)]
    near = 2
    far = [1 << at for at in range(peers.bit_length() - 2, 1, -1)]
    bits = [1] + far + [near]
    masks_a = [sum(bits[:at]) for at in range(len(bits))]
    masks_b = [1 + near + sum(far[:at]) for at in range(len(far))]

    def job(known, bit, mine, other, parts=1, halved=0):
        size = room((1 << (known | bit).bit_count()) / peers)
        if known + bit == peers - 1:
            size = ENTRIES
        return known, bit, halved, parts, mine, other, size

    merge = functools.partial(merged, blocks, per_device)
    kept, sent = pack(blocks, cache_k, cache_v, room(1 / peers))
    mine_a, mine_b = merge([job(0, 1, kept, swapped(sent, 1), parts=STAGES)])
    before = permuted(jnp.concatenate([span_k, span_v], axis=1), ahead)
    short = jnp.logical_not(fits(blocks, per_device, peers, masks_a + masks_b)).astype(jnp.int32)

    steps_a = list(zip(masks_a[1:], far))
    steps_b = list(zip([1] + masks_b, [near] + far))
    other_a = swapped(mine_a, far[0])
    other_b = swapped(mine_b, near)
    other_a, before, short = lax.optimization_barrier((other_a, before, short))
    for at in range(len(far)):
        job_a = job(*steps_a[at], mine_a, other_a)
        job_b = job(*steps_b[at], mine_b, other_b, halved=near if at == 0 else 0)
        if at < len(far) - 1:
            mine_a, mine_b = merge([job_a, job_b])
        else:
            (mine_a,), (mine_b,) = merge([job_a]), merge([job_b])
        other_a = swapped(mine_a, (far + [near])[at + 1])
        other_b = swapped(mine_b, far[at])
        if at < len(far) - 1:
            other_a, other_b = lax.optimization_barrier((other_a, other_b))
    (mine_b,) = merge([job(*steps_b[-1], mine_b, other_b)])
    other_a, mine_b = lax.optimization_barrier((other_a, mine_b))
    other_b = swapped(mine_b, near)
    twin_a, twin_b = swapped(mine_a, 1), swapped(mine_b, 1)

    bands = (before, span_k, span_v)
    shared = (peers - 1 - near, near, per_device, blocks, queries)
    lists = (mine_a, other_a, twin_a, swapped(other_a, 1))
    state = attend_stage(*shared, lists, offsets=offsets, bands=bands)
    state, late = lax.optimization_barrier((state, other_b))
    lists = (mine_b, late, twin_b, swapped(late, 1))
    fast = attend_stage(*shared, lists, state=state)

    def again(carry):
        return 0, general(queries, bands, cache_k, cache_v, blocks, offsets, bits)

    return lax.while_loop(lambda carry: carry[0] > 0, again, (short, fast))[1]


def solution(mesh):
    rows = P(("groups", "ctx"), None)
    heads = P("groups", None)
    return jax.shard_map(
        shards,
        mesh=mesh,
        in_specs=(rows, rows, rows, rows, rows, heads, heads),
        out_specs=rows,
        check_vma=False,
    )
```

```python
import functools
import math

import jax
import jax.numpy as jnp
from jax import lax
from jax.experimental import pallas as pl
from jax.experimental.pallas import tpu as pltpu
from jax.sharding import PartitionSpec as P

KVH = 4
GROUP = 8
HD = 128
QDEV = 128
VBLOCK = 64
NV = 16
NS = 64
SMAX = 128
ENTRIES = KVH * NV
FACTOR = math.log2(math.e) / math.sqrt(HD)
LOW = -1e38

ANY = pl.BlockSpec(memory_space=pl.ANY)
SMEM = pl.BlockSpec(memory_space=pltpu.SMEM)


def band_mask(offsets, head, first):
    columns = lax.broadcasted_iota(jnp.int32, (8, SMAX + QDEV), 1)
    distance = SMAX - columns
    row = jnp.zeros((8, SMAX + QDEV), jnp.int32)
    for at in range(NS):
        row = jnp.where(distance == offsets[head, at], 1, row)
    rows = jnp.concatenate([row] * (QDEV // 8), axis=0)
    rolled = pltpu.roll(rows, 0, 1, stride=1, stride_axis=0)
    keys = lax.broadcasted_iota(jnp.int32, (QDEV, SMAX + QDEV), 1)
    return (rolled > 0) & (keys >= jnp.where(first, SMAX, 0))


def attend_rows(rows, keys, values_ones, mask, floor=None):
    scores = lax.dot_general(
        rows, keys, (((1,), (1,)), ((), ())), preferred_element_type=jnp.float32
    )
    if mask is not None:
        wide = scores.shape[1] - mask.shape[1]
        reps = rows.shape[0] // QDEV
        tiled = jnp.concatenate([mask] * reps, axis=0)
        band = jnp.where(tiled, scores[:, wide:], LOW)
        scores = jnp.concatenate([scores[:, :wide], band], axis=1)
    largest = jnp.max(scores, axis=1, keepdims=True) * FACTOR
    if floor is not None:
        largest = jnp.maximum(jnp.broadcast_to(largest, floor.shape), floor)
        above = jnp.concatenate([largest] * (scores.shape[1] // HD), axis=1)
    else:
        above = largest
    weights = jnp.exp2(scores * FACTOR - above).astype(jnp.bfloat16)
    mixed = jnp.dot(weights, values_ones, preferred_element_type=jnp.float32)
    return largest, mixed


def dense_kernel(
    offsets, queries, keys, values, before_k, own_k, before_v, own_v, out, kbuf, vbuf
):
    head = pl.program_id(0)
    first = lax.axis_index("ctx") == 0
    wide = NV * VBLOCK
    kbuf[:wide] = keys[0]
    kbuf[wide : wide + SMAX] = before_k[...]
    kbuf[wide + SMAX :] = own_k[...]
    vbuf[:wide, :HD] = values[0]
    vbuf[wide : wide + SMAX, :HD] = before_v[...]
    vbuf[wide + SMAX :, :HD] = own_v[...]
    vbuf[:, HD:] = jnp.ones((wide + SMAX + QDEV, HD), jnp.bfloat16)
    mask = band_mask(offsets, head, first)
    for at in range(0, GROUP, 2):
        rows = jnp.concatenate(
            [queries[:, (at + i) * HD : (at + i + 1) * HD] for i in range(2)], axis=0
        )
        _, mixed = attend_rows(rows, kbuf[...], vbuf[...], mask)
        result = (mixed[:, :HD] / mixed[:, HD:]).astype(jnp.bfloat16)
        for i in range(2):
            out[:, (at + i) * HD : (at + i + 1) * HD] = result[i * QDEV : (i + 1) * QDEV]


def head_block(rows):
    return pl.BlockSpec((rows, HD), lambda head: (0, head))


def attend_dense(offsets, queries, keys, values, bands):
    wide = NV * VBLOCK
    return pl.pallas_call(
        dense_kernel,
        grid=(KVH,),
        out_shape=jax.ShapeDtypeStruct(queries.shape, jnp.bfloat16),
        in_specs=[
            SMEM,
            pl.BlockSpec((QDEV, GROUP * HD), lambda head: (0, head)),
            pl.BlockSpec((1, wide, HD), lambda head: (head, 0, 0)),
            pl.BlockSpec((1, wide, HD), lambda head: (head, 0, 0)),
        ]
        + [head_block(QDEV)] * 4,
        out_specs=pl.BlockSpec((QDEV, GROUP * HD), lambda head: (0, head)),
        scratch_shapes=[
            pltpu.VMEM((wide + SMAX + QDEV, HD), jnp.bfloat16),
            pltpu.VMEM((wide + SMAX + QDEV, 2 * HD), jnp.bfloat16),
        ],
        compiler_params=pltpu.CompilerParams(vmem_limit_bytes=48 * 2**20),
        name="attend_dense",
    )(offsets, queries, keys, values, *bands)


def owned_kernel(per_device, blocks, cache_k, cache_v, out_k, out_v, sems):
    me = lax.axis_index("ctx")
    out_k[...] = jnp.zeros_like(out_k)
    out_v[...] = jnp.zeros_like(out_v)

    def copies(entry):
        head, at = entry // NV, entry % NV
        block = blocks[head, at]
        local = block % per_device
        rows = pl.ds(pl.multiple_of(local * VBLOCK, VBLOCK), VBLOCK)
        columns = pl.ds(pl.multiple_of(head * HD, HD), HD)
        pairs = ((cache_k, out_k, 0), (cache_v, out_v, 1))
        return block // per_device == me, [
            pltpu.make_async_copy(source.at[rows, columns], target.at[entry], sems.at[entry, i])
            for source, target, i in pairs
        ]

    def start(entry, carry):
        mine, both = copies(entry)

        @pl.when(mine)
        def _():
            for copy in both:
                copy.start()

        return carry

    def wait(entry, carry):
        mine, both = copies(entry)

        @pl.when(mine)
        def _():
            for copy in both:
                copy.wait()

        return carry

    lax.fori_loop(0, ENTRIES, start, 0)
    lax.fori_loop(0, ENTRIES, wait, 0)


def owned_blocks(blocks, cache_k, cache_v):
    shape = jax.ShapeDtypeStruct((ENTRIES, VBLOCK, HD), jnp.bfloat16)
    whole = pl.BlockSpec(memory_space=pltpu.VMEM)
    return pl.pallas_call(
        functools.partial(owned_kernel, cache_k.shape[0] // VBLOCK),
        out_shape=(shape, shape),
        in_specs=[SMEM, ANY, ANY],
        out_specs=(whole, whole),
        scratch_shapes=[pltpu.SemaphoreType.DMA((ENTRIES, 2))],
        compiler_params=pltpu.CompilerParams(vmem_limit_bytes=16 * 2**20),
        name="owned_blocks",
    )(blocks, cache_k, cache_v)


STAGES = 2
TILE = 2
OUT_SPACE = pltpu.HBM
VMEM = 24
COST = 2**20
ROWS = VBLOCK // STAGES
WHOLE = pl.BlockSpec(memory_space=pltpu.VMEM)


def room(share):
    mean = ENTRIES * share
    wide = mean + 3.0 * math.sqrt(mean * (1.0 - share)) + 1.5
    return min(ENTRIES + 1, math.ceil(wide))


def owner_of(block, per_device):
    if per_device & (per_device - 1) == 0:
        return lax.shift_right_logical(block, per_device.bit_length() - 1)
    return lax.div(block, per_device)


def pack_kernel(per_device, limit, blocks, cache_k, cache_v, kept, sent, sems):
    me = lax.axis_index("ctx")
    even = lax.rem(me, 2) == 0
    count = jnp.int32(0)
    table = blocks[...]
    for entry in range(ENTRIES):
        head = entry // NV
        block = table[head, entry % NV]
        owner = owner_of(block, per_device)
        mine = owner == me
        local = block - owner * per_device

        def start(pair, head=head, local=local, count=count):
            rows = pl.ds(pl.multiple_of(local * VBLOCK, VBLOCK), VBLOCK)
            for i, target in enumerate((kept, sent)):
                source = pair[i].at[rows, pl.ds(head * HD, HD)]
                pltpu.make_async_copy(source, target.at[count], sems.at[count, i]).start()

        @pl.when(mine & (count < limit))
        def _(start=start):
            @pl.when(even)
            def _():
                start((cache_k, cache_v))

            @pl.when(jnp.logical_not(even))
            def _():
                start((cache_v, cache_k))

        count += mine.astype(jnp.int32)

    for at in range(limit):

        @pl.when(at < count)
        def _(at=at):
            for i, target in enumerate((kept, sent)):
                source = cache_k.at[pl.ds(0, VBLOCK), pl.ds(0, HD)]
                pltpu.make_async_copy(source, target.at[at], sems.at[at, i]).wait()


def pack(blocks, cache_k, cache_v, limit):
    shape = jax.ShapeDtypeStruct((limit, VBLOCK, HD), jnp.bfloat16)
    return pl.pallas_call(
        functools.partial(pack_kernel, cache_k.shape[0] // VBLOCK, limit),
        out_shape=(shape, shape),
        in_specs=[WHOLE, ANY, ANY],
        out_specs=(WHOLE, WHOLE),
        scratch_shapes=[pltpu.SemaphoreType.DMA((limit, 2))],
        compiler_params=pltpu.CompilerParams(vmem_limit_bytes=16 * 2**20),
        name="pack",
    )(blocks, cache_k, cache_v)


def walk(blocks, per_device, known, bit, limits, act):
    me = lax.axis_index("ctx")
    table = blocks[...]
    at_mine = at_other = jnp.int32(0)
    for entry in range(ENTRIES):
        away = (owner_of(table[entry // NV, entry % NV], per_device) ^ me) & ~known
        mine, other = away == 0, away == bit
        tops = jnp.minimum(at_mine, limits[0] - 1), jnp.minimum(at_other, limits[1] - 1)
        act(entry, *tops, at_mine + at_other, other)
        at_mine += mine.astype(jnp.int32)
        at_other += other.astype(jnp.int32)


def merge_kernel(per_device, jobs, blocks, *refs):
    refs = list(refs)
    me = lax.axis_index("ctx")
    sources = [(refs.pop(0), refs.pop(0)) for _ in jobs]
    for (known, bit, halved, parts), (mine, other) in zip(jobs, sources):
        outs = [refs.pop(0) for _ in range(parts)]
        size, rows = outs[0].shape[:2]
        first = pl.multiple_of(jnp.where((me & halved) == 0, 0, rows), rows) if halved else 0

        def act(
            entry, at_mine, at_other, place, theirs, mine=mine, other=other, outs=outs, first=first
        ):
            place = jnp.minimum(place, outs[0].shape[0] - 1)
            for at, out in enumerate(outs):
                span = pl.ds(first + at * out.shape[1], out.shape[1])
                out[place] = jnp.where(theirs, other[at_other, span], mine[at_mine, span])

        walk(blocks, per_device, known, bit, (mine.shape[0], other.shape[0]), act)


def merged(blocks, per_device, jobs):
    shapes, lists = [], []
    for _, _, halved, parts, mine, other, size in jobs:
        rows = mine.shape[1] // (2 if halved else parts)
        shapes += [jax.ShapeDtypeStruct((size, rows, HD), jnp.bfloat16)] * parts
        lists += [mine, other]
    return pl.pallas_call(
        functools.partial(merge_kernel, per_device, [job[:4] for job in jobs]),
        out_shape=tuple(shapes),
        in_specs=[WHOLE] * (1 + len(lists)),
        out_specs=(WHOLE,) * len(shapes),
        compiler_params=pltpu.CompilerParams(vmem_limit_bytes=16 * 2**20),
        name="merge",
    )(blocks, *lists)


def stage_kernel(per_device, known, bit, banded, last, *refs):
    refs = list(refs)
    blocks = refs.pop(0)
    offsets = refs.pop(0) if banded else None
    queries, mine, other, mine_twin, other_twin = refs[:5]
    refs = refs[5:]
    if banded:
        before, own_k, own_v = refs[:3]
        refs = refs[3:]
    else:
        largest_in, total_in, mixed_in = refs[:3]
        refs = refs[3:]
    if last:
        out, kbuf, vbuf, held, sems = refs
    else:
        largest_out, total_out, mixed_out, kbuf, vbuf = refs
    me = lax.axis_index("ctx")
    even = lax.rem(me, 2) == 0
    wide = NV * ROWS

    def act(entry, at_mine, at_other, place, theirs):
        tile = jnp.where(theirs, other[at_other], mine[at_mine])
        twin = jnp.where(theirs, other_twin[at_other], mine_twin[at_mine])
        rows = pl.ds(entry % NV * ROWS, ROWS)
        kbuf[entry // NV, rows] = jnp.where(even, tile, twin)
        vbuf[entry // NV, rows, :HD] = jnp.where(even, twin, tile)

    if not last:
        walk(blocks, per_device, known, bit, (mine.shape[0], other.shape[0]), act)
    else:
        half = wide // 2
        for head in range(KVH):
            span = slice(head * NV, (head + 1) * NV)
            for at, (own, twin) in enumerate(((mine, mine_twin), (other, other_twin))):
                tile, pair = own[span].reshape(half, HD), twin[span].reshape(half, HD)
                rows = slice(at * half, (at + 1) * half)
                kbuf[head, rows] = jnp.where(even, tile, pair)
                vbuf[head, rows, :HD] = jnp.where(even, pair, tile)
    copies = []
    for head in range(KVH):
        columns = slice(head * HD, (head + 1) * HD)
        vbuf[head, :, HD:] = jnp.ones((vbuf.shape[1], HD), jnp.bfloat16)
        mask = None
        if banded:
            values = slice((KVH + head) * HD, (KVH + head + 1) * HD)
            kbuf[head, wide : wide + SMAX] = before[:, columns]
            kbuf[head, wide + SMAX :] = own_k[:, columns]
            vbuf[head, wide : wide + SMAX, :HD] = before[:, values]
            vbuf[head, wide + SMAX :, :HD] = own_v[:, columns]
            mask = band_mask(offsets[...], head, me == 0)
        for at in range(0, GROUP, TILE):
            rows = jnp.concatenate(
                [
                    queries[:, (head * GROUP + at + i) * HD : (head * GROUP + at + i + 1) * HD]
                    for i in range(TILE)
                ],
                axis=0,
            )
            start = (head * GROUP + at) * QDEV
            tile = slice(start, start + TILE * QDEV)
            floor = None if banded else largest_in[tile]
            largest, mixed = attend_rows(rows, kbuf[head], vbuf[head], mask, floor)
            mixed, total = mixed[:, :HD], mixed[:, HD:]
            if not banded:
                then = jnp.exp2(floor - largest)
                mixed = mixed + mixed_in[tile] * then
                total = total + total_in[tile] * then
            if last:
                result = (mixed / total).astype(jnp.bfloat16)
                for i in range(TILE):
                    held[head, :, (at + i) * HD : (at + i + 1) * HD] = result[
                        i * QDEV : (i + 1) * QDEV
                    ]
            else:
                largest_out[tile] = jnp.broadcast_to(largest, mixed.shape)
                total_out[tile] = total
                mixed_out[tile] = mixed
        if last:
            span = pl.ds(head * GROUP * HD, GROUP * HD)
            copies.append(pltpu.make_async_copy(held.at[head], out.at[:, span], sems.at[head]))
            copies[-1].start()
    for copy in copies:
        copy.wait()


def attend_stage(known, bit, per_device, blocks, queries, lists, offsets=None, bands=None, state=None):
    banded, last = bands is not None, state is not None
    tall = KVH * GROUP * QDEV
    args = [blocks] + [offsets] * banded + [queries, *lists]
    args += list(bands if banded else state)
    specs = [WHOLE] * len(args)
    keys = NV * ROWS + (SMAX + QDEV) * banded
    scratch = [
        pltpu.VMEM((KVH, keys, HD), jnp.bfloat16),
        pltpu.VMEM((KVH, keys, 2 * HD), jnp.bfloat16),
    ]
    if last:
        out_shape = jax.ShapeDtypeStruct(queries.shape, jnp.bfloat16)
        out_specs = pl.BlockSpec(memory_space=OUT_SPACE)
        scratch += [
            pltpu.VMEM((KVH, QDEV, GROUP * HD), jnp.bfloat16),
            pltpu.SemaphoreType.DMA((KVH,)),
        ]
    else:
        out_shape = (jax.ShapeDtypeStruct((tall, HD), jnp.float32),) * 3
        out_specs = (WHOLE,) * 3
    return pl.pallas_call(
        functools.partial(stage_kernel, per_device, known, bit, banded, last),
        out_shape=out_shape,
        in_specs=specs,
        out_specs=out_specs,
        scratch_shapes=scratch,
        compiler_params=pltpu.CompilerParams(vmem_limit_bytes=VMEM * 2**20),
        cost_estimate=pl.CostEstimate(flops=COST, bytes_accessed=COST, transcendentals=0),
        name="attend_last" if last else "attend_first",
    )(*args)


def permuted(array, pairs):
    return lax.ppermute(array, "ctx", pairs)


def swapped(array, bit):
    return permuted(array, [(i, i ^ bit) for i in range(lax.axis_size("ctx"))])


def fits(blocks, per_device, peers, masks):
    most = [room((1 << mask.bit_count()) / peers) - (mask > 0) for mask in masks]
    owners = (blocks // per_device).reshape(1, 1, ENTRIES)
    ids = jnp.arange(peers, dtype=jnp.int32)[None, :, None]
    away = (owners ^ ids) & ~jnp.array(masks, jnp.int32)[:, None, None]
    counts = jnp.sum((away == 0).astype(jnp.int32), axis=2)
    return jnp.all(counts <= jnp.array(most, jnp.int32)[:, None])


def general(queries, bands, cache_k, cache_v, blocks, offsets, bits):
    keys, values = owned_blocks(blocks, cache_k, cache_v)
    for bit in bits:
        keys, values = keys + swapped(keys, bit), values + swapped(values, bit)
    keys = keys.reshape(KVH, NV * VBLOCK, HD)
    values = values.reshape(KVH, NV * VBLOCK, HD)
    before, own_k, own_v = bands
    wide = KVH * HD
    bands = (before[:, :wide], own_k, before[:, wide:], own_v)
    return attend_dense(offsets, queries, keys, values, bands)


def shards(queries, span_k, span_v, cache_k, cache_v, blocks, offsets):
    peers = lax.axis_size("ctx")
    per_device = cache_k.shape[0] // VBLOCK
    ahead = [(i, i + 1) for i in range(peers - 1)]
    near = 2
    far = [1 << at for at in range(peers.bit_length() - 2, 1, -1)]
    bits = [1] + far + [near]
    masks_a = [sum(bits[:at]) for at in range(len(bits))]
    masks_b = [1 + near + sum(far[:at]) for at in range(len(far))]

    def job(known, bit, mine, other, parts=1, halved=0):
        size = room((1 << (known | bit).bit_count()) / peers)
        if known + bit == peers - 1:
            size = ENTRIES
        return known, bit, halved, parts, mine, other, size

    merge = functools.partial(merged, blocks, per_device)
    kept, sent = pack(blocks, cache_k, cache_v, room(1 / peers))
    mine_a, mine_b = merge([job(0, 1, kept, swapped(sent, 1), parts=STAGES)])
    before = permuted(jnp.concatenate([span_k, span_v], axis=1), ahead)
    short = jnp.logical_not(fits(blocks, per_device, peers, masks_a + masks_b)).astype(jnp.int32)

    steps_a = list(zip(masks_a[1:], far))
    steps_b = list(zip([1] + masks_b, [near] + far))
    other_a = swapped(mine_a, far[0])
    other_b = swapped(mine_b, near)
    other_a, before, short = lax.optimization_barrier((other_a, before, short))
    for at in range(len(far)):
        job_a = job(*steps_a[at], mine_a, other_a)
        job_b = job(*steps_b[at], mine_b, other_b, halved=near if at == 0 else 0)
        if at < len(far) - 1:
            mine_a, mine_b = merge([job_a, job_b])
        else:
            (mine_a,), (mine_b,) = merge([job_a]), merge([job_b])
        other_a = swapped(mine_a, (far + [near])[at + 1])
        other_b = swapped(mine_b, far[at])
        if at < len(far) - 1:
            other_a, other_b = lax.optimization_barrier((other_a, other_b))
    (mine_b,) = merge([job(*steps_b[-1], mine_b, other_b)])
    other_a, mine_b = lax.optimization_barrier((other_a, mine_b))
    other_b = swapped(mine_b, near)
    twin_a, twin_b = swapped(mine_a, 1), swapped(mine_b, 1)

    bands = (before, span_k, span_v)
    shared = (peers - 1 - near, near, per_device, blocks, queries)
    lists = (mine_a, other_a, twin_a, swapped(other_a, 1))
    state = attend_stage(*shared, lists, offsets=offsets, bands=bands)
    state, late = lax.optimization_barrier((state, other_b))
    lists = (mine_b, late, twin_b, swapped(late, 1))
    fast = attend_stage(*shared, lists, state=state)

    def again(carry):
        return 0, general(queries, bands, cache_k, cache_v, blocks, offsets, bits)

    return lax.while_loop(lambda carry: carry[0] > 0, again, (short, fast))[1]


def solution(mesh):
    rows = P(("groups", "ctx"), None)
    heads = P("groups", None)
    return jax.shard_map(
        shards,
        mesh=mesh,
        in_specs=(rows, rows, rows, rows, rows, heads, heads),
        out_specs=rows,
        check_vma=False,
    )
```

```python
import functools
import math

import jax
import jax.numpy as jnp
from jax import lax
from jax.experimental import pallas as pl
from jax.experimental.pallas import tpu as pltpu
from jax.sharding import PartitionSpec as P

KVH = 4
GROUP = 8
HD = 128
QDEV = 128
VBLOCK = 64
NV = 16
NS = 64
SMAX = 128
ENTRIES = KVH * NV
FACTOR = math.log2(math.e) / math.sqrt(HD)
LOW = -1e38

ANY = pl.BlockSpec(memory_space=pl.ANY)
SMEM = pl.BlockSpec(memory_space=pltpu.SMEM)


def band_mask(offsets, head, first):
    columns = lax.broadcasted_iota(jnp.int32, (8, SMAX + QDEV), 1)
    distance = SMAX - columns
    row = jnp.zeros((8, SMAX + QDEV), jnp.int32)
    for at in range(NS):
        row = jnp.where(distance == offsets[head, at], 1, row)
    rows = jnp.concatenate([row] * (QDEV // 8), axis=0)
    rolled = pltpu.roll(rows, 0, 1, stride=1, stride_axis=0)
    keys = lax.broadcasted_iota(jnp.int32, (QDEV, SMAX + QDEV), 1)
    return (rolled > 0) & (keys >= jnp.where(first, SMAX, 0))


def attend_rows(rows, keys, values_ones, mask, floor=None):
    scores = lax.dot_general(
        rows, keys, (((1,), (1,)), ((), ())), preferred_element_type=jnp.float32
    )
    if mask is not None:
        wide = scores.shape[1] - mask.shape[1]
        reps = rows.shape[0] // QDEV
        tiled = jnp.concatenate([mask] * reps, axis=0)
        band = jnp.where(tiled, scores[:, wide:], LOW)
        scores = jnp.concatenate([scores[:, :wide], band], axis=1)
    largest = jnp.max(scores, axis=1, keepdims=True) * FACTOR
    if floor is not None:
        largest = jnp.maximum(jnp.broadcast_to(largest, floor.shape), floor)
        above = jnp.concatenate([largest] * (scores.shape[1] // HD), axis=1)
    else:
        above = largest
    weights = jnp.exp2(scores * FACTOR - above).astype(jnp.bfloat16)
    mixed = jnp.dot(weights, values_ones, preferred_element_type=jnp.float32)
    return largest, mixed


def dense_kernel(
    offsets, queries, keys, values, before_k, own_k, before_v, own_v, out, kbuf, vbuf
):
    head = pl.program_id(0)
    first = lax.axis_index("ctx") == 0
    wide = NV * VBLOCK
    kbuf[:wide] = keys[0]
    kbuf[wide : wide + SMAX] = before_k[...]
    kbuf[wide + SMAX :] = own_k[...]
    vbuf[:wide, :HD] = values[0]
    vbuf[wide : wide + SMAX, :HD] = before_v[...]
    vbuf[wide + SMAX :, :HD] = own_v[...]
    vbuf[:, HD:] = jnp.ones((wide + SMAX + QDEV, HD), jnp.bfloat16)
    mask = band_mask(offsets, head, first)
    for at in range(0, GROUP, 2):
        rows = jnp.concatenate(
            [queries[:, (at + i) * HD : (at + i + 1) * HD] for i in range(2)], axis=0
        )
        _, mixed = attend_rows(rows, kbuf[...], vbuf[...], mask)
        result = (mixed[:, :HD] / mixed[:, HD:]).astype(jnp.bfloat16)
        for i in range(2):
            out[:, (at + i) * HD : (at + i + 1) * HD] = result[i * QDEV : (i + 1) * QDEV]


def head_block(rows):
    return pl.BlockSpec((rows, HD), lambda head: (0, head))


def attend_dense(offsets, queries, keys, values, bands):
    wide = NV * VBLOCK
    return pl.pallas_call(
        dense_kernel,
        grid=(KVH,),
        out_shape=jax.ShapeDtypeStruct(queries.shape, jnp.bfloat16),
        in_specs=[
            SMEM,
            pl.BlockSpec((QDEV, GROUP * HD), lambda head: (0, head)),
            pl.BlockSpec((1, wide, HD), lambda head: (head, 0, 0)),
            pl.BlockSpec((1, wide, HD), lambda head: (head, 0, 0)),
        ]
        + [head_block(QDEV)] * 4,
        out_specs=pl.BlockSpec((QDEV, GROUP * HD), lambda head: (0, head)),
        scratch_shapes=[
            pltpu.VMEM((wide + SMAX + QDEV, HD), jnp.bfloat16),
            pltpu.VMEM((wide + SMAX + QDEV, 2 * HD), jnp.bfloat16),
        ],
        compiler_params=pltpu.CompilerParams(vmem_limit_bytes=48 * 2**20),
        name="attend_dense",
    )(offsets, queries, keys, values, *bands)


def owned_kernel(per_device, blocks, cache_k, cache_v, out_k, out_v, sems):
    me = lax.axis_index("ctx")
    out_k[...] = jnp.zeros_like(out_k)
    out_v[...] = jnp.zeros_like(out_v)

    def copies(entry):
        head, at = entry // NV, entry % NV
        block = blocks[head, at]
        local = block % per_device
        rows = pl.ds(pl.multiple_of(local * VBLOCK, VBLOCK), VBLOCK)
        columns = pl.ds(pl.multiple_of(head * HD, HD), HD)
        pairs = ((cache_k, out_k, 0), (cache_v, out_v, 1))
        return block // per_device == me, [
            pltpu.make_async_copy(source.at[rows, columns], target.at[entry], sems.at[entry, i])
            for source, target, i in pairs
        ]

    def start(entry, carry):
        mine, both = copies(entry)

        @pl.when(mine)
        def _():
            for copy in both:
                copy.start()

        return carry

    def wait(entry, carry):
        mine, both = copies(entry)

        @pl.when(mine)
        def _():
            for copy in both:
                copy.wait()

        return carry

    lax.fori_loop(0, ENTRIES, start, 0)
    lax.fori_loop(0, ENTRIES, wait, 0)


def owned_blocks(blocks, cache_k, cache_v):
    shape = jax.ShapeDtypeStruct((ENTRIES, VBLOCK, HD), jnp.bfloat16)
    whole = pl.BlockSpec(memory_space=pltpu.VMEM)
    return pl.pallas_call(
        functools.partial(owned_kernel, cache_k.shape[0] // VBLOCK),
        out_shape=(shape, shape),
        in_specs=[SMEM, ANY, ANY],
        out_specs=(whole, whole),
        scratch_shapes=[pltpu.SemaphoreType.DMA((ENTRIES, 2))],
        compiler_params=pltpu.CompilerParams(vmem_limit_bytes=16 * 2**20),
        name="owned_blocks",
    )(blocks, cache_k, cache_v)


STAGES = 2
TILE = 2
OUT_SPACE = pltpu.HBM
VMEM = 24
COST = 2**20
ROWS = VBLOCK // STAGES
WHOLE = pl.BlockSpec(memory_space=pltpu.VMEM)


def room(share):
    mean = ENTRIES * share
    wide = mean + 3.0 * math.sqrt(mean * (1.0 - share)) + 1.5
    return min(ENTRIES + 1, math.ceil(wide))


def owner_of(block, per_device):
    if per_device & (per_device - 1) == 0:
        return lax.shift_right_logical(block, per_device.bit_length() - 1)
    return lax.div(block, per_device)


def pack_kernel(per_device, limit, blocks, cache_k, cache_v, kept, sent, sems):
    me = lax.axis_index("ctx")
    even = lax.rem(me, 2) == 0
    count = jnp.int32(0)
    table = blocks[...]
    for entry in range(ENTRIES):
        head = entry // NV
        block = table[head, entry % NV]
        owner = owner_of(block, per_device)
        mine = owner == me
        local = block - owner * per_device

        def start(pair, head=head, local=local, count=count):
            rows = pl.ds(pl.multiple_of(local * VBLOCK, VBLOCK), VBLOCK)
            for i, target in enumerate((kept, sent)):
                source = pair[i].at[rows, pl.ds(head * HD, HD)]
                pltpu.make_async_copy(source, target.at[count], sems.at[count, i]).start()

        @pl.when(mine & (count < limit))
        def _(start=start):
            @pl.when(even)
            def _():
                start((cache_k, cache_v))

            @pl.when(jnp.logical_not(even))
            def _():
                start((cache_v, cache_k))

        count += mine.astype(jnp.int32)

    for at in range(limit):

        @pl.when(at < count)
        def _(at=at):
            for i, target in enumerate((kept, sent)):
                source = cache_k.at[pl.ds(0, VBLOCK), pl.ds(0, HD)]
                pltpu.make_async_copy(source, target.at[at], sems.at[at, i]).wait()


def pack(blocks, cache_k, cache_v, limit):
    shape = jax.ShapeDtypeStruct((limit, VBLOCK, HD), jnp.bfloat16)
    return pl.pallas_call(
        functools.partial(pack_kernel, cache_k.shape[0] // VBLOCK, limit),
        out_shape=(shape, shape),
        in_specs=[WHOLE, ANY, ANY],
        out_specs=(WHOLE, WHOLE),
        scratch_shapes=[pltpu.SemaphoreType.DMA((limit, 2))],
        compiler_params=pltpu.CompilerParams(vmem_limit_bytes=16 * 2**20),
        name="pack",
    )(blocks, cache_k, cache_v)


def walk(blocks, per_device, known, bit, limits, act):
    me = lax.axis_index("ctx")
    table = blocks[...]
    at_mine = at_other = jnp.int32(0)
    for entry in range(ENTRIES):
        away = (owner_of(table[entry // NV, entry % NV], per_device) ^ me) & ~known
        mine, other = away == 0, away == bit
        tops = jnp.minimum(at_mine, limits[0] - 1), jnp.minimum(at_other, limits[1] - 1)
        act(entry, *tops, at_mine + at_other, other)
        at_mine += mine.astype(jnp.int32)
        at_other += other.astype(jnp.int32)


def merge_kernel(per_device, jobs, blocks, *refs):
    refs = list(refs)
    me = lax.axis_index("ctx")
    sources = [(refs.pop(0), refs.pop(0)) for _ in jobs]
    for (known, bit, halved, parts), (mine, other) in zip(jobs, sources):
        outs = [refs.pop(0) for _ in range(parts)]
        size, rows = outs[0].shape[:2]
        first = pl.multiple_of(jnp.where((me & halved) == 0, 0, rows), rows) if halved else 0

        def act(
            entry, at_mine, at_other, place, theirs, mine=mine, other=other, outs=outs, first=first
        ):
            place = jnp.minimum(place, outs[0].shape[0] - 1)
            for at, out in enumerate(outs):
                span = pl.ds(first + at * out.shape[1], out.shape[1])
                out[place] = jnp.where(theirs, other[at_other, span], mine[at_mine, span])

        walk(blocks, per_device, known, bit, (mine.shape[0], other.shape[0]), act)


def merged(blocks, per_device, jobs):
    shapes, lists = [], []
    for _, _, halved, parts, mine, other, size in jobs:
        rows = mine.shape[1] // (2 if halved else parts)
        shapes += [jax.ShapeDtypeStruct((size, rows, HD), jnp.bfloat16)] * parts
        lists += [mine, other]
    return pl.pallas_call(
        functools.partial(merge_kernel, per_device, [job[:4] for job in jobs]),
        out_shape=tuple(shapes),
        in_specs=[WHOLE] * (1 + len(lists)),
        out_specs=(WHOLE,) * len(shapes),
        compiler_params=pltpu.CompilerParams(vmem_limit_bytes=16 * 2**20),
        name="merge",
    )(blocks, *lists)


def stage_kernel(per_device, known, bit, banded, last, *refs):
    refs = list(refs)
    blocks = refs.pop(0)
    offsets = refs.pop(0) if banded else None
    queries, mine, other, mine_twin, other_twin = refs[:5]
    refs = refs[5:]
    if banded:
        before, own_k, own_v = refs[:3]
        refs = refs[3:]
    else:
        largest_in, total_in, mixed_in = refs[:3]
        refs = refs[3:]
    if last:
        out, kbuf, vbuf, held, sems = refs
    else:
        largest_out, total_out, mixed_out, kbuf, vbuf = refs
    me = lax.axis_index("ctx")
    even = lax.rem(me, 2) == 0
    wide = NV * ROWS

    def act(entry, at_mine, at_other, place, theirs):
        tile = jnp.where(theirs, other[at_other], mine[at_mine])
        twin = jnp.where(theirs, other_twin[at_other], mine_twin[at_mine])
        rows = pl.ds(entry % NV * ROWS, ROWS)
        kbuf[entry // NV, rows] = jnp.where(even, tile, twin)
        vbuf[entry // NV, rows, :HD] = jnp.where(even, twin, tile)

    if not last:
        walk(blocks, per_device, known, bit, (mine.shape[0], other.shape[0]), act)
    else:
        half = wide // 2
        for head in range(KVH):
            span = slice(head * NV, (head + 1) * NV)
            for at, (own, twin) in enumerate(((mine, mine_twin), (other, other_twin))):
                tile, pair = own[span].reshape(half, HD), twin[span].reshape(half, HD)
                rows = slice(at * half, (at + 1) * half)
                kbuf[head, rows] = jnp.where(even, tile, pair)
                vbuf[head, rows, :HD] = jnp.where(even, pair, tile)
    copies = []
    for head in range(KVH):
        columns = slice(head * HD, (head + 1) * HD)
        vbuf[head, :, HD:] = jnp.ones((vbuf.shape[1], HD), jnp.bfloat16)
        mask = None
        if banded:
            values = slice((KVH + head) * HD, (KVH + head + 1) * HD)
            kbuf[head, wide : wide + SMAX] = before[:, columns]
            kbuf[head, wide + SMAX :] = own_k[:, columns]
            vbuf[head, wide : wide + SMAX, :HD] = before[:, values]
            vbuf[head, wide + SMAX :, :HD] = own_v[:, columns]
            mask = band_mask(offsets[...], head, me == 0)
        for at in range(0, GROUP, TILE):
            rows = jnp.concatenate(
                [
                    queries[:, (head * GROUP + at + i) * HD : (head * GROUP + at + i + 1) * HD]
                    for i in range(TILE)
                ],
                axis=0,
            )
            start = (head * GROUP + at) * QDEV
            tile = slice(start, start + TILE * QDEV)
            floor = None if banded else largest_in[tile]
            largest, mixed = attend_rows(rows, kbuf[head], vbuf[head], mask, floor)
            mixed, total = mixed[:, :HD], mixed[:, HD:]
            if not banded:
                then = jnp.exp2(floor - largest)
                mixed = mixed + mixed_in[tile] * then
                total = total + total_in[tile] * then
            if last:
                result = (mixed / total).astype(jnp.bfloat16)
                for i in range(TILE):
                    held[head, :, (at + i) * HD : (at + i + 1) * HD] = result[
                        i * QDEV : (i + 1) * QDEV
                    ]
            else:
                largest_out[tile] = jnp.broadcast_to(largest, mixed.shape)
                total_out[tile] = total
                mixed_out[tile] = mixed
        if last:
            span = pl.ds(head * GROUP * HD, GROUP * HD)
            copies.append(pltpu.make_async_copy(held.at[head], out.at[:, span], sems.at[head]))
            copies[-1].start()
    for copy in copies:
        copy.wait()


def attend_stage(known, bit, per_device, blocks, queries, lists, offsets=None, bands=None, state=None):
    banded, last = bands is not None, state is not None
    tall = KVH * GROUP * QDEV
    args = [blocks] + [offsets] * banded + [queries, *lists]
    args += list(bands if banded else state)
    specs = [WHOLE] * len(args)
    keys = NV * ROWS + (SMAX + QDEV) * banded
    scratch = [
        pltpu.VMEM((KVH, keys, HD), jnp.bfloat16),
        pltpu.VMEM((KVH, keys, 2 * HD), jnp.bfloat16),
    ]
    if last:
        out_shape = jax.ShapeDtypeStruct(queries.shape, jnp.bfloat16)
        out_specs = pl.BlockSpec(memory_space=OUT_SPACE)
        scratch += [
            pltpu.VMEM((KVH, QDEV, GROUP * HD), jnp.bfloat16),
            pltpu.SemaphoreType.DMA((KVH,)),
        ]
    else:
        out_shape = (jax.ShapeDtypeStruct((tall, HD), jnp.float32),) * 3
        out_specs = (WHOLE,) * 3
    return pl.pallas_call(
        functools.partial(stage_kernel, per_device, known, bit, banded, last),
        out_shape=out_shape,
        in_specs=specs,
        out_specs=out_specs,
        scratch_shapes=scratch,
        compiler_params=pltpu.CompilerParams(vmem_limit_bytes=VMEM * 2**20),
        cost_estimate=pl.CostEstimate(flops=COST, bytes_accessed=COST, transcendentals=0),
        name="attend_last" if last else "attend_first",
    )(*args)


def permuted(array, pairs):
    return lax.ppermute(array, "ctx", pairs)


def swapped(array, bit):
    return permuted(array, [(i, i ^ bit) for i in range(lax.axis_size("ctx"))])


def fits(blocks, per_device, peers, masks):
    most = [room((1 << mask.bit_count()) / peers) - (mask > 0) for mask in masks]
    owners = (blocks // per_device).reshape(1, 1, ENTRIES)
    ids = jnp.arange(peers, dtype=jnp.int32)[None, :, None]
    away = (owners ^ ids) & ~jnp.array(masks, jnp.int32)[:, None, None]
    counts = jnp.sum((away == 0).astype(jnp.int32), axis=2)
    return jnp.all(counts <= jnp.array(most, jnp.int32)[:, None])


def general(queries, bands, cache_k, cache_v, blocks, offsets, bits):
    keys, values = owned_blocks(blocks, cache_k, cache_v)
    for bit in bits:
        keys, values = keys + swapped(keys, bit), values + swapped(values, bit)
    keys = keys.reshape(KVH, NV * VBLOCK, HD)
    values = values.reshape(KVH, NV * VBLOCK, HD)
    before, own_k, own_v = bands
    wide = KVH * HD
    bands = (before[:, :wide], own_k, before[:, wide:], own_v)
    return attend_dense(offsets, queries, keys, values, bands)


def shards(queries, span_k, span_v, cache_k, cache_v, blocks, offsets):
    peers = lax.axis_size("ctx")
    per_device = cache_k.shape[0] // VBLOCK
    ahead = [(i, i + 1) for i in range(peers - 1)]
    near = 2
    far = [1 << at for at in range(peers.bit_length() - 2, 1, -1)]
    bits = [1] + far + [near]
    masks_a = [sum(bits[:at]) for at in range(len(bits))]
    masks_b = [1 + near + sum(far[:at]) for at in range(len(far))]

    def job(known, bit, mine, other, parts=1, halved=0):
        size = room((1 << (known | bit).bit_count()) / peers)
        if known + bit == peers - 1:
            size = ENTRIES
        return known, bit, halved, parts, mine, other, size

    merge = functools.partial(merged, blocks, per_device)
    kept, sent = pack(blocks, cache_k, cache_v, room(1 / peers))
    mine_a, mine_b = merge([job(0, 1, kept, swapped(sent, 1), parts=STAGES)])
    spans, mine_b = lax.optimization_barrier((jnp.concatenate([span_k, span_v], axis=1), mine_b))
    before = permuted(spans, ahead)
    short = jnp.logical_not(fits(blocks, per_device, peers, masks_a + masks_b)).astype(jnp.int32)

    steps_a = list(zip(masks_a[1:], far))
    steps_b = list(zip([1] + masks_b, [near] + far))
    other_a = swapped(mine_a, far[0])
    other_b = swapped(mine_b, near)
    other_a, short = lax.optimization_barrier((other_a, short))
    for at in range(len(far)):
        job_a = job(*steps_a[at], mine_a, other_a)
        job_b = job(*steps_b[at], mine_b, other_b, halved=near if at == 0 else 0)
        if at < len(far) - 1:
            mine_a, mine_b = merge([job_a, job_b])
            if at == 0:
                mine_b, before = lax.optimization_barrier((mine_b, before))
        else:
            (mine_a,), (mine_b,) = merge([job_a]), merge([job_b])
        other_a = swapped(mine_a, (far + [near])[at + 1])
        other_b = swapped(mine_b, far[at])
        if at < len(far) - 1:
            other_a, other_b = lax.optimization_barrier((other_a, other_b))
    (mine_b,) = merge([job(*steps_b[-1], mine_b, other_b)])
    other_a, mine_b = lax.optimization_barrier((other_a, mine_b))
    other_b = swapped(mine_b, near)
    twin_a, twin_b = swapped(mine_a, 1), swapped(mine_b, 1)

    bands = (before, span_k, span_v)
    shared = (peers - 1 - near, near, per_device, blocks, queries)
    lists = (mine_a, other_a, twin_a, swapped(other_a, 1))
    state = attend_stage(*shared, lists, offsets=offsets, bands=bands)
    state, late = lax.optimization_barrier((state, other_b))
    lists = (mine_b, late, twin_b, swapped(late, 1))
    fast = attend_stage(*shared, lists, state=state)

    def again(carry):
        return 0, general(queries, bands, cache_k, cache_v, blocks, offsets, bits)

    return lax.while_loop(lambda carry: carry[0] > 0, again, (short, fast))[1]


def solution(mesh):
    rows = P(("groups", "ctx"), None)
    heads = P("groups", None)
    return jax.shard_map(
        shards,
        mesh=mesh,
        in_specs=(rows, rows, rows, rows, rows, heads, heads),
        out_specs=rows,
        check_vma=False,
    )
```

```python
import functools
import math

import jax
import jax.numpy as jnp
from jax import lax
from jax.experimental import pallas as pl
from jax.experimental.pallas import tpu as pltpu
from jax.sharding import PartitionSpec as P

KVH = 4
GROUP = 8
HD = 128
QDEV = 128
VBLOCK = 64
NV = 16
NS = 64
SMAX = 128
ENTRIES = KVH * NV
FACTOR = math.log2(math.e) / math.sqrt(HD)
LOW = -1e38

ANY = pl.BlockSpec(memory_space=pl.ANY)
SMEM = pl.BlockSpec(memory_space=pltpu.SMEM)


def band_mask(offsets, head, first):
    columns = lax.broadcasted_iota(jnp.int32, (8, SMAX + QDEV), 1)
    distance = SMAX - columns
    row = jnp.zeros((8, SMAX + QDEV), jnp.int32)
    for at in range(NS):
        row = jnp.where(distance == offsets[head, at], 1, row)
    rows = jnp.concatenate([row] * (QDEV // 8), axis=0)
    rolled = pltpu.roll(rows, 0, 1, stride=1, stride_axis=0)
    keys = lax.broadcasted_iota(jnp.int32, (QDEV, SMAX + QDEV), 1)
    return (rolled > 0) & (keys >= jnp.where(first, SMAX, 0))


def attend_rows(rows, keys, values_ones, mask, floor=None):
    scores = lax.dot_general(
        rows, keys, (((1,), (1,)), ((), ())), preferred_element_type=jnp.float32
    )
    if mask is not None:
        wide = scores.shape[1] - mask.shape[1]
        reps = rows.shape[0] // QDEV
        tiled = jnp.concatenate([mask] * reps, axis=0)
        band = jnp.where(tiled, scores[:, wide:], LOW)
        scores = jnp.concatenate([scores[:, :wide], band], axis=1)
    largest = jnp.max(scores, axis=1, keepdims=True) * FACTOR
    if floor is not None:
        largest = jnp.maximum(jnp.broadcast_to(largest, floor.shape), floor)
        above = jnp.concatenate([largest] * (scores.shape[1] // HD), axis=1)
    else:
        above = largest
    weights = jnp.exp2(scores * FACTOR - above).astype(jnp.bfloat16)
    mixed = jnp.dot(weights, values_ones, preferred_element_type=jnp.float32)
    return largest, mixed


def dense_kernel(
    offsets, queries, keys, values, before_k, own_k, before_v, own_v, out, kbuf, vbuf
):
    head = pl.program_id(0)
    first = lax.axis_index("ctx") == 0
    wide = NV * VBLOCK
    kbuf[:wide] = keys[0]
    kbuf[wide : wide + SMAX] = before_k[...]
    kbuf[wide + SMAX :] = own_k[...]
    vbuf[:wide, :HD] = values[0]
    vbuf[wide : wide + SMAX, :HD] = before_v[...]
    vbuf[wide + SMAX :, :HD] = own_v[...]
    vbuf[:, HD:] = jnp.ones((wide + SMAX + QDEV, HD), jnp.bfloat16)
    mask = band_mask(offsets, head, first)
    for at in range(0, GROUP, 2):
        rows = jnp.concatenate(
            [queries[:, (at + i) * HD : (at + i + 1) * HD] for i in range(2)], axis=0
        )
        _, mixed = attend_rows(rows, kbuf[...], vbuf[...], mask)
        result = (mixed[:, :HD] / mixed[:, HD:]).astype(jnp.bfloat16)
        for i in range(2):
            out[:, (at + i) * HD : (at + i + 1) * HD] = result[i * QDEV : (i + 1) * QDEV]


def head_block(rows):
    return pl.BlockSpec((rows, HD), lambda head: (0, head))


def attend_dense(offsets, queries, keys, values, bands):
    wide = NV * VBLOCK
    return pl.pallas_call(
        dense_kernel,
        grid=(KVH,),
        out_shape=jax.ShapeDtypeStruct(queries.shape, jnp.bfloat16),
        in_specs=[
            SMEM,
            pl.BlockSpec((QDEV, GROUP * HD), lambda head: (0, head)),
            pl.BlockSpec((1, wide, HD), lambda head: (head, 0, 0)),
            pl.BlockSpec((1, wide, HD), lambda head: (head, 0, 0)),
        ]
        + [head_block(QDEV)] * 4,
        out_specs=pl.BlockSpec((QDEV, GROUP * HD), lambda head: (0, head)),
        scratch_shapes=[
            pltpu.VMEM((wide + SMAX + QDEV, HD), jnp.bfloat16),
            pltpu.VMEM((wide + SMAX + QDEV, 2 * HD), jnp.bfloat16),
        ],
        compiler_params=pltpu.CompilerParams(vmem_limit_bytes=48 * 2**20),
        name="attend_dense",
    )(offsets, queries, keys, values, *bands)


def owned_kernel(per_device, blocks, cache_k, cache_v, out_k, out_v, sems):
    me = lax.axis_index("ctx")
    out_k[...] = jnp.zeros_like(out_k)
    out_v[...] = jnp.zeros_like(out_v)

    def copies(entry):
        head, at = entry // NV, entry % NV
        block = blocks[head, at]
        local = block % per_device
        rows = pl.ds(pl.multiple_of(local * VBLOCK, VBLOCK), VBLOCK)
        columns = pl.ds(pl.multiple_of(head * HD, HD), HD)
        pairs = ((cache_k, out_k, 0), (cache_v, out_v, 1))
        return block // per_device == me, [
            pltpu.make_async_copy(source.at[rows, columns], target.at[entry], sems.at[entry, i])
            for source, target, i in pairs
        ]

    def start(entry, carry):
        mine, both = copies(entry)

        @pl.when(mine)
        def _():
            for copy in both:
                copy.start()

        return carry

    def wait(entry, carry):
        mine, both = copies(entry)

        @pl.when(mine)
        def _():
            for copy in both:
                copy.wait()

        return carry

    lax.fori_loop(0, ENTRIES, start, 0)
    lax.fori_loop(0, ENTRIES, wait, 0)


def owned_blocks(blocks, cache_k, cache_v):
    shape = jax.ShapeDtypeStruct((ENTRIES, VBLOCK, HD), jnp.bfloat16)
    whole = pl.BlockSpec(memory_space=pltpu.VMEM)
    return pl.pallas_call(
        functools.partial(owned_kernel, cache_k.shape[0] // VBLOCK),
        out_shape=(shape, shape),
        in_specs=[SMEM, ANY, ANY],
        out_specs=(whole, whole),
        scratch_shapes=[pltpu.SemaphoreType.DMA((ENTRIES, 2))],
        compiler_params=pltpu.CompilerParams(vmem_limit_bytes=16 * 2**20),
        name="owned_blocks",
    )(blocks, cache_k, cache_v)


STAGES = 2
TILE = 2
OUT_SPACE = pltpu.HBM
VMEM = 24
COST = 2**20
ROWS = VBLOCK // STAGES
WHOLE = pl.BlockSpec(memory_space=pltpu.VMEM)


def room(share):
    mean = ENTRIES * share
    wide = mean + 3.0 * math.sqrt(mean * (1.0 - share)) + 1.5
    return min(ENTRIES + 1, math.ceil(wide))


def owner_of(block, per_device):
    if per_device & (per_device - 1) == 0:
        return lax.shift_right_logical(block, per_device.bit_length() - 1)
    return lax.div(block, per_device)


def pack_kernel(per_device, limit, blocks, cache_k, cache_v, kept, sent, sems):
    me = lax.axis_index("ctx")
    even = lax.rem(me, 2) == 0
    count = jnp.int32(0)
    for entry in range(ENTRIES):
        head = entry // NV
        block = blocks[head, entry % NV]
        owner = owner_of(block, per_device)
        mine = owner == me
        local = block - owner * per_device

        def start(pair, head=head, local=local, count=count):
            rows = pl.ds(pl.multiple_of(local * VBLOCK, VBLOCK), VBLOCK)
            for i, target in enumerate((kept, sent)):
                source = pair[i].at[rows, pl.ds(head * HD, HD)]
                pltpu.make_async_copy(source, target.at[count], sems.at[count, i]).start()

        @pl.when(mine & (count < limit))
        def _(start=start):
            @pl.when(even)
            def _():
                start((cache_k, cache_v))

            @pl.when(jnp.logical_not(even))
            def _():
                start((cache_v, cache_k))

        count += mine.astype(jnp.int32)

    for at in range(limit):

        @pl.when(at < count)
        def _(at=at):
            for i, target in enumerate((kept, sent)):
                source = cache_k.at[pl.ds(0, VBLOCK), pl.ds(0, HD)]
                pltpu.make_async_copy(source, target.at[at], sems.at[at, i]).wait()


def pack(blocks, cache_k, cache_v, limit):
    shape = jax.ShapeDtypeStruct((limit, VBLOCK, HD), jnp.bfloat16)
    return pl.pallas_call(
        functools.partial(pack_kernel, cache_k.shape[0] // VBLOCK, limit),
        out_shape=(shape, shape),
        in_specs=[SMEM, ANY, ANY],
        out_specs=(WHOLE, WHOLE),
        scratch_shapes=[pltpu.SemaphoreType.DMA((limit, 2))],
        compiler_params=pltpu.CompilerParams(vmem_limit_bytes=16 * 2**20),
        name="pack",
    )(blocks, cache_k, cache_v)


def walk(blocks, per_device, known, bit, limits, act):
    me = lax.axis_index("ctx")
    table = blocks[...]
    at_mine = at_other = jnp.int32(0)
    for entry in range(ENTRIES):
        away = (owner_of(table[entry // NV, entry % NV], per_device) ^ me) & ~known
        mine, other = away == 0, away == bit
        tops = jnp.minimum(at_mine, limits[0] - 1), jnp.minimum(at_other, limits[1] - 1)
        act(entry, *tops, at_mine + at_other, other)
        at_mine += mine.astype(jnp.int32)
        at_other += other.astype(jnp.int32)


def merge_kernel(per_device, jobs, blocks, *refs):
    refs = list(refs)
    me = lax.axis_index("ctx")
    sources = [(refs.pop(0), refs.pop(0)) for _ in jobs]
    for (known, bit, halved, parts), (mine, other) in zip(jobs, sources):
        outs = [refs.pop(0) for _ in range(parts)]
        size, rows = outs[0].shape[:2]
        first = pl.multiple_of(jnp.where((me & halved) == 0, 0, rows), rows) if halved else 0

        def act(
            entry, at_mine, at_other, place, theirs, mine=mine, other=other, outs=outs, first=first
        ):
            place = jnp.minimum(place, outs[0].shape[0] - 1)
            for at, out in enumerate(outs):
                span = pl.ds(first + at * out.shape[1], out.shape[1])
                out[place] = jnp.where(theirs, other[at_other, span], mine[at_mine, span])

        walk(blocks, per_device, known, bit, (mine.shape[0], other.shape[0]), act)


def merged(blocks, per_device, jobs):
    shapes, lists = [], []
    for _, _, halved, parts, mine, other, size in jobs:
        rows = mine.shape[1] // (2 if halved else parts)
        shapes += [jax.ShapeDtypeStruct((size, rows, HD), jnp.bfloat16)] * parts
        lists += [mine, other]
    return pl.pallas_call(
        functools.partial(merge_kernel, per_device, [job[:4] for job in jobs]),
        out_shape=tuple(shapes),
        in_specs=[WHOLE] * (1 + len(lists)),
        out_specs=(WHOLE,) * len(shapes),
        compiler_params=pltpu.CompilerParams(vmem_limit_bytes=16 * 2**20),
        name="merge",
    )(blocks, *lists)


def stage_kernel(per_device, known, bit, banded, last, *refs):
    refs = list(refs)
    blocks = refs.pop(0)
    offsets = refs.pop(0) if banded else None
    queries, mine, other, mine_twin, other_twin = refs[:5]
    refs = refs[5:]
    if banded:
        before, own_k, own_v = refs[:3]
        refs = refs[3:]
    else:
        largest_in, total_in, mixed_in = refs[:3]
        refs = refs[3:]
    if last:
        out, kbuf, vbuf, held, sems = refs
    else:
        largest_out, total_out, mixed_out, kbuf, vbuf = refs
    me = lax.axis_index("ctx")
    even = lax.rem(me, 2) == 0
    wide = NV * ROWS

    def act(entry, at_mine, at_other, place, theirs):
        tile = jnp.where(theirs, other[at_other], mine[at_mine])
        twin = jnp.where(theirs, other_twin[at_other], mine_twin[at_mine])
        rows = pl.ds(entry % NV * ROWS, ROWS)
        kbuf[entry // NV, rows] = jnp.where(even, tile, twin)
        vbuf[entry // NV, rows, :HD] = jnp.where(even, twin, tile)

    if not last:
        walk(blocks, per_device, known, bit, (mine.shape[0], other.shape[0]), act)
    else:
        half = wide // 2
        for head in range(KVH):
            span = slice(head * NV, (head + 1) * NV)
            for at, (own, twin) in enumerate(((mine, mine_twin), (other, other_twin))):
                tile, pair = own[span].reshape(half, HD), twin[span].reshape(half, HD)
                rows = slice(at * half, (at + 1) * half)
                kbuf[head, rows] = jnp.where(even, tile, pair)
                vbuf[head, rows, :HD] = jnp.where(even, pair, tile)
    copies = []
    for head in range(KVH):
        columns = slice(head * HD, (head + 1) * HD)
        vbuf[head, :, HD:] = jnp.ones((vbuf.shape[1], HD), jnp.bfloat16)
        mask = None
        if banded:
            values = slice((KVH + head) * HD, (KVH + head + 1) * HD)
            kbuf[head, wide : wide + SMAX] = before[:, columns]
            kbuf[head, wide + SMAX :] = own_k[:, columns]
            vbuf[head, wide : wide + SMAX, :HD] = before[:, values]
            vbuf[head, wide + SMAX :, :HD] = own_v[:, columns]
            mask = band_mask(offsets[...], head, me == 0)
        for at in range(0, GROUP, TILE):
            rows = jnp.concatenate(
                [
                    queries[:, (head * GROUP + at + i) * HD : (head * GROUP + at + i + 1) * HD]
                    for i in range(TILE)
                ],
                axis=0,
            )
            start = (head * GROUP + at) * QDEV
            tile = slice(start, start + TILE * QDEV)
            floor = None if banded else largest_in[tile]
            largest, mixed = attend_rows(rows, kbuf[head], vbuf[head], mask, floor)
            mixed, total = mixed[:, :HD], mixed[:, HD:]
            if not banded:
                then = jnp.exp2(floor - largest)
                mixed = mixed + mixed_in[tile] * then
                total = total + total_in[tile] * then
            if last:
                result = (mixed / total).astype(jnp.bfloat16)
                for i in range(TILE):
                    held[head, :, (at + i) * HD : (at + i + 1) * HD] = result[
                        i * QDEV : (i + 1) * QDEV
                    ]
            else:
                largest_out[tile] = jnp.broadcast_to(largest, mixed.shape)
                total_out[tile] = total
                mixed_out[tile] = mixed
        if last:
            span = pl.ds(head * GROUP * HD, GROUP * HD)
            copies.append(pltpu.make_async_copy(held.at[head], out.at[:, span], sems.at[head]))
            copies[-1].start()
    for copy in copies:
        copy.wait()


def attend_stage(known, bit, per_device, blocks, queries, lists, offsets=None, bands=None, state=None):
    banded, last = bands is not None, state is not None
    tall = KVH * GROUP * QDEV
    args = [blocks] + [offsets] * banded + [queries, *lists]
    args += list(bands if banded else state)
    specs = [WHOLE] * len(args)
    keys = NV * ROWS + (SMAX + QDEV) * banded
    scratch = [
        pltpu.VMEM((KVH, keys, HD), jnp.bfloat16),
        pltpu.VMEM((KVH, keys, 2 * HD), jnp.bfloat16),
    ]
    if last:
        out_shape = jax.ShapeDtypeStruct(queries.shape, jnp.bfloat16)
        out_specs = pl.BlockSpec(memory_space=OUT_SPACE)
        scratch += [
            pltpu.VMEM((KVH, QDEV, GROUP * HD), jnp.bfloat16),
            pltpu.SemaphoreType.DMA((KVH,)),
        ]
    else:
        out_shape = (jax.ShapeDtypeStruct((tall, HD), jnp.float32),) * 3
        out_specs = (WHOLE,) * 3
    return pl.pallas_call(
        functools.partial(stage_kernel, per_device, known, bit, banded, last),
        out_shape=out_shape,
        in_specs=specs,
        out_specs=out_specs,
        scratch_shapes=scratch,
        compiler_params=pltpu.CompilerParams(vmem_limit_bytes=VMEM * 2**20),
        cost_estimate=pl.CostEstimate(flops=COST, bytes_accessed=COST, transcendentals=0),
        name="attend_last" if last else "attend_first",
    )(*args)


def permuted(array, pairs):
    return lax.ppermute(array, "ctx", pairs)


def swapped(array, bit):
    return permuted(array, [(i, i ^ bit) for i in range(lax.axis_size("ctx"))])


def fits(blocks, per_device, peers, masks):
    most = [room((1 << mask.bit_count()) / peers) - (mask > 0) for mask in masks]
    owners = (blocks // per_device).reshape(1, 1, ENTRIES)
    ids = jnp.arange(peers, dtype=jnp.int32)[None, :, None]
    away = (owners ^ ids) & ~jnp.array(masks, jnp.int32)[:, None, None]
    counts = jnp.sum((away == 0).astype(jnp.int32), axis=2)
    return jnp.all(counts <= jnp.array(most, jnp.int32)[:, None])


def general(queries, bands, cache_k, cache_v, blocks, offsets, bits):
    keys, values = owned_blocks(blocks, cache_k, cache_v)
    for bit in bits:
        keys, values = keys + swapped(keys, bit), values + swapped(values, bit)
    keys = keys.reshape(KVH, NV * VBLOCK, HD)
    values = values.reshape(KVH, NV * VBLOCK, HD)
    before, own_k, own_v = bands
    wide = KVH * HD
    bands = (before[:, :wide], own_k, before[:, wide:], own_v)
    return attend_dense(offsets, queries, keys, values, bands)


def shards(queries, span_k, span_v, cache_k, cache_v, blocks, offsets):
    peers = lax.axis_size("ctx")
    per_device = cache_k.shape[0] // VBLOCK
    ahead = [(i, i + 1) for i in range(peers - 1)]
    near = 2
    far = [1 << at for at in range(peers.bit_length() - 2, 1, -1)]
    bits = [1] + far + [near]
    masks_a = [sum(bits[:at]) for at in range(len(bits))]
    masks_b = [1 + near + sum(far[:at]) for at in range(len(far))]

    def job(known, bit, mine, other, parts=1, halved=0):
        size = room((1 << (known | bit).bit_count()) / peers)
        if known + bit == peers - 1:
            size = ENTRIES
        return known, bit, halved, parts, mine, other, size

    merge = functools.partial(merged, blocks, per_device)
    kept, sent = pack(blocks, cache_k, cache_v, room(1 / peers))
    mine_a, mine_b = merge([job(0, 1, kept, swapped(sent, 1), parts=STAGES)])
    spans, mine_b = lax.optimization_barrier((jnp.concatenate([span_k, span_v], axis=1), mine_b))
    before = permuted(spans, ahead)
    short = jnp.logical_not(fits(blocks, per_device, peers, masks_a + masks_b)).astype(jnp.int32)

    steps_a = list(zip(masks_a[1:], far))
    steps_b = list(zip([1] + masks_b, [near] + far))
    other_a = swapped(mine_a, far[0])
    other_b = swapped(mine_b, near)
    other_a, short = lax.optimization_barrier((other_a, short))
    for at in range(len(far)):
        job_a = job(*steps_a[at], mine_a, other_a)
        job_b = job(*steps_b[at], mine_b, other_b, halved=near if at == 0 else 0)
        if at < len(far) - 1:
            mine_a, mine_b = merge([job_a, job_b])
        else:
            (mine_a,), (mine_b,) = merge([job_a]), merge([job_b])
        other_a = swapped(mine_a, (far + [near])[at + 1])
        other_b = swapped(mine_b, far[at])
        if at < len(far) - 1:
            other_a, other_b, before = lax.optimization_barrier((other_a, other_b, before))
    (mine_b,) = merge([job(*steps_b[-1], mine_b, other_b)])
    other_a, mine_b = lax.optimization_barrier((other_a, mine_b))
    other_b = swapped(mine_b, near)
    twin_a, twin_b = swapped(mine_a, 1), swapped(mine_b, 1)

    bands = (before, span_k, span_v)
    shared = (peers - 1 - near, near, per_device, blocks, queries)
    lists = (mine_a, other_a, twin_a, swapped(other_a, 1))
    state = attend_stage(*shared, lists, offsets=offsets, bands=bands)
    state, late = lax.optimization_barrier((state, other_b))
    lists = (mine_b, late, twin_b, swapped(late, 1))
    fast = attend_stage(*shared, lists, state=state)

    def again(carry):
        return 0, general(queries, bands, cache_k, cache_v, blocks, offsets, bits)

    return lax.while_loop(lambda carry: carry[0] > 0, again, (short, fast))[1]


def solution(mesh):
    rows = P(("groups", "ctx"), None)
    heads = P("groups", None)
    return jax.shard_map(
        shards,
        mesh=mesh,
        in_specs=(rows, rows, rows, rows, rows, heads, heads),
        out_specs=rows,
        check_vma=False,
    )
```

```python
import functools
import math

import jax
import jax.numpy as jnp
from jax import lax
from jax.experimental import pallas as pl
from jax.experimental.pallas import tpu as pltpu
from jax.sharding import PartitionSpec as P

KVH = 4
GROUP = 8
HD = 128
QDEV = 128
VBLOCK = 64
NV = 16
NS = 64
SMAX = 128
ENTRIES = KVH * NV
FACTOR = math.log2(math.e) / math.sqrt(HD)
LOW = -1e38

ANY = pl.BlockSpec(memory_space=pl.ANY)
SMEM = pl.BlockSpec(memory_space=pltpu.SMEM)


def band_mask(offsets, head, first):
    columns = lax.broadcasted_iota(jnp.int32, (8, SMAX + QDEV), 1)
    distance = SMAX - columns
    row = jnp.zeros((8, SMAX + QDEV), jnp.int32)
    for at in range(NS):
        row = jnp.where(distance == offsets[head, at], 1, row)
    rows = jnp.concatenate([row] * (QDEV // 8), axis=0)
    rolled = pltpu.roll(rows, 0, 1, stride=1, stride_axis=0)
    keys = lax.broadcasted_iota(jnp.int32, (QDEV, SMAX + QDEV), 1)
    return (rolled > 0) & (keys >= jnp.where(first, SMAX, 0))


def attend_rows(rows, keys, values_ones, mask, floor=None):
    scores = lax.dot_general(
        rows, keys, (((1,), (1,)), ((), ())), preferred_element_type=jnp.float32
    )
    if mask is not None:
        wide = scores.shape[1] - mask.shape[1]
        reps = rows.shape[0] // QDEV
        tiled = jnp.concatenate([mask] * reps, axis=0)
        band = jnp.where(tiled, scores[:, wide:], LOW)
        scores = jnp.concatenate([scores[:, :wide], band], axis=1)
    largest = jnp.max(scores, axis=1, keepdims=True) * FACTOR
    if floor is not None:
        largest = jnp.maximum(jnp.broadcast_to(largest, floor.shape), floor)
        above = jnp.concatenate([largest] * (scores.shape[1] // HD), axis=1)
    else:
        above = largest
    weights = jnp.exp2(scores * FACTOR - above).astype(jnp.bfloat16)
    mixed = jnp.dot(weights, values_ones, preferred_element_type=jnp.float32)
    return largest, mixed


def dense_kernel(
    offsets, queries, keys, values, before_k, own_k, before_v, own_v, out, kbuf, vbuf
):
    head = pl.program_id(0)
    first = lax.axis_index("ctx") == 0
    wide = NV * VBLOCK
    kbuf[:wide] = keys[0]
    kbuf[wide : wide + SMAX] = before_k[...]
    kbuf[wide + SMAX :] = own_k[...]
    vbuf[:wide, :HD] = values[0]
    vbuf[wide : wide + SMAX, :HD] = before_v[...]
    vbuf[wide + SMAX :, :HD] = own_v[...]
    vbuf[:, HD:] = jnp.ones((wide + SMAX + QDEV, HD), jnp.bfloat16)
    mask = band_mask(offsets, head, first)
    for at in range(0, GROUP, 2):
        rows = jnp.concatenate(
            [queries[:, (at + i) * HD : (at + i + 1) * HD] for i in range(2)], axis=0
        )
        _, mixed = attend_rows(rows, kbuf[...], vbuf[...], mask)
        result = (mixed[:, :HD] / mixed[:, HD:]).astype(jnp.bfloat16)
        for i in range(2):
            out[:, (at + i) * HD : (at + i + 1) * HD] = result[i * QDEV : (i + 1) * QDEV]


def head_block(rows):
    return pl.BlockSpec((rows, HD), lambda head: (0, head))


def attend_dense(offsets, queries, keys, values, bands):
    wide = NV * VBLOCK
    return pl.pallas_call(
        dense_kernel,
        grid=(KVH,),
        out_shape=jax.ShapeDtypeStruct(queries.shape, jnp.bfloat16),
        in_specs=[
            SMEM,
            pl.BlockSpec((QDEV, GROUP * HD), lambda head: (0, head)),
            pl.BlockSpec((1, wide, HD), lambda head: (head, 0, 0)),
            pl.BlockSpec((1, wide, HD), lambda head: (head, 0, 0)),
        ]
        + [head_block(QDEV)] * 4,
        out_specs=pl.BlockSpec((QDEV, GROUP * HD), lambda head: (0, head)),
        scratch_shapes=[
            pltpu.VMEM((wide + SMAX + QDEV, HD), jnp.bfloat16),
            pltpu.VMEM((wide + SMAX + QDEV, 2 * HD), jnp.bfloat16),
        ],
        compiler_params=pltpu.CompilerParams(vmem_limit_bytes=48 * 2**20),
        name="attend_dense",
    )(offsets, queries, keys, values, *bands)


def owned_kernel(per_device, blocks, cache_k, cache_v, out_k, out_v, sems):
    me = lax.axis_index("ctx")
    out_k[...] = jnp.zeros_like(out_k)
    out_v[...] = jnp.zeros_like(out_v)

    def copies(entry):
        head, at = entry // NV, entry % NV
        block = blocks[head, at]
        local = block % per_device
        rows = pl.ds(pl.multiple_of(local * VBLOCK, VBLOCK), VBLOCK)
        columns = pl.ds(pl.multiple_of(head * HD, HD), HD)
        pairs = ((cache_k, out_k, 0), (cache_v, out_v, 1))
        return block // per_device == me, [
            pltpu.make_async_copy(source.at[rows, columns], target.at[entry], sems.at[entry, i])
            for source, target, i in pairs
        ]

    def start(entry, carry):
        mine, both = copies(entry)

        @pl.when(mine)
        def _():
            for copy in both:
                copy.start()

        return carry

    def wait(entry, carry):
        mine, both = copies(entry)

        @pl.when(mine)
        def _():
            for copy in both:
                copy.wait()

        return carry

    lax.fori_loop(0, ENTRIES, start, 0)
    lax.fori_loop(0, ENTRIES, wait, 0)


def owned_blocks(blocks, cache_k, cache_v):
    shape = jax.ShapeDtypeStruct((ENTRIES, VBLOCK, HD), jnp.bfloat16)
    whole = pl.BlockSpec(memory_space=pltpu.VMEM)
    return pl.pallas_call(
        functools.partial(owned_kernel, cache_k.shape[0] // VBLOCK),
        out_shape=(shape, shape),
        in_specs=[SMEM, ANY, ANY],
        out_specs=(whole, whole),
        scratch_shapes=[pltpu.SemaphoreType.DMA((ENTRIES, 2))],
        compiler_params=pltpu.CompilerParams(vmem_limit_bytes=16 * 2**20),
        name="owned_blocks",
    )(blocks, cache_k, cache_v)


STAGES = 2
TILE = 2
OUT_SPACE = pltpu.HBM
VMEM = 24
COST = 2**20
ROWS = VBLOCK // STAGES
WHOLE = pl.BlockSpec(memory_space=pltpu.VMEM)


def room(share):
    mean = ENTRIES * share
    wide = mean + 3.2 * math.sqrt(mean * (1.0 - share)) + 2.0
    return min(ENTRIES + 1, math.ceil(wide))


def owner_of(block, per_device):
    if per_device & (per_device - 1) == 0:
        return lax.shift_right_logical(block, per_device.bit_length() - 1)
    return lax.div(block, per_device)


def pack_kernel(per_device, limit, blocks, cache_k, cache_v, kept, sent, sems):
    me = lax.axis_index("ctx")
    even = lax.rem(me, 2) == 0
    count = jnp.int32(0)
    for entry in range(ENTRIES):
        head = entry // NV
        block = blocks[head, entry % NV]
        owner = owner_of(block, per_device)
        mine = owner == me
        local = block - owner * per_device

        def start(pair, head=head, local=local, count=count):
            rows = pl.ds(pl.multiple_of(local * VBLOCK, VBLOCK), VBLOCK)
            for i, target in enumerate((kept, sent)):
                source = pair[i].at[rows, pl.ds(head * HD, HD)]
                pltpu.make_async_copy(source, target.at[count], sems.at[count, i]).start()

        @pl.when(mine & (count < limit))
        def _(start=start):
            @pl.when(even)
            def _():
                start((cache_k, cache_v))

            @pl.when(jnp.logical_not(even))
            def _():
                start((cache_v, cache_k))

        count += mine.astype(jnp.int32)

    for at in range(limit):

        @pl.when(at < count)
        def _(at=at):
            for i, target in enumerate((kept, sent)):
                source = cache_k.at[pl.ds(0, VBLOCK), pl.ds(0, HD)]
                pltpu.make_async_copy(source, target.at[at], sems.at[at, i]).wait()


def pack(blocks, cache_k, cache_v, limit):
    shape = jax.ShapeDtypeStruct((limit, VBLOCK, HD), jnp.bfloat16)
    return pl.pallas_call(
        functools.partial(pack_kernel, cache_k.shape[0] // VBLOCK, limit),
        out_shape=(shape, shape),
        in_specs=[SMEM, ANY, ANY],
        out_specs=(WHOLE, WHOLE),
        scratch_shapes=[pltpu.SemaphoreType.DMA((limit, 2))],
        compiler_params=pltpu.CompilerParams(vmem_limit_bytes=16 * 2**20),
        name="pack",
    )(blocks, cache_k, cache_v)


def walk(blocks, per_device, known, bit, limits, act):
    me = lax.axis_index("ctx")
    table = blocks[...]
    at_mine = at_other = jnp.int32(0)
    for entry in range(ENTRIES):
        away = (owner_of(table[entry // NV, entry % NV], per_device) ^ me) & ~known
        mine, other = away == 0, away == bit
        tops = jnp.minimum(at_mine, limits[0] - 1), jnp.minimum(at_other, limits[1] - 1)
        act(entry, *tops, at_mine + at_other, other)
        at_mine += mine.astype(jnp.int32)
        at_other += other.astype(jnp.int32)


def merge_kernel(per_device, jobs, blocks, *refs):
    refs = list(refs)
    me = lax.axis_index("ctx")
    sources = [(refs.pop(0), refs.pop(0)) for _ in jobs]
    for (known, bit, halved, parts), (mine, other) in zip(jobs, sources):
        outs = [refs.pop(0) for _ in range(parts)]
        size, rows = outs[0].shape[:2]
        first = pl.multiple_of(jnp.where((me & halved) == 0, 0, rows), rows) if halved else 0

        def act(
            entry, at_mine, at_other, place, theirs, mine=mine, other=other, outs=outs, first=first
        ):
            place = jnp.minimum(place, outs[0].shape[0] - 1)
            for at, out in enumerate(outs):
                span = pl.ds(first + at * out.shape[1], out.shape[1])
                out[place] = jnp.where(theirs, other[at_other, span], mine[at_mine, span])

        walk(blocks, per_device, known, bit, (mine.shape[0], other.shape[0]), act)


def merged(blocks, per_device, jobs):
    shapes, lists = [], []
    for _, _, halved, parts, mine, other, size in jobs:
        rows = mine.shape[1] // (2 if halved else parts)
        shapes += [jax.ShapeDtypeStruct((size, rows, HD), jnp.bfloat16)] * parts
        lists += [mine, other]
    return pl.pallas_call(
        functools.partial(merge_kernel, per_device, [job[:4] for job in jobs]),
        out_shape=tuple(shapes),
        in_specs=[WHOLE] * (1 + len(lists)),
        out_specs=(WHOLE,) * len(shapes),
        compiler_params=pltpu.CompilerParams(vmem_limit_bytes=16 * 2**20),
        name="merge",
    )(blocks, *lists)


def stage_kernel(per_device, known, bit, banded, last, *refs):
    refs = list(refs)
    blocks = refs.pop(0)
    offsets = refs.pop(0) if banded else None
    queries, mine, other, mine_twin, other_twin = refs[:5]
    refs = refs[5:]
    if banded:
        before, own_k, own_v = refs[:3]
        refs = refs[3:]
    else:
        largest_in, total_in, mixed_in = refs[:3]
        refs = refs[3:]
    if last:
        out, kbuf, vbuf, held, sems = refs
    else:
        largest_out, total_out, mixed_out, kbuf, vbuf = refs
    me = lax.axis_index("ctx")
    even = lax.rem(me, 2) == 0
    wide = NV * ROWS

    def act(entry, at_mine, at_other, place, theirs):
        tile = jnp.where(theirs, other[at_other], mine[at_mine])
        twin = jnp.where(theirs, other_twin[at_other], mine_twin[at_mine])
        rows = pl.ds(entry % NV * ROWS, ROWS)
        kbuf[entry // NV, rows] = jnp.where(even, tile, twin)
        vbuf[entry // NV, rows, :HD] = jnp.where(even, twin, tile)

    if not last:
        walk(blocks, per_device, known, bit, (mine.shape[0], other.shape[0]), act)
    else:
        half = wide // 2
        for head in range(KVH):
            span = slice(head * NV, (head + 1) * NV)
            for at, (own, twin) in enumerate(((mine, mine_twin), (other, other_twin))):
                tile, pair = own[span].reshape(half, HD), twin[span].reshape(half, HD)
                rows = slice(at * half, (at + 1) * half)
                kbuf[head, rows] = jnp.where(even, tile, pair)
                vbuf[head, rows, :HD] = jnp.where(even, pair, tile)
    copies = []
    for head in range(KVH):
        columns = slice(head * HD, (head + 1) * HD)
        vbuf[head, :, HD:] = jnp.ones((vbuf.shape[1], HD), jnp.bfloat16)
        mask = None
        if banded:
            values = slice((KVH + head) * HD, (KVH + head + 1) * HD)
            kbuf[head, wide : wide + SMAX] = before[:, columns]
            kbuf[head, wide + SMAX :] = own_k[:, columns]
            vbuf[head, wide : wide + SMAX, :HD] = before[:, values]
            vbuf[head, wide + SMAX :, :HD] = own_v[:, columns]
            mask = band_mask(offsets[...], head, me == 0)
        for at in range(0, GROUP, TILE):
            rows = jnp.concatenate(
                [
                    queries[:, (head * GROUP + at + i) * HD : (head * GROUP + at + i + 1) * HD]
                    for i in range(TILE)
                ],
                axis=0,
            )
            start = (head * GROUP + at) * QDEV
            tile = slice(start, start + TILE * QDEV)
            floor = None if banded else largest_in[tile]
            largest, mixed = attend_rows(rows, kbuf[head], vbuf[head], mask, floor)
            mixed, total = mixed[:, :HD], mixed[:, HD:]
            if not banded:
                then = jnp.exp2(floor - largest)
                mixed = mixed + mixed_in[tile] * then
                total = total + total_in[tile] * then
            if last:
                result = (mixed / total).astype(jnp.bfloat16)
                for i in range(TILE):
                    held[head, :, (at + i) * HD : (at + i + 1) * HD] = result[
                        i * QDEV : (i + 1) * QDEV
                    ]
            else:
                largest_out[tile] = jnp.broadcast_to(largest, mixed.shape)
                total_out[tile] = total
                mixed_out[tile] = mixed
        if last:
            span = pl.ds(head * GROUP * HD, GROUP * HD)
            copies.append(pltpu.make_async_copy(held.at[head], out.at[:, span], sems.at[head]))
            copies[-1].start()
    for copy in copies:
        copy.wait()


def attend_stage(known, bit, per_device, blocks, queries, lists, offsets=None, bands=None, state=None):
    banded, last = bands is not None, state is not None
    tall = KVH * GROUP * QDEV
    args = [blocks] + [offsets] * banded + [queries, *lists]
    args += list(bands if banded else state)
    specs = [WHOLE] * len(args)
    keys = NV * ROWS + (SMAX + QDEV) * banded
    scratch = [
        pltpu.VMEM((KVH, keys, HD), jnp.bfloat16),
        pltpu.VMEM((KVH, keys, 2 * HD), jnp.bfloat16),
    ]
    if last:
        out_shape = jax.ShapeDtypeStruct(queries.shape, jnp.bfloat16)
        out_specs = pl.BlockSpec(memory_space=OUT_SPACE)
        scratch += [
            pltpu.VMEM((KVH, QDEV, GROUP * HD), jnp.bfloat16),
            pltpu.SemaphoreType.DMA((KVH,)),
        ]
    else:
        out_shape = (jax.ShapeDtypeStruct((tall, HD), jnp.float32),) * 3
        out_specs = (WHOLE,) * 3
    return pl.pallas_call(
        functools.partial(stage_kernel, per_device, known, bit, banded, last),
        out_shape=out_shape,
        in_specs=specs,
        out_specs=out_specs,
        scratch_shapes=scratch,
        compiler_params=pltpu.CompilerParams(vmem_limit_bytes=VMEM * 2**20),
        cost_estimate=pl.CostEstimate(flops=COST, bytes_accessed=COST, transcendentals=0),
        name="attend_last" if last else "attend_first",
    )(*args)


def permuted(array, pairs):
    return lax.ppermute(array, "ctx", pairs)


def swapped(array, bit):
    return permuted(array, [(i, i ^ bit) for i in range(lax.axis_size("ctx"))])


def fits(blocks, per_device, peers, masks):
    most = [room((1 << mask.bit_count()) / peers) - (mask > 0) for mask in masks]
    owners = (blocks // per_device).reshape(1, 1, ENTRIES)
    ids = jnp.arange(peers, dtype=jnp.int32)[None, :, None]
    away = (owners ^ ids) & ~jnp.array(masks, jnp.int32)[:, None, None]
    counts = jnp.sum((away == 0).astype(jnp.int32), axis=2)
    return jnp.all(counts <= jnp.array(most, jnp.int32)[:, None])


def general(queries, bands, cache_k, cache_v, blocks, offsets, bits):
    keys, values = owned_blocks(blocks, cache_k, cache_v)
    even = lax.axis_index("ctx") % 2 == 0
    mine = jnp.where(even, keys, values) + swapped(jnp.where(even, values, keys), 1)
    for bit in bits[1:]:
        mine = mine + swapped(mine, bit)
    twin = swapped(mine, 1)
    keys, values = jnp.where(even, mine, twin), jnp.where(even, twin, mine)
    keys = keys.reshape(KVH, NV * VBLOCK, HD)
    values = values.reshape(KVH, NV * VBLOCK, HD)
    before, own_k, own_v = bands
    wide = KVH * HD
    bands = (before[:, :wide], own_k, before[:, wide:], own_v)
    return attend_dense(offsets, queries, keys, values, bands)


def shards(queries, span_k, span_v, cache_k, cache_v, blocks, offsets):
    peers = lax.axis_size("ctx")
    per_device = cache_k.shape[0] // VBLOCK
    ahead = [(i, i + 1) for i in range(peers - 1)]
    near = 2
    far = [1 << at for at in range(peers.bit_length() - 2, 1, -1)]
    bits = [1] + far + [near]
    masks_a = [sum(bits[:at]) for at in range(len(bits))]
    masks_b = [1 + near + sum(far[:at]) for at in range(len(far))]

    def job(known, bit, mine, other, parts=1, halved=0):
        size = room((1 << (known | bit).bit_count()) / peers)
        if known + bit == peers - 1:
            size = ENTRIES
        return known, bit, halved, parts, mine, other, size

    merge = functools.partial(merged, blocks, per_device)
    kept, sent = pack(blocks, cache_k, cache_v, room(1 / peers))
    mine_a, mine_b = merge([job(0, 1, kept, swapped(sent, 1), parts=STAGES)])
    spans, mine_b = lax.optimization_barrier((jnp.concatenate([span_k, span_v], axis=1), mine_b))
    before = permuted(spans, ahead)
    short = jnp.logical_not(fits(blocks, per_device, peers, masks_a + masks_b)).astype(jnp.int32)

    steps_a = list(zip(masks_a[1:], far))
    steps_b = list(zip([1] + masks_b, [near] + far))
    other_a = swapped(mine_a, far[0])
    other_b = swapped(mine_b, near)
    other_a, short = lax.optimization_barrier((other_a, short))
    for at in range(len(far)):
        job_a = job(*steps_a[at], mine_a, other_a)
        job_b = job(*steps_b[at], mine_b, other_b, halved=near if at == 0 else 0)
        if at < len(far) - 1:
            mine_a, mine_b = merge([job_a, job_b])
        else:
            (mine_a,), (mine_b,) = merge([job_a]), merge([job_b])
        other_a = swapped(mine_a, (far + [near])[at + 1])
        other_b = swapped(mine_b, far[at])
        if at < len(far) - 1:
            other_a, other_b, before = lax.optimization_barrier((other_a, other_b, before))
    (mine_b,) = merge([job(*steps_b[-1], mine_b, other_b)])
    other_a, mine_b = lax.optimization_barrier((other_a, mine_b))
    other_b = swapped(mine_b, near)
    twin_a, twin_b = swapped(mine_a, 1), swapped(mine_b, 1)

    bands = (before, span_k, span_v)
    shared = (peers - 1 - near, near, per_device, blocks, queries)
    lists = (mine_a, other_a, twin_a, swapped(other_a, 1))
    state = attend_stage(*shared, lists, offsets=offsets, bands=bands)
    state, late = lax.optimization_barrier((state, other_b))
    lists = (mine_b, late, twin_b, swapped(late, 1))
    fast = attend_stage(*shared, lists, state=state)

    def again(carry):
        return 0, general(queries, bands, cache_k, cache_v, blocks, offsets, bits)

    return lax.while_loop(lambda carry: carry[0] > 0, again, (short, fast))[1]


def solution(mesh):
    rows = P(("groups", "ctx"), None)
    heads = P("groups", None)
    return jax.shard_map(
        shards,
        mesh=mesh,
        in_specs=(rows, rows, rows, rows, rows, heads, heads),
        out_specs=rows,
        check_vma=False,
    )
```

```python
import functools
import math

import jax
import jax.numpy as jnp
from jax import lax
from jax.experimental import pallas as pl
from jax.experimental.pallas import tpu as pltpu
from jax.sharding import PartitionSpec as P

KVH = 4
GROUP = 8
HD = 128
QDEV = 128
VBLOCK = 64
NV = 16
NS = 64
SMAX = 128
ENTRIES = KVH * NV
FACTOR = math.log2(math.e) / math.sqrt(HD)
LOW = -1e38

ANY = pl.BlockSpec(memory_space=pl.ANY)
SMEM = pl.BlockSpec(memory_space=pltpu.SMEM)


def band_mask(offsets, head, first):
    columns = lax.broadcasted_iota(jnp.int32, (8, SMAX + QDEV), 1)
    distance = SMAX - columns
    row = jnp.zeros((8, SMAX + QDEV), jnp.int32)
    for at in range(NS):
        row = jnp.where(distance == offsets[head, at], 1, row)
    rows = jnp.concatenate([row] * (QDEV // 8), axis=0)
    rolled = pltpu.roll(rows, 0, 1, stride=1, stride_axis=0)
    keys = lax.broadcasted_iota(jnp.int32, (QDEV, SMAX + QDEV), 1)
    return (rolled > 0) & (keys >= jnp.where(first, SMAX, 0))


def attend_rows(rows, keys, values_ones, mask, floor=None):
    scores = lax.dot_general(
        rows, keys, (((1,), (1,)), ((), ())), preferred_element_type=jnp.float32
    )
    if mask is not None:
        wide = scores.shape[1] - mask.shape[1]
        reps = rows.shape[0] // QDEV
        tiled = jnp.concatenate([mask] * reps, axis=0)
        band = jnp.where(tiled, scores[:, wide:], LOW)
        scores = jnp.concatenate([scores[:, :wide], band], axis=1)
    largest = jnp.max(scores, axis=1, keepdims=True) * FACTOR
    if floor is not None:
        largest = jnp.maximum(jnp.broadcast_to(largest, floor.shape), floor)
        above = jnp.concatenate([largest] * (scores.shape[1] // HD), axis=1)
    else:
        above = largest
    weights = jnp.exp2(scores * FACTOR - above).astype(jnp.bfloat16)
    mixed = jnp.dot(weights, values_ones, preferred_element_type=jnp.float32)
    return largest, mixed


def dense_kernel(
    offsets, queries, keys, values, before_k, own_k, before_v, own_v, out, kbuf, vbuf
):
    head = pl.program_id(0)
    first = lax.axis_index("ctx") == 0
    wide = NV * VBLOCK
    kbuf[:wide] = keys[0]
    kbuf[wide : wide + SMAX] = before_k[...]
    kbuf[wide + SMAX :] = own_k[...]
    vbuf[:wide, :HD] = values[0]
    vbuf[wide : wide + SMAX, :HD] = before_v[...]
    vbuf[wide + SMAX :, :HD] = own_v[...]
    vbuf[:, HD:] = jnp.ones((wide + SMAX + QDEV, HD), jnp.bfloat16)
    mask = band_mask(offsets, head, first)
    for at in range(0, GROUP, 2):
        rows = jnp.concatenate(
            [queries[:, (at + i) * HD : (at + i + 1) * HD] for i in range(2)], axis=0
        )
        _, mixed = attend_rows(rows, kbuf[...], vbuf[...], mask)
        result = (mixed[:, :HD] / mixed[:, HD:]).astype(jnp.bfloat16)
        for i in range(2):
            out[:, (at + i) * HD : (at + i + 1) * HD] = result[i * QDEV : (i + 1) * QDEV]


def head_block(rows):
    return pl.BlockSpec((rows, HD), lambda head: (0, head))


def attend_dense(offsets, queries, keys, values, bands):
    wide = NV * VBLOCK
    return pl.pallas_call(
        dense_kernel,
        grid=(KVH,),
        out_shape=jax.ShapeDtypeStruct(queries.shape, jnp.bfloat16),
        in_specs=[
            SMEM,
            pl.BlockSpec((QDEV, GROUP * HD), lambda head: (0, head)),
            pl.BlockSpec((1, wide, HD), lambda head: (head, 0, 0)),
            pl.BlockSpec((1, wide, HD), lambda head: (head, 0, 0)),
        ]
        + [head_block(QDEV)] * 4,
        out_specs=pl.BlockSpec((QDEV, GROUP * HD), lambda head: (0, head)),
        scratch_shapes=[
            pltpu.VMEM((wide + SMAX + QDEV, HD), jnp.bfloat16),
            pltpu.VMEM((wide + SMAX + QDEV, 2 * HD), jnp.bfloat16),
        ],
        compiler_params=pltpu.CompilerParams(vmem_limit_bytes=48 * 2**20),
        name="attend_dense",
    )(offsets, queries, keys, values, *bands)


def owned_kernel(per_device, blocks, cache_k, cache_v, out_k, out_v, sems):
    me = lax.axis_index("ctx")
    out_k[...] = jnp.zeros_like(out_k)
    out_v[...] = jnp.zeros_like(out_v)

    def copies(entry):
        head, at = entry // NV, entry % NV
        block = blocks[head, at]
        local = block % per_device
        rows = pl.ds(pl.multiple_of(local * VBLOCK, VBLOCK), VBLOCK)
        columns = pl.ds(pl.multiple_of(head * HD, HD), HD)
        pairs = ((cache_k, out_k, 0), (cache_v, out_v, 1))
        return block // per_device == me, [
            pltpu.make_async_copy(source.at[rows, columns], target.at[entry], sems.at[entry, i])
            for source, target, i in pairs
        ]

    def start(entry, carry):
        mine, both = copies(entry)

        @pl.when(mine)
        def _():
            for copy in both:
                copy.start()

        return carry

    def wait(entry, carry):
        mine, both = copies(entry)

        @pl.when(mine)
        def _():
            for copy in both:
                copy.wait()

        return carry

    lax.fori_loop(0, ENTRIES, start, 0)
    lax.fori_loop(0, ENTRIES, wait, 0)


def owned_blocks(blocks, cache_k, cache_v):
    shape = jax.ShapeDtypeStruct((ENTRIES, VBLOCK, HD), jnp.bfloat16)
    whole = pl.BlockSpec(memory_space=pltpu.VMEM)
    return pl.pallas_call(
        functools.partial(owned_kernel, cache_k.shape[0] // VBLOCK),
        out_shape=(shape, shape),
        in_specs=[SMEM, ANY, ANY],
        out_specs=(whole, whole),
        scratch_shapes=[pltpu.SemaphoreType.DMA((ENTRIES, 2))],
        compiler_params=pltpu.CompilerParams(vmem_limit_bytes=16 * 2**20),
        name="owned_blocks",
    )(blocks, cache_k, cache_v)


STAGES = 2
TILE = 2
OUT_SPACE = pltpu.HBM
VMEM = 24
COST = 2**20
ROWS = VBLOCK // STAGES
WHOLE = pl.BlockSpec(memory_space=pltpu.VMEM)


def room(share):
    mean = ENTRIES * share
    wide = mean + 3.0 * math.sqrt(mean * (1.0 - share)) + 1.5
    return min(ENTRIES + 1, math.ceil(wide))


def owner_of(block, per_device):
    if per_device & (per_device - 1) == 0:
        return lax.shift_right_logical(block, per_device.bit_length() - 1)
    return lax.div(block, per_device)


def pack_kernel(per_device, limit, blocks, cache_k, cache_v, kept, sent, sems):
    me = lax.axis_index("ctx")
    even = lax.rem(me, 2) == 0
    count = jnp.int32(0)
    for entry in range(ENTRIES):
        head = entry // NV
        block = blocks[head, entry % NV]
        owner = owner_of(block, per_device)
        mine = owner == me
        local = block - owner * per_device

        def start(pair, head=head, local=local, count=count):
            rows = pl.ds(pl.multiple_of(local * VBLOCK, VBLOCK), VBLOCK)
            for i, target in enumerate((kept, sent)):
                source = pair[i].at[rows, pl.ds(head * HD, HD)]
                pltpu.make_async_copy(source, target.at[count], sems.at[count, i]).start()

        @pl.when(mine & (count < limit))
        def _(start=start):
            @pl.when(even)
            def _():
                start((cache_k, cache_v))

            @pl.when(jnp.logical_not(even))
            def _():
                start((cache_v, cache_k))

        count += mine.astype(jnp.int32)

    for at in range(limit):

        @pl.when(at < count)
        def _(at=at):
            for i, target in enumerate((kept, sent)):
                source = cache_k.at[pl.ds(0, VBLOCK), pl.ds(0, HD)]
                pltpu.make_async_copy(source, target.at[at], sems.at[at, i]).wait()


def pack(blocks, cache_k, cache_v, limit):
    shape = jax.ShapeDtypeStruct((limit, VBLOCK, HD), jnp.bfloat16)
    return pl.pallas_call(
        functools.partial(pack_kernel, cache_k.shape[0] // VBLOCK, limit),
        out_shape=(shape, shape),
        in_specs=[SMEM, ANY, ANY],
        out_specs=(WHOLE, WHOLE),
        scratch_shapes=[pltpu.SemaphoreType.DMA((limit, 2))],
        compiler_params=pltpu.CompilerParams(vmem_limit_bytes=16 * 2**20),
        name="pack",
    )(blocks, cache_k, cache_v)


def walk(blocks, per_device, known, bit, limits, act):
    me = lax.axis_index("ctx")
    table = blocks[...]
    at_mine = at_other = jnp.int32(0)
    for entry in range(ENTRIES):
        away = (owner_of(table[entry // NV, entry % NV], per_device) ^ me) & ~known
        mine, other = away == 0, away == bit
        tops = jnp.minimum(at_mine, limits[0] - 1), jnp.minimum(at_other, limits[1] - 1)
        act(entry, *tops, at_mine + at_other, other)
        at_mine += mine.astype(jnp.int32)
        at_other += other.astype(jnp.int32)


def merge_kernel(per_device, jobs, blocks, *refs):
    refs = list(refs)
    me = lax.axis_index("ctx")
    sources = [(refs.pop(0), refs.pop(0)) for _ in jobs]
    for (known, bit, halved, parts), (mine, other) in zip(jobs, sources):
        outs = [refs.pop(0) for _ in range(parts)]
        size, rows = outs[0].shape[:2]
        first = pl.multiple_of(jnp.where((me & halved) == 0, 0, rows), rows) if halved else 0

        def act(
            entry, at_mine, at_other, place, theirs, mine=mine, other=other, outs=outs, first=first
        ):
            place = jnp.minimum(place, outs[0].shape[0] - 1)
            for at, out in enumerate(outs):
                span = pl.ds(first + at * out.shape[1], out.shape[1])
                out[place] = jnp.where(theirs, other[at_other, span], mine[at_mine, span])

        walk(blocks, per_device, known, bit, (mine.shape[0], other.shape[0]), act)


def merged(blocks, per_device, jobs):
    shapes, lists = [], []
    for _, _, halved, parts, mine, other, size in jobs:
        rows = mine.shape[1] // (2 if halved else parts)
        shapes += [jax.ShapeDtypeStruct((size, rows, HD), jnp.bfloat16)] * parts
        lists += [mine, other]
    return pl.pallas_call(
        functools.partial(merge_kernel, per_device, [job[:4] for job in jobs]),
        out_shape=tuple(shapes),
        in_specs=[WHOLE] * (1 + len(lists)),
        out_specs=(WHOLE,) * len(shapes),
        compiler_params=pltpu.CompilerParams(vmem_limit_bytes=16 * 2**20),
        name="merge",
    )(blocks, *lists)


def stage_kernel(per_device, known, bit, banded, last, *refs):
    refs = list(refs)
    blocks = refs.pop(0)
    offsets = refs.pop(0) if banded else None
    queries, mine, other, mine_twin, other_twin = refs[:5]
    refs = refs[5:]
    if banded:
        before, own_k, own_v = refs[:3]
        refs = refs[3:]
    else:
        largest_in, total_in, mixed_in = refs[:3]
        refs = refs[3:]
    if last:
        out, kbuf, vbuf, held, sems = refs
    else:
        largest_out, total_out, mixed_out, kbuf, vbuf = refs
    me = lax.axis_index("ctx")
    even = lax.rem(me, 2) == 0
    wide = NV * ROWS

    def act(entry, at_mine, at_other, place, theirs):
        tile = jnp.where(theirs, other[at_other], mine[at_mine])
        twin = jnp.where(theirs, other_twin[at_other], mine_twin[at_mine])
        rows = pl.ds(entry % NV * ROWS, ROWS)
        kbuf[entry // NV, rows] = jnp.where(even, tile, twin)
        vbuf[entry // NV, rows, :HD] = jnp.where(even, twin, tile)

    if not last:
        walk(blocks, per_device, known, bit, (mine.shape[0], other.shape[0]), act)
    else:
        half = wide // 2
        for head in range(KVH):
            span = slice(head * NV, (head + 1) * NV)
            for at, (own, twin) in enumerate(((mine, mine_twin), (other, other_twin))):
                tile, pair = own[span].reshape(half, HD), twin[span].reshape(half, HD)
                rows = slice(at * half, (at + 1) * half)
                kbuf[head, rows] = jnp.where(even, tile, pair)
                vbuf[head, rows, :HD] = jnp.where(even, pair, tile)
    copies = []
    for head in range(KVH):
        columns = slice(head * HD, (head + 1) * HD)
        vbuf[head, :, HD:] = jnp.ones((vbuf.shape[1], HD), jnp.bfloat16)
        mask = None
        if banded:
            values = slice((KVH + head) * HD, (KVH + head + 1) * HD)
            kbuf[head, wide : wide + SMAX] = before[:, columns]
            kbuf[head, wide + SMAX :] = own_k[:, columns]
            vbuf[head, wide : wide + SMAX, :HD] = before[:, values]
            vbuf[head, wide + SMAX :, :HD] = own_v[:, columns]
            mask = band_mask(offsets[...], head, me == 0)
        for at in range(0, GROUP, TILE):
            rows = jnp.concatenate(
                [
                    queries[:, (head * GROUP + at + i) * HD : (head * GROUP + at + i + 1) * HD]
                    for i in range(TILE)
                ],
                axis=0,
            )
            start = (head * GROUP + at) * QDEV
            tile = slice(start, start + TILE * QDEV)
            floor = None if banded else largest_in[tile]
            largest, mixed = attend_rows(rows, kbuf[head], vbuf[head], mask, floor)
            mixed, total = mixed[:, :HD], mixed[:, HD:]
            if not banded:
                then = jnp.exp2(floor - largest)
                mixed = mixed + mixed_in[tile] * then
                total = total + total_in[tile] * then
            if last:
                result = (mixed / total).astype(jnp.bfloat16)
                for i in range(TILE):
                    held[head, :, (at + i) * HD : (at + i + 1) * HD] = result[
                        i * QDEV : (i + 1) * QDEV
                    ]
            else:
                largest_out[tile] = jnp.broadcast_to(largest, mixed.shape)
                total_out[tile] = total
                mixed_out[tile] = mixed
        if last:
            span = pl.ds(head * GROUP * HD, GROUP * HD)
            copies.append(pltpu.make_async_copy(held.at[head], out.at[:, span], sems.at[head]))
            copies[-1].start()
    for copy in copies:
        copy.wait()


def attend_stage(known, bit, per_device, blocks, queries, lists, offsets=None, bands=None, state=None):
    banded, last = bands is not None, state is not None
    tall = KVH * GROUP * QDEV
    args = [blocks] + [offsets] * banded + [queries, *lists]
    args += list(bands if banded else state)
    specs = [WHOLE] * len(args)
    keys = NV * ROWS + (SMAX + QDEV) * banded
    scratch = [
        pltpu.VMEM((KVH, keys, HD), jnp.bfloat16),
        pltpu.VMEM((KVH, keys, 2 * HD), jnp.bfloat16),
    ]
    if last:
        out_shape = jax.ShapeDtypeStruct(queries.shape, jnp.bfloat16)
        out_specs = pl.BlockSpec(memory_space=OUT_SPACE)
        scratch += [
            pltpu.VMEM((KVH, QDEV, GROUP * HD), jnp.bfloat16),
            pltpu.SemaphoreType.DMA((KVH,)),
        ]
    else:
        out_shape = (jax.ShapeDtypeStruct((tall, HD), jnp.float32),) * 3
        out_specs = (WHOLE,) * 3
    return pl.pallas_call(
        functools.partial(stage_kernel, per_device, known, bit, banded, last),
        out_shape=out_shape,
        in_specs=specs,
        out_specs=out_specs,
        scratch_shapes=scratch,
        compiler_params=pltpu.CompilerParams(vmem_limit_bytes=VMEM * 2**20),
        cost_estimate=pl.CostEstimate(flops=COST, bytes_accessed=COST, transcendentals=0),
        name="attend_last" if last else "attend_first",
    )(*args)


def permuted(array, pairs):
    return lax.ppermute(array, "ctx", pairs)


def swapped(array, bit):
    return permuted(array, [(i, i ^ bit) for i in range(lax.axis_size("ctx"))])


def fits(blocks, per_device, peers, masks):
    most = [room((1 << mask.bit_count()) / peers) + (-1 if mask else 1) for mask in masks]
    owners = (blocks // per_device).reshape(1, 1, ENTRIES)
    ids = jnp.arange(peers, dtype=jnp.int32)[None, :, None]
    away = (owners ^ ids) & ~jnp.array(masks, jnp.int32)[:, None, None]
    counts = jnp.sum((away == 0).astype(jnp.int32), axis=2)
    return jnp.all(counts <= jnp.array(most, jnp.int32)[:, None])


def general(queries, bands, cache_k, cache_v, blocks, offsets, bits):
    keys, values = owned_blocks(blocks, cache_k, cache_v)
    even = lax.axis_index("ctx") % 2 == 0
    mine = jnp.where(even, keys, values) + swapped(jnp.where(even, values, keys), 1)
    for bit in bits[1:]:
        mine = mine + swapped(mine, bit)
    twin = swapped(mine, 1)
    keys, values = jnp.where(even, mine, twin), jnp.where(even, twin, mine)
    keys = keys.reshape(KVH, NV * VBLOCK, HD)
    values = values.reshape(KVH, NV * VBLOCK, HD)
    before, own_k, own_v = bands
    wide = KVH * HD
    bands = (before[:, :wide], own_k, before[:, wide:], own_v)
    return attend_dense(offsets, queries, keys, values, bands)


def shards(queries, span_k, span_v, cache_k, cache_v, blocks, offsets):
    peers = lax.axis_size("ctx")
    per_device = cache_k.shape[0] // VBLOCK
    ahead = [(i, i + 1) for i in range(peers - 1)]
    near = 2
    far = [1 << at for at in range(peers.bit_length() - 2, 1, -1)]
    bits = [1] + far + [near]
    masks_a = [sum(bits[:at]) for at in range(len(bits))]
    masks_b = [1 + near + sum(far[:at]) for at in range(len(far))]

    def job(known, bit, mine, other, parts=1, halved=0):
        size = room((1 << (known | bit).bit_count()) / peers)
        if known + bit == peers - 1:
            size = ENTRIES
        return known, bit, halved, parts, mine, other, size

    merge = functools.partial(merged, blocks, per_device)
    kept, sent = pack(blocks, cache_k, cache_v, room(1 / peers) + 1)
    mine_a, mine_b = merge([job(0, 1, kept, swapped(sent, 1), parts=STAGES)])
    spans, mine_b = lax.optimization_barrier((jnp.concatenate([span_k, span_v], axis=1), mine_b))
    before = permuted(spans, ahead)
    short = jnp.logical_not(fits(blocks, per_device, peers, masks_a + masks_b)).astype(jnp.int32)

    steps_a = list(zip(masks_a[1:], far))
    steps_b = list(zip([1] + masks_b, [near] + far))
    other_a = swapped(mine_a, far[0])
    other_b = swapped(mine_b, near)
    other_a, short = lax.optimization_barrier((other_a, short))
    for at in range(len(far)):
        job_a = job(*steps_a[at], mine_a, other_a)
        job_b = job(*steps_b[at], mine_b, other_b, halved=near if at == 0 else 0)
        if at < len(far) - 1:
            mine_a, mine_b = merge([job_a, job_b])
        else:
            (mine_a,), (mine_b,) = merge([job_a]), merge([job_b])
        other_a = swapped(mine_a, (far + [near])[at + 1])
        other_b = swapped(mine_b, far[at])
        if at < len(far) - 1:
            other_a, other_b, before = lax.optimization_barrier((other_a, other_b, before))
    (mine_b,) = merge([job(*steps_b[-1], mine_b, other_b)])
    other_a, mine_b = lax.optimization_barrier((other_a, mine_b))
    other_b = swapped(mine_b, near)
    twin_a, twin_b = swapped(mine_a, 1), swapped(mine_b, 1)

    bands = (before, span_k, span_v)
    shared = (peers - 1 - near, near, per_device, blocks, queries)
    lists = (mine_a, other_a, twin_a, swapped(other_a, 1))
    state = attend_stage(*shared, lists, offsets=offsets, bands=bands)
    state, late = lax.optimization_barrier((state, other_b))
    lists = (mine_b, late, twin_b, swapped(late, 1))
    fast = attend_stage(*shared, lists, state=state)

    def again(carry):
        return 0, general(queries, bands, cache_k, cache_v, blocks, offsets, bits)

    return lax.while_loop(lambda carry: carry[0] > 0, again, (short, fast))[1]


def solution(mesh):
    rows = P(("groups", "ctx"), None)
    heads = P("groups", None)
    return jax.shard_map(
        shards,
        mesh=mesh,
        in_specs=(rows, rows, rows, rows, rows, heads, heads),
        out_specs=rows,
        check_vma=False,
    )
```

```python
import functools
import math

import jax
import jax.numpy as jnp
from jax import lax
from jax.experimental import pallas as pl
from jax.experimental.pallas import tpu as pltpu
from jax.sharding import PartitionSpec as P

KVH = 4
GROUP = 8
HD = 128
QDEV = 128
VBLOCK = 64
NV = 16
NS = 64
SMAX = 128
ENTRIES = KVH * NV
FACTOR = math.log2(math.e) / math.sqrt(HD)
LOW = -1e38

ANY = pl.BlockSpec(memory_space=pl.ANY)
SMEM = pl.BlockSpec(memory_space=pltpu.SMEM)


def band_mask(offsets, head, first):
    columns = lax.broadcasted_iota(jnp.int32, (8, SMAX + QDEV), 1)
    distance = SMAX - columns
    row = jnp.zeros((8, SMAX + QDEV), jnp.int32)
    for at in range(NS):
        row = jnp.where(distance == offsets[head, at], 1, row)
    rows = jnp.concatenate([row] * (QDEV // 8), axis=0)
    rolled = pltpu.roll(rows, 0, 1, stride=1, stride_axis=0)
    keys = lax.broadcasted_iota(jnp.int32, (QDEV, SMAX + QDEV), 1)
    return (rolled > 0) & (keys >= jnp.where(first, SMAX, 0))


def attend_rows(rows, keys, values_ones, mask, floor=None):
    scores = lax.dot_general(
        rows, keys, (((1,), (1,)), ((), ())), preferred_element_type=jnp.float32
    )
    if mask is not None:
        wide = scores.shape[1] - mask.shape[1]
        reps = rows.shape[0] // QDEV
        tiled = jnp.concatenate([mask] * reps, axis=0)
        band = jnp.where(tiled, scores[:, wide:], LOW)
        scores = jnp.concatenate([scores[:, :wide], band], axis=1)
    largest = jnp.max(scores, axis=1, keepdims=True) * FACTOR
    if floor is not None:
        largest = jnp.maximum(jnp.broadcast_to(largest, floor.shape), floor)
        above = jnp.concatenate([largest] * (scores.shape[1] // HD), axis=1)
    else:
        above = largest
    weights = jnp.exp2(scores * FACTOR - above).astype(jnp.bfloat16)
    mixed = jnp.dot(weights, values_ones, preferred_element_type=jnp.float32)
    return largest, mixed


def dense_kernel(
    offsets, queries, keys, values, before_k, own_k, before_v, own_v, out, kbuf, vbuf
):
    head = pl.program_id(0)
    first = lax.axis_index("ctx") == 0
    wide = NV * VBLOCK
    kbuf[:wide] = keys[0]
    kbuf[wide : wide + SMAX] = before_k[...]
    kbuf[wide + SMAX :] = own_k[...]
    vbuf[:wide, :HD] = values[0]
    vbuf[wide : wide + SMAX, :HD] = before_v[...]
    vbuf[wide + SMAX :, :HD] = own_v[...]
    vbuf[:, HD:] = jnp.ones((wide + SMAX + QDEV, HD), jnp.bfloat16)
    mask = band_mask(offsets, head, first)
    for at in range(0, GROUP, 2):
        rows = jnp.concatenate(
            [queries[:, (at + i) * HD : (at + i + 1) * HD] for i in range(2)], axis=0
        )
        _, mixed = attend_rows(rows, kbuf[...], vbuf[...], mask)
        result = (mixed[:, :HD] / mixed[:, HD:]).astype(jnp.bfloat16)
        for i in range(2):
            out[:, (at + i) * HD : (at + i + 1) * HD] = result[i * QDEV : (i + 1) * QDEV]


def head_block(rows):
    return pl.BlockSpec((rows, HD), lambda head: (0, head))


def attend_dense(offsets, queries, keys, values, bands):
    wide = NV * VBLOCK
    return pl.pallas_call(
        dense_kernel,
        grid=(KVH,),
        out_shape=jax.ShapeDtypeStruct(queries.shape, jnp.bfloat16),
        in_specs=[
            SMEM,
            pl.BlockSpec((QDEV, GROUP * HD), lambda head: (0, head)),
            pl.BlockSpec((1, wide, HD), lambda head: (head, 0, 0)),
            pl.BlockSpec((1, wide, HD), lambda head: (head, 0, 0)),
        ]
        + [head_block(QDEV)] * 4,
        out_specs=pl.BlockSpec((QDEV, GROUP * HD), lambda head: (0, head)),
        scratch_shapes=[
            pltpu.VMEM((wide + SMAX + QDEV, HD), jnp.bfloat16),
            pltpu.VMEM((wide + SMAX + QDEV, 2 * HD), jnp.bfloat16),
        ],
        compiler_params=pltpu.CompilerParams(vmem_limit_bytes=48 * 2**20),
        name="attend_dense",
    )(offsets, queries, keys, values, *bands)


def owned_kernel(per_device, blocks, cache_k, cache_v, out_k, out_v, sems):
    me = lax.axis_index("ctx")
    out_k[...] = jnp.zeros_like(out_k)
    out_v[...] = jnp.zeros_like(out_v)

    def copies(entry):
        head, at = entry // NV, entry % NV
        block = blocks[head, at]
        local = block % per_device
        rows = pl.ds(pl.multiple_of(local * VBLOCK, VBLOCK), VBLOCK)
        columns = pl.ds(pl.multiple_of(head * HD, HD), HD)
        pairs = ((cache_k, out_k, 0), (cache_v, out_v, 1))
        return block // per_device == me, [
            pltpu.make_async_copy(source.at[rows, columns], target.at[entry], sems.at[entry, i])
            for source, target, i in pairs
        ]

    def start(entry, carry):
        mine, both = copies(entry)

        @pl.when(mine)
        def _():
            for copy in both:
                copy.start()

        return carry

    def wait(entry, carry):
        mine, both = copies(entry)

        @pl.when(mine)
        def _():
            for copy in both:
                copy.wait()

        return carry

    lax.fori_loop(0, ENTRIES, start, 0)
    lax.fori_loop(0, ENTRIES, wait, 0)


def owned_blocks(blocks, cache_k, cache_v):
    shape = jax.ShapeDtypeStruct((ENTRIES, VBLOCK, HD), jnp.bfloat16)
    whole = pl.BlockSpec(memory_space=pltpu.VMEM)
    return pl.pallas_call(
        functools.partial(owned_kernel, cache_k.shape[0] // VBLOCK),
        out_shape=(shape, shape),
        in_specs=[SMEM, ANY, ANY],
        out_specs=(whole, whole),
        scratch_shapes=[pltpu.SemaphoreType.DMA((ENTRIES, 2))],
        compiler_params=pltpu.CompilerParams(vmem_limit_bytes=16 * 2**20),
        name="owned_blocks",
    )(blocks, cache_k, cache_v)


STAGES = 2
TILE = 2
OUT_SPACE = pltpu.HBM
VMEM = 24
COST = 2**20
ROWS = VBLOCK // STAGES
WHOLE = pl.BlockSpec(memory_space=pltpu.VMEM)


def room(share):
    mean = ENTRIES * share
    wide = mean + 3.0 * math.sqrt(mean * (1.0 - share)) + 1.5
    return min(ENTRIES + 1, math.ceil(wide))


def owner_of(block, per_device):
    if per_device & (per_device - 1) == 0:
        return lax.shift_right_logical(block, per_device.bit_length() - 1)
    return lax.div(block, per_device)


def pack_kernel(per_device, limit, blocks, cache_k, cache_v, kept, sent, sems):
    me = lax.axis_index("ctx")
    even = lax.rem(me, 2) == 0
    count = jnp.int32(0)
    for entry in range(ENTRIES):
        head = entry // NV
        block = blocks[head, entry % NV]
        owner = owner_of(block, per_device)
        mine = owner == me
        local = block - owner * per_device

        def start(pair, head=head, local=local, count=count):
            rows = pl.ds(pl.multiple_of(local * VBLOCK, VBLOCK), VBLOCK)
            for i, target in enumerate((kept, sent)):
                source = pair[i].at[rows, pl.ds(head * HD, HD)]
                pltpu.make_async_copy(source, target.at[count], sems.at[count, i]).start()

        @pl.when(mine & (count < limit))
        def _(start=start):
            @pl.when(even)
            def _():
                start((cache_k, cache_v))

            @pl.when(jnp.logical_not(even))
            def _():
                start((cache_v, cache_k))

        count += mine.astype(jnp.int32)

    for at in range(limit):

        @pl.when(at < count)
        def _(at=at):
            for i, target in enumerate((kept, sent)):
                source = cache_k.at[pl.ds(0, VBLOCK), pl.ds(0, HD)]
                pltpu.make_async_copy(source, target.at[at], sems.at[at, i]).wait()


def pack(blocks, cache_k, cache_v, limit):
    shape = jax.ShapeDtypeStruct((limit, VBLOCK, HD), jnp.bfloat16)
    return pl.pallas_call(
        functools.partial(pack_kernel, cache_k.shape[0] // VBLOCK, limit),
        out_shape=(shape, shape),
        in_specs=[SMEM, ANY, ANY],
        out_specs=(WHOLE, WHOLE),
        scratch_shapes=[pltpu.SemaphoreType.DMA((limit, 2))],
        compiler_params=pltpu.CompilerParams(vmem_limit_bytes=16 * 2**20),
        name="pack",
    )(blocks, cache_k, cache_v)


def walk(blocks, per_device, known, bit, limits, act):
    me = lax.axis_index("ctx")
    table = blocks[...]
    at_mine = at_other = jnp.int32(0)
    for entry in range(ENTRIES):
        away = (owner_of(table[entry // NV, entry % NV], per_device) ^ me) & ~known
        mine, other = away == 0, away == bit
        tops = jnp.minimum(at_mine, limits[0] - 1), jnp.minimum(at_other, limits[1] - 1)
        act(entry, *tops, at_mine + at_other, other)
        at_mine += mine.astype(jnp.int32)
        at_other += other.astype(jnp.int32)


def merge_kernel(per_device, jobs, blocks, *refs):
    refs = list(refs)
    me = lax.axis_index("ctx")
    sources = [(refs.pop(0), refs.pop(0)) for _ in jobs]
    for (known, bit, halved, parts), (mine, other) in zip(jobs, sources):
        outs = [refs.pop(0) for _ in range(parts)]
        size, rows = outs[0].shape[:2]
        first = pl.multiple_of(jnp.where((me & halved) == 0, 0, rows), rows) if halved else 0

        def act(
            entry, at_mine, at_other, place, theirs, mine=mine, other=other, outs=outs, first=first
        ):
            place = jnp.minimum(place, outs[0].shape[0] - 1)
            for at, out in enumerate(outs):
                span = pl.ds(first + at * out.shape[1], out.shape[1])
                out[place] = jnp.where(theirs, other[at_other, span], mine[at_mine, span])

        walk(blocks, per_device, known, bit, (mine.shape[0], other.shape[0]), act)


def merged(blocks, per_device, jobs):
    shapes, lists = [], []
    for _, _, halved, parts, mine, other, size in jobs:
        rows = mine.shape[1] // (2 if halved else parts)
        shapes += [jax.ShapeDtypeStruct((size, rows, HD), jnp.bfloat16)] * parts
        lists += [mine, other]
    return pl.pallas_call(
        functools.partial(merge_kernel, per_device, [job[:4] for job in jobs]),
        out_shape=tuple(shapes),
        in_specs=[WHOLE] * (1 + len(lists)),
        out_specs=(WHOLE,) * len(shapes),
        compiler_params=pltpu.CompilerParams(vmem_limit_bytes=16 * 2**20),
        name="merge",
    )(blocks, *lists)


def stage_kernel(per_device, known, bit, banded, last, *refs):
    refs = list(refs)
    blocks = refs.pop(0)
    offsets = refs.pop(0) if banded else None
    queries, mine, other, mine_twin, other_twin = refs[:5]
    refs = refs[5:]
    if banded:
        before, own_k, own_v = refs[:3]
        refs = refs[3:]
    else:
        largest_in, total_in, mixed_in = refs[:3]
        refs = refs[3:]
    if last:
        out, kbuf, vbuf, held, sems = refs
    else:
        largest_out, total_out, mixed_out, kbuf, vbuf = refs
    me = lax.axis_index("ctx")
    even = lax.rem(me, 2) == 0
    wide = NV * ROWS

    def act(entry, at_mine, at_other, place, theirs):
        tile = jnp.where(theirs, other[at_other], mine[at_mine])
        twin = jnp.where(theirs, other_twin[at_other], mine_twin[at_mine])
        rows = pl.ds(entry % NV * ROWS, ROWS)
        kbuf[entry // NV, rows] = jnp.where(even, tile, twin)
        vbuf[entry // NV, rows, :HD] = jnp.where(even, twin, tile)

    if not last:
        walk(blocks, per_device, known, bit, (mine.shape[0], other.shape[0]), act)
    else:
        half = wide // 2
        for head in range(KVH):
            span = slice(head * NV, (head + 1) * NV)
            for at, (own, twin) in enumerate(((mine, mine_twin), (other, other_twin))):
                tile, pair = own[span].reshape(half, HD), twin[span].reshape(half, HD)
                rows = slice(at * half, (at + 1) * half)
                kbuf[head, rows] = jnp.where(even, tile, pair)
                vbuf[head, rows, :HD] = jnp.where(even, pair, tile)
    copies = []
    for head in range(KVH):
        columns = slice(head * HD, (head + 1) * HD)
        vbuf[head, :, HD:] = jnp.ones((vbuf.shape[1], HD), jnp.bfloat16)
        mask = None
        if banded:
            values = slice((KVH + head) * HD, (KVH + head + 1) * HD)
            kbuf[head, wide : wide + SMAX] = before[:, columns]
            kbuf[head, wide + SMAX :] = own_k[:, columns]
            vbuf[head, wide : wide + SMAX, :HD] = before[:, values]
            vbuf[head, wide + SMAX :, :HD] = own_v[:, columns]
            mask = band_mask(offsets[...], head, me == 0)
        for at in range(0, GROUP, TILE):
            rows = jnp.concatenate(
                [
                    queries[:, (head * GROUP + at + i) * HD : (head * GROUP + at + i + 1) * HD]
                    for i in range(TILE)
                ],
                axis=0,
            )
            start = (head * GROUP + at) * QDEV
            tile = slice(start, start + TILE * QDEV)
            floor = None if banded else largest_in[tile]
            largest, mixed = attend_rows(rows, kbuf[head], vbuf[head], mask, floor)
            mixed, total = mixed[:, :HD], mixed[:, HD:]
            if not banded:
                then = jnp.exp2(floor - largest)
                mixed = mixed + mixed_in[tile] * then
                total = total + total_in[tile] * then
            if last:
                result = (mixed / total).astype(jnp.bfloat16)
                for i in range(TILE):
                    held[head, :, (at + i) * HD : (at + i + 1) * HD] = result[
                        i * QDEV : (i + 1) * QDEV
                    ]
            else:
                largest_out[tile] = jnp.broadcast_to(largest, mixed.shape)
                total_out[tile] = total
                mixed_out[tile] = mixed
        if last:
            span = pl.ds(head * GROUP * HD, GROUP * HD)
            copies.append(pltpu.make_async_copy(held.at[head], out.at[:, span], sems.at[head]))
            copies[-1].start()
    for copy in copies:
        copy.wait()


def attend_stage(known, bit, per_device, blocks, queries, lists, offsets=None, bands=None, state=None):
    banded, last = bands is not None, state is not None
    tall = KVH * GROUP * QDEV
    args = [blocks] + [offsets] * banded + [queries, *lists]
    args += list(bands if banded else state)
    specs = [WHOLE] * len(args)
    keys = NV * ROWS + (SMAX + QDEV) * banded
    scratch = [
        pltpu.VMEM((KVH, keys, HD), jnp.bfloat16),
        pltpu.VMEM((KVH, keys, 2 * HD), jnp.bfloat16),
    ]
    if last:
        out_shape = jax.ShapeDtypeStruct(queries.shape, jnp.bfloat16)
        out_specs = pl.BlockSpec(memory_space=OUT_SPACE)
        scratch += [
            pltpu.VMEM((KVH, QDEV, GROUP * HD), jnp.bfloat16),
            pltpu.SemaphoreType.DMA((KVH,)),
        ]
    else:
        out_shape = (jax.ShapeDtypeStruct((tall, HD), jnp.float32),) * 3
        out_specs = (WHOLE,) * 3
    return pl.pallas_call(
        functools.partial(stage_kernel, per_device, known, bit, banded, last),
        out_shape=out_shape,
        in_specs=specs,
        out_specs=out_specs,
        scratch_shapes=scratch,
        compiler_params=pltpu.CompilerParams(vmem_limit_bytes=VMEM * 2**20),
        cost_estimate=pl.CostEstimate(flops=COST, bytes_accessed=COST, transcendentals=0),
        name="attend_last" if last else "attend_first",
    )(*args)


def permuted(array, pairs):
    return lax.ppermute(array, "ctx", pairs)


def swapped(array, bit):
    return permuted(array, [(i, i ^ bit) for i in range(lax.axis_size("ctx"))])


def fits(blocks, per_device, peers, masks):
    most = [room((1 << mask.bit_count()) / peers) + (-1 if mask else 1) for mask in masks]
    owners = (blocks // per_device).reshape(1, 1, ENTRIES)
    ids = jnp.arange(peers, dtype=jnp.int32)[None, :, None]
    away = (owners ^ ids) & ~jnp.array(masks, jnp.int32)[:, None, None]
    counts = jnp.sum((away == 0).astype(jnp.int32), axis=2)
    return jnp.all(counts <= jnp.array(most, jnp.int32)[:, None])


def general(queries, bands, cache_k, cache_v, blocks, offsets, bits):
    keys, values = owned_blocks(blocks, cache_k, cache_v)
    even = lax.axis_index("ctx") % 2 == 0
    mine = jnp.where(even, keys, values) + swapped(jnp.where(even, values, keys), 1)
    for bit in bits[1:]:
        mine = mine + swapped(mine, bit)
    twin = swapped(mine, 1)
    keys, values = jnp.where(even, mine, twin), jnp.where(even, twin, mine)
    keys = keys.reshape(KVH, NV * VBLOCK, HD)
    values = values.reshape(KVH, NV * VBLOCK, HD)
    before, own_k, own_v = bands
    wide = KVH * HD
    bands = (before[:, :wide], own_k, before[:, wide:], own_v)
    return attend_dense(offsets, queries, keys, values, bands)


def shards(queries, span_k, span_v, cache_k, cache_v, blocks, offsets):
    peers = lax.axis_size("ctx")
    per_device = cache_k.shape[0] // VBLOCK
    ahead = [(i, i + 1) for i in range(peers - 1)]
    near = 2
    far = [1 << at for at in range(peers.bit_length() - 2, 1, -1)]
    bits = [1] + far + [near]
    masks_a = [sum(bits[:at]) for at in range(len(bits))]
    masks_b = [1 + near + sum(far[:at]) for at in range(len(far))]

    def job(known, bit, mine, other, parts=1, halved=0):
        size = room((1 << (known | bit).bit_count()) / peers)
        if known + bit == peers - 1:
            size = ENTRIES
        return known, bit, halved, parts, mine, other, size

    merge = functools.partial(merged, blocks, per_device)
    kept, sent = pack(blocks, cache_k, cache_v, room(1 / peers) + 1)
    mine_a, mine_b = merge([job(0, 1, kept, swapped(sent, 1), parts=STAGES)])
    spans, mine_b = lax.optimization_barrier((jnp.concatenate([span_k, span_v], axis=1), mine_b))
    before = permuted(spans, ahead)
    short = jnp.logical_not(fits(blocks, per_device, peers, masks_a + masks_b)).astype(jnp.int32)

    steps_a = list(zip(masks_a[1:], far))
    steps_b = list(zip([1] + masks_b, [near] + far))
    other_a = swapped(mine_a, far[0])
    other_b = swapped(mine_b, near)
    other_a, short = lax.optimization_barrier((other_a, short))
    for at in range(len(far)):
        job_a = job(*steps_a[at], mine_a, other_a)
        job_b = job(*steps_b[at], mine_b, other_b, halved=near if at == 0 else 0)
        if at < len(far) - 1:
            mine_a, mine_b = merge([job_a, job_b])
        else:
            (mine_a,), (mine_b,) = merge([job_a]), merge([job_b])
        other_a = swapped(mine_a, (far + [near])[at + 1])
        other_b = swapped(mine_b, far[at])
        if at < len(far) - 1:
            other_a, before = lax.optimization_barrier((other_a, before))
    (mine_b,) = merge([job(*steps_b[-1], mine_b, other_b)])
    other_a, mine_b = lax.optimization_barrier((other_a, mine_b))
    other_b = swapped(mine_b, near)
    twin_a, twin_b = swapped(mine_a, 1), swapped(mine_b, 1)

    bands = (before, span_k, span_v)
    shared = (peers - 1 - near, near, per_device, blocks, queries)
    lists = (mine_a, other_a, twin_a, swapped(other_a, 1))
    state = attend_stage(*shared, lists, offsets=offsets, bands=bands)
    state, late = lax.optimization_barrier((state, other_b))
    lists = (mine_b, late, twin_b, swapped(late, 1))
    fast = attend_stage(*shared, lists, state=state)

    def again(carry):
        return 0, general(queries, bands, cache_k, cache_v, blocks, offsets, bits)

    return lax.while_loop(lambda carry: carry[0] > 0, again, (short, fast))[1]


def solution(mesh):
    rows = P(("groups", "ctx"), None)
    heads = P("groups", None)
    return jax.shard_map(
        shards,
        mesh=mesh,
        in_specs=(rows, rows, rows, rows, rows, heads, heads),
        out_specs=rows,
        check_vma=False,
    )
```

```python
import functools
import math

import jax
import jax.numpy as jnp
from jax import lax
from jax.experimental import pallas as pl
from jax.experimental.pallas import tpu as pltpu
from jax.sharding import PartitionSpec as P

KVH = 4
GROUP = 8
HD = 128
QDEV = 128
VBLOCK = 64
NV = 16
NS = 64
SMAX = 128
ENTRIES = KVH * NV
FACTOR = math.log2(math.e) / math.sqrt(HD)
LOW = -1e38

ANY = pl.BlockSpec(memory_space=pl.ANY)
SMEM = pl.BlockSpec(memory_space=pltpu.SMEM)


def band_mask(offsets, head, first):
    columns = lax.broadcasted_iota(jnp.int32, (8, SMAX + QDEV), 1)
    distance = SMAX - columns
    row = jnp.zeros((8, SMAX + QDEV), jnp.int32)
    for at in range(NS):
        row = jnp.where(distance == offsets[head, at], 1, row)
    rows = jnp.concatenate([row] * (QDEV // 8), axis=0)
    rolled = pltpu.roll(rows, 0, 1, stride=1, stride_axis=0)
    keys = lax.broadcasted_iota(jnp.int32, (QDEV, SMAX + QDEV), 1)
    return (rolled > 0) & (keys >= jnp.where(first, SMAX, 0))


def attend_rows(rows, keys, values_ones, mask, floor=None):
    scores = lax.dot_general(
        rows, keys, (((1,), (1,)), ((), ())), preferred_element_type=jnp.float32
    )
    if mask is not None:
        wide = scores.shape[1] - mask.shape[1]
        reps = rows.shape[0] // QDEV
        tiled = jnp.concatenate([mask] * reps, axis=0)
        band = jnp.where(tiled, scores[:, wide:], LOW)
        scores = jnp.concatenate([scores[:, :wide], band], axis=1)
    largest = jnp.max(scores, axis=1, keepdims=True) * FACTOR
    if floor is not None:
        largest = jnp.maximum(jnp.broadcast_to(largest, floor.shape), floor)
        above = jnp.concatenate([largest] * (scores.shape[1] // HD), axis=1)
    else:
        above = largest
    weights = jnp.exp2(scores * FACTOR - above).astype(jnp.bfloat16)
    mixed = jnp.dot(weights, values_ones, preferred_element_type=jnp.float32)
    return largest, mixed


def dense_kernel(
    offsets, queries, keys, values, before_k, own_k, before_v, own_v, out, kbuf, vbuf
):
    head = pl.program_id(0)
    first = lax.axis_index("ctx") == 0
    wide = NV * VBLOCK
    kbuf[:wide] = keys[0]
    kbuf[wide : wide + SMAX] = before_k[...]
    kbuf[wide + SMAX :] = own_k[...]
    vbuf[:wide, :HD] = values[0]
    vbuf[wide : wide + SMAX, :HD] = before_v[...]
    vbuf[wide + SMAX :, :HD] = own_v[...]
    vbuf[:, HD:] = jnp.ones((wide + SMAX + QDEV, HD), jnp.bfloat16)
    mask = band_mask(offsets, head, first)
    for at in range(0, GROUP, 2):
        rows = jnp.concatenate(
            [queries[:, (at + i) * HD : (at + i + 1) * HD] for i in range(2)], axis=0
        )
        _, mixed = attend_rows(rows, kbuf[...], vbuf[...], mask)
        result = (mixed[:, :HD] / mixed[:, HD:]).astype(jnp.bfloat16)
        for i in range(2):
            out[:, (at + i) * HD : (at + i + 1) * HD] = result[i * QDEV : (i + 1) * QDEV]


def head_block(rows):
    return pl.BlockSpec((rows, HD), lambda head: (0, head))


def attend_dense(offsets, queries, keys, values, bands):
    wide = NV * VBLOCK
    return pl.pallas_call(
        dense_kernel,
        grid=(KVH,),
        out_shape=jax.ShapeDtypeStruct(queries.shape, jnp.bfloat16),
        in_specs=[
            SMEM,
            pl.BlockSpec((QDEV, GROUP * HD), lambda head: (0, head)),
            pl.BlockSpec((1, wide, HD), lambda head: (head, 0, 0)),
            pl.BlockSpec((1, wide, HD), lambda head: (head, 0, 0)),
        ]
        + [head_block(QDEV)] * 4,
        out_specs=pl.BlockSpec((QDEV, GROUP * HD), lambda head: (0, head)),
        scratch_shapes=[
            pltpu.VMEM((wide + SMAX + QDEV, HD), jnp.bfloat16),
            pltpu.VMEM((wide + SMAX + QDEV, 2 * HD), jnp.bfloat16),
        ],
        compiler_params=pltpu.CompilerParams(vmem_limit_bytes=48 * 2**20),
        name="attend_dense",
    )(offsets, queries, keys, values, *bands)


def owned_kernel(per_device, blocks, cache_k, cache_v, out_k, out_v, sems):
    me = lax.axis_index("ctx")
    out_k[...] = jnp.zeros_like(out_k)
    out_v[...] = jnp.zeros_like(out_v)

    def copies(entry):
        head, at = entry // NV, entry % NV
        block = blocks[head, at]
        local = block % per_device
        rows = pl.ds(pl.multiple_of(local * VBLOCK, VBLOCK), VBLOCK)
        columns = pl.ds(pl.multiple_of(head * HD, HD), HD)
        pairs = ((cache_k, out_k, 0), (cache_v, out_v, 1))
        return block // per_device == me, [
            pltpu.make_async_copy(source.at[rows, columns], target.at[entry], sems.at[entry, i])
            for source, target, i in pairs
        ]

    def start(entry, carry):
        mine, both = copies(entry)

        @pl.when(mine)
        def _():
            for copy in both:
                copy.start()

        return carry

    def wait(entry, carry):
        mine, both = copies(entry)

        @pl.when(mine)
        def _():
            for copy in both:
                copy.wait()

        return carry

    lax.fori_loop(0, ENTRIES, start, 0)
    lax.fori_loop(0, ENTRIES, wait, 0)


def owned_blocks(blocks, cache_k, cache_v):
    shape = jax.ShapeDtypeStruct((ENTRIES, VBLOCK, HD), jnp.bfloat16)
    whole = pl.BlockSpec(memory_space=pltpu.VMEM)
    return pl.pallas_call(
        functools.partial(owned_kernel, cache_k.shape[0] // VBLOCK),
        out_shape=(shape, shape),
        in_specs=[SMEM, ANY, ANY],
        out_specs=(whole, whole),
        scratch_shapes=[pltpu.SemaphoreType.DMA((ENTRIES, 2))],
        compiler_params=pltpu.CompilerParams(vmem_limit_bytes=16 * 2**20),
        name="owned_blocks",
    )(blocks, cache_k, cache_v)


STAGES = 2
TILE = 2
OUT_SPACE = pltpu.HBM
VMEM = 24
COST = 2**20
ROWS = VBLOCK // STAGES
WHOLE = pl.BlockSpec(memory_space=pltpu.VMEM)


def room(share):
    mean = ENTRIES * share
    wide = mean + 3.0 * math.sqrt(mean * (1.0 - share)) + 1.5
    return min(ENTRIES + 1, math.ceil(wide))


def owner_of(block, per_device):
    if per_device & (per_device - 1) == 0:
        return lax.shift_right_logical(block, per_device.bit_length() - 1)
    return lax.div(block, per_device)


def pack_kernel(per_device, limit, blocks, cache_k, cache_v, kept, sent, sems):
    me = lax.axis_index("ctx")
    even = lax.rem(me, 2) == 0
    count = jnp.int32(0)
    for entry in range(ENTRIES):
        head = entry // NV
        block = blocks[head, entry % NV]
        owner = owner_of(block, per_device)
        mine = owner == me
        local = block - owner * per_device

        def start(pair, head=head, local=local, count=count):
            rows = pl.ds(pl.multiple_of(local * VBLOCK, VBLOCK), VBLOCK)
            for i, target in enumerate((kept, sent)):
                source = pair[i].at[rows, pl.ds(head * HD, HD)]
                pltpu.make_async_copy(source, target.at[count], sems.at[count, i]).start()

        @pl.when(mine & (count < limit))
        def _(start=start):
            @pl.when(even)
            def _():
                start((cache_k, cache_v))

            @pl.when(jnp.logical_not(even))
            def _():
                start((cache_v, cache_k))

        count += mine.astype(jnp.int32)

    for at in range(limit):

        @pl.when(at < count)
        def _(at=at):
            for i, target in enumerate((kept, sent)):
                source = cache_k.at[pl.ds(0, VBLOCK), pl.ds(0, HD)]
                pltpu.make_async_copy(source, target.at[at], sems.at[at, i]).wait()


def pack(blocks, cache_k, cache_v, limit):
    shape = jax.ShapeDtypeStruct((limit, VBLOCK, HD), jnp.bfloat16)
    return pl.pallas_call(
        functools.partial(pack_kernel, cache_k.shape[0] // VBLOCK, limit),
        out_shape=(shape, shape),
        in_specs=[SMEM, ANY, ANY],
        out_specs=(WHOLE, WHOLE),
        scratch_shapes=[pltpu.SemaphoreType.DMA((limit, 2))],
        compiler_params=pltpu.CompilerParams(vmem_limit_bytes=16 * 2**20),
        name="pack",
    )(blocks, cache_k, cache_v)


def walk(blocks, per_device, known, bit, limits, act):
    me = lax.axis_index("ctx")
    table = blocks[...]
    at_mine = at_other = jnp.int32(0)
    for entry in range(ENTRIES):
        away = (owner_of(table[entry // NV, entry % NV], per_device) ^ me) & ~known
        mine, other = away == 0, away == bit
        tops = jnp.minimum(at_mine, limits[0] - 1), jnp.minimum(at_other, limits[1] - 1)
        act(entry, *tops, at_mine + at_other, other)
        at_mine += mine.astype(jnp.int32)
        at_other += other.astype(jnp.int32)


def merge_kernel(per_device, jobs, blocks, *refs):
    refs = list(refs)
    me = lax.axis_index("ctx")
    sources = [(refs.pop(0), refs.pop(0)) for _ in jobs]
    for (known, bit, halved, parts), (mine, other) in zip(jobs, sources):
        outs = [refs.pop(0) for _ in range(parts)]
        size, rows = outs[0].shape[:2]
        first = pl.multiple_of(jnp.where((me & halved) == 0, 0, rows), rows) if halved else 0

        def act(
            entry, at_mine, at_other, place, theirs, mine=mine, other=other, outs=outs, first=first
        ):
            place = jnp.minimum(place, outs[0].shape[0] - 1)
            for at, out in enumerate(outs):
                span = pl.ds(first + at * out.shape[1], out.shape[1])
                out[place] = jnp.where(theirs, other[at_other, span], mine[at_mine, span])

        walk(blocks, per_device, known, bit, (mine.shape[0], other.shape[0]), act)


def merged(blocks, per_device, jobs):
    shapes, lists = [], []
    for _, _, halved, parts, mine, other, size in jobs:
        rows = mine.shape[1] // (2 if halved else parts)
        shapes += [jax.ShapeDtypeStruct((size, rows, HD), jnp.bfloat16)] * parts
        lists += [mine, other]
    return pl.pallas_call(
        functools.partial(merge_kernel, per_device, [job[:4] for job in jobs]),
        out_shape=tuple(shapes),
        in_specs=[WHOLE] * (1 + len(lists)),
        out_specs=(WHOLE,) * len(shapes),
        compiler_params=pltpu.CompilerParams(vmem_limit_bytes=16 * 2**20),
        name="merge",
    )(blocks, *lists)


def stage_kernel(per_device, known, bit, banded, last, *refs):
    refs = list(refs)
    blocks = refs.pop(0)
    offsets = refs.pop(0) if banded else None
    queries, mine, other, mine_twin, other_twin = refs[:5]
    refs = refs[5:]
    if banded:
        before, own_k, own_v = refs[:3]
        refs = refs[3:]
    else:
        largest_in, total_in, mixed_in = refs[:3]
        refs = refs[3:]
    if last:
        out, kbuf, vbuf, held, sems = refs
    else:
        largest_out, total_out, mixed_out, kbuf, vbuf = refs
    me = lax.axis_index("ctx")
    even = lax.rem(me, 2) == 0
    wide = NV * ROWS

    def act(entry, at_mine, at_other, place, theirs):
        tile = jnp.where(theirs, other[at_other], mine[at_mine])
        twin = jnp.where(theirs, other_twin[at_other], mine_twin[at_mine])
        rows = pl.ds(entry % NV * ROWS, ROWS)
        kbuf[entry // NV, rows] = jnp.where(even, tile, twin)
        vbuf[entry // NV, rows, :HD] = jnp.where(even, twin, tile)

    if not last:
        walk(blocks, per_device, known, bit, (mine.shape[0], other.shape[0]), act)
    else:
        half = wide // 2
        for head in range(KVH):
            span = slice(head * NV, (head + 1) * NV)
            for at, (own, twin) in enumerate(((mine, mine_twin), (other, other_twin))):
                tile, pair = own[span].reshape(half, HD), twin[span].reshape(half, HD)
                rows = slice(at * half, (at + 1) * half)
                kbuf[head, rows] = jnp.where(even, tile, pair)
                vbuf[head, rows, :HD] = jnp.where(even, pair, tile)
    copies = []
    for head in range(KVH):
        columns = slice(head * HD, (head + 1) * HD)
        vbuf[head, :, HD:] = jnp.ones((vbuf.shape[1], HD), jnp.bfloat16)
        mask = None
        if banded:
            values = slice((KVH + head) * HD, (KVH + head + 1) * HD)
            kbuf[head, wide : wide + SMAX] = before[:, columns]
            kbuf[head, wide + SMAX :] = own_k[:, columns]
            vbuf[head, wide : wide + SMAX, :HD] = before[:, values]
            vbuf[head, wide + SMAX :, :HD] = own_v[:, columns]
            mask = band_mask(offsets[...], head, me == 0)
        for at in range(0, GROUP, TILE):
            rows = jnp.concatenate(
                [
                    queries[:, (head * GROUP + at + i) * HD : (head * GROUP + at + i + 1) * HD]
                    for i in range(TILE)
                ],
                axis=0,
            )
            start = (head * GROUP + at) * QDEV
            tile = slice(start, start + TILE * QDEV)
            floor = None if banded else largest_in[tile]
            largest, mixed = attend_rows(rows, kbuf[head], vbuf[head], mask, floor)
            mixed, total = mixed[:, :HD], mixed[:, HD:]
            if not banded:
                then = jnp.exp2(floor - largest)
                mixed = mixed + mixed_in[tile] * then
                total = total + total_in[tile] * then
            if last:
                result = (mixed / total).astype(jnp.bfloat16)
                for i in range(TILE):
                    held[head, :, (at + i) * HD : (at + i + 1) * HD] = result[
                        i * QDEV : (i + 1) * QDEV
                    ]
            else:
                largest_out[tile] = jnp.broadcast_to(largest, mixed.shape)
                total_out[tile] = total
                mixed_out[tile] = mixed
        if last:
            span = pl.ds(head * GROUP * HD, GROUP * HD)
            copies.append(pltpu.make_async_copy(held.at[head], out.at[:, span], sems.at[head]))
            copies[-1].start()
    for copy in copies:
        copy.wait()


def attend_stage(known, bit, per_device, blocks, queries, lists, offsets=None, bands=None, state=None):
    banded, last = bands is not None, state is not None
    tall = KVH * GROUP * QDEV
    args = [blocks] + [offsets] * banded + [queries, *lists]
    args += list(bands if banded else state)
    specs = [WHOLE] * len(args)
    keys = NV * ROWS + (SMAX + QDEV) * banded
    scratch = [
        pltpu.VMEM((KVH, keys, HD), jnp.bfloat16),
        pltpu.VMEM((KVH, keys, 2 * HD), jnp.bfloat16),
    ]
    if last:
        out_shape = jax.ShapeDtypeStruct(queries.shape, jnp.bfloat16)
        out_specs = pl.BlockSpec(memory_space=OUT_SPACE)
        scratch += [
            pltpu.VMEM((KVH, QDEV, GROUP * HD), jnp.bfloat16),
            pltpu.SemaphoreType.DMA((KVH,)),
        ]
    else:
        out_shape = (jax.ShapeDtypeStruct((tall, HD), jnp.float32),) * 3
        out_specs = (WHOLE,) * 3
    return pl.pallas_call(
        functools.partial(stage_kernel, per_device, known, bit, banded, last),
        out_shape=out_shape,
        in_specs=specs,
        out_specs=out_specs,
        scratch_shapes=scratch,
        compiler_params=pltpu.CompilerParams(vmem_limit_bytes=VMEM * 2**20),
        cost_estimate=pl.CostEstimate(flops=COST, bytes_accessed=COST, transcendentals=0),
        name="attend_last" if last else "attend_first",
    )(*args)


def permuted(array, pairs):
    return lax.ppermute(array, "ctx", pairs)


def swapped(array, bit):
    return permuted(array, [(i, i ^ bit) for i in range(lax.axis_size("ctx"))])


def fits(blocks, per_device, peers, masks):
    most = [room((1 << mask.bit_count()) / peers) + (-1 if mask else 1) for mask in masks]
    owners = (blocks // per_device).reshape(1, 1, ENTRIES)
    ids = jnp.arange(peers, dtype=jnp.int32)[None, :, None]
    away = (owners ^ ids) & ~jnp.array(masks, jnp.int32)[:, None, None]
    counts = jnp.sum((away == 0).astype(jnp.int32), axis=2)
    return jnp.all(counts <= jnp.array(most, jnp.int32)[:, None])


def general(queries, bands, cache_k, cache_v, blocks, offsets, bits):
    keys, values = owned_blocks(blocks, cache_k, cache_v)
    even = lax.axis_index("ctx") % 2 == 0
    mine = jnp.where(even, keys, values) + swapped(jnp.where(even, values, keys), 1)
    for bit in bits[1:]:
        mine = mine + swapped(mine, bit)
    twin = swapped(mine, 1)
    keys, values = jnp.where(even, mine, twin), jnp.where(even, twin, mine)
    keys = keys.reshape(KVH, NV * VBLOCK, HD)
    values = values.reshape(KVH, NV * VBLOCK, HD)
    before, own_k, own_v = bands
    wide = KVH * HD
    bands = (before[:, :wide], own_k, before[:, wide:], own_v)
    return attend_dense(offsets, queries, keys, values, bands)


def shards(queries, span_k, span_v, cache_k, cache_v, blocks, offsets):
    peers = lax.axis_size("ctx")
    per_device = cache_k.shape[0] // VBLOCK
    ahead = [(i, i + 1) for i in range(peers - 1)]
    near = 2
    far = [1 << at for at in range(peers.bit_length() - 2, 1, -1)]
    bits = [1] + far + [near]
    masks_a = [sum(bits[:at]) for at in range(len(bits))]
    masks_b = [1 + near + sum(far[:at]) for at in range(len(far))]

    def job(known, bit, mine, other, parts=1, halved=0):
        size = room((1 << (known | bit).bit_count()) / peers)
        if known + bit == peers - 1:
            size = ENTRIES
        return known, bit, halved, parts, mine, other, size

    merge = functools.partial(merged, blocks, per_device)
    kept, sent = pack(blocks, cache_k, cache_v, room(1 / peers) + 1)
    mine_a, mine_b = merge([job(0, 1, kept, swapped(sent, 1), parts=STAGES)])
    spans, mine_b = lax.optimization_barrier((jnp.concatenate([span_k, span_v], axis=1), mine_b))
    before = permuted(spans, ahead)
    short = jnp.logical_not(fits(blocks, per_device, peers, masks_a + masks_b)).astype(jnp.int32)

    steps_a = list(zip(masks_a[1:], far))
    steps_b = list(zip([1] + masks_b, [near] + far))
    other_a = swapped(mine_a, far[0])
    other_b = swapped(mine_b, near)
    other_b, short = lax.optimization_barrier((other_b, short))
    for at in range(len(far)):
        job_a = job(*steps_a[at], mine_a, other_a)
        job_b = job(*steps_b[at], mine_b, other_b, halved=near if at == 0 else 0)
        if at < len(far) - 1:
            (mine_b,) = merge([job_b])
            other_a, mine_b = lax.optimization_barrier((other_a, mine_b))
            (mine_a,) = merge([job(*steps_a[at], mine_a, other_a)])
        else:
            (mine_a,), (mine_b,) = merge([job_a]), merge([job_b])
        other_a = swapped(mine_a, (far + [near])[at + 1])
        other_b = swapped(mine_b, far[at])
        if at < len(far) - 1:
            other_a, other_b, before = lax.optimization_barrier((other_a, other_b, before))
    (mine_b,) = merge([job(*steps_b[-1], mine_b, other_b)])
    other_a, mine_b = lax.optimization_barrier((other_a, mine_b))
    other_b = swapped(mine_b, near)
    twin_a, twin_b = swapped(mine_a, 1), swapped(mine_b, 1)

    bands = (before, span_k, span_v)
    shared = (peers - 1 - near, near, per_device, blocks, queries)
    lists = (mine_a, other_a, twin_a, swapped(other_a, 1))
    state = attend_stage(*shared, lists, offsets=offsets, bands=bands)
    state, late = lax.optimization_barrier((state, other_b))
    lists = (mine_b, late, twin_b, swapped(late, 1))
    fast = attend_stage(*shared, lists, state=state)

    def again(carry):
        return 0, general(queries, bands, cache_k, cache_v, blocks, offsets, bits)

    return lax.while_loop(lambda carry: carry[0] > 0, again, (short, fast))[1]


def solution(mesh):
    rows = P(("groups", "ctx"), None)
    heads = P("groups", None)
    return jax.shard_map(
        shards,
        mesh=mesh,
        in_specs=(rows, rows, rows, rows, rows, heads, heads),
        out_specs=rows,
        check_vma=False,
    )
```
